32 devices in a mesh: rows: 4 (over y, x), mp: 8 (over z, core).
Axes of the slice: x: 2, y: 2, z: 4, core: 2. Of those that a mesh axis runs over, the one named last changes fastest.
Arguments:
- tokens: bfloat16 [32768, 1024], P(('rows', 'mp')), may hold values from -6 to 6
- qkv_weight: bfloat16 [3, 1024, 1024], P(None, None, 'mp'), may hold values from -0.1875 to 0.1875
- qv_bias: bfloat16 [2, 1024], P(None, 'mp'), may hold values from -1.1953125 to 1.1953125
- out_weight: bfloat16 [1024, 1024], P('mp'), may hold values from -0.75 to 0.75
- up_weight: bfloat16 [1024, 4096], P(None, 'mp'), may hold values from -0.1875 to 0.1875
- up_bias: bfloat16 [4096], P('mp'), may hold values from -1.1953125 to 1.1953125
- down_weight: bfloat16 [4096, 1024], P('mp'), may hold values from -0.09375 to 0.09375
- norm_gains: bfloat16 [2, 1024], replicated, may hold values from 0.5 to 1.5
- shift_vectors: bfloat16 [4, 1024], replicated, may hold values from -1.1953125 to 1.1953125
- lengths: int32 [32, 6], P('rows'), may hold values from 1 to 1019, as said below
- cotangent: bfloat16 [32768, 1024], P(('rows', 'mp')), may hold values from -6 to 6
Outputs:
- mixed: bfloat16 [32768, 1024], P(('rows', 'mp'))
- block_loss: float32 [32], P('rows')
- input_grad: float32 [32768, 1024], P(('rows', 'mp'))
- qkv_grad: float32 [3, 1024, 1024], P(None, None, 'mp')
- qv_bias_grad: float32 [2, 1024], P(None, 'mp')
- out_weight_grad: float32 [1024, 1024], P('mp')
- up_weight_grad: float32 [1024, 4096], P(None, 'mp')
- up_bias_grad: float32 [4096], P('mp')
- down_weight_grad: float32 [4096, 1024], P('mp')
- vector_grad: float32 [6, 1024], P(None, 'mp')
The draws below stay inside these ranges and needn't reach their ends.
Inputs may be any that keep to these rules, and one draw needn't show every extreme that they name: Each block's 6 documents fill its first slots in order and the rest of the block is padding; a block's lengths sum to at most 1024. In at least one block the lengths sum to exactly 1024, and one of its documents has 1019 slots.
All inputs are finite; a program needn't handle non-finite values.
Results may differ from the reference program's by a relative error of at most 0.012.
The reference program's roundings to bfloat16 on the way count: a program that leaves them out, or rounds other values in their place, can miss the bound.
Values may be sent and summed in bfloat16 or wider, within the bound.
No kernel may reach another device: no remote copies, remote signals or barrier semaphores. Data moves between devices by JAX's collectives and lax.ppermute only.
A program may use at most 512 MiB of HBM per device.

```python
import math
import jax
import jax.numpy as jnp
from jax import lax

D = 1024
HEADS = 16
HD = 64
FF = 4096
SLOTS = 1024
DOCS = 6
BLOCKS = 32
TOKENS = 32768


def draw_lengths(key, part):
    key = jax.random.fold_in(key, 11)
    streams = jax.random.split(key, 5)
    padding = jax.random.randint(streams[0], (BLOCKS,), 0, SLOTS * 3 // 10 + 1)
    full_block = jax.random.randint(streams[1], (), 0, BLOCKS)
    padding = jnp.where(jnp.arange(BLOCKS) == full_block, 0, padding)
    filled = SLOTS - padding
    weights = jax.random.randint(streams[2], (BLOCKS, DOCS), 1, 9)
    longest = jax.random.randint(streams[3], (BLOCKS, 1), 0, DOCS)
    boost = jax.random.randint(streams[4], (BLOCKS, 1), 8, 25)
    weights = jnp.where(jnp.arange(DOCS)[None, :] == longest, weights * boost, weights)
    spare = filled[:, None] - DOCS
    shares = spare * weights // jnp.sum(weights, axis=1, keepdims=True)
    result = 1 + shares
    remain = filled - jnp.sum(result, axis=1)
    result = result.at[:, DOCS - 1].add(remain)
    single = jnp.where(jnp.arange(DOCS)[None, :] == longest, SLOTS - DOCS + 1, 1)
    result = jnp.where((jnp.arange(BLOCKS) == full_block)[:, None], single, result)
    return result.astype(jnp.int32)


def block_scale(key, dims, cuts, least, largest):
    def one(axis_at, shards_of):
        draws = jax.random.uniform(jax.random.fold_in(jax.random.fold_in(key, 6), axis_at), (shards_of,), jnp.float32, least / len(cuts), largest / len(cuts))
        return jnp.repeat(jnp.exp(draws), dims[axis_at] // shards_of).reshape((-1,) + (1,) * (len(dims) - axis_at - 1))

    factor_of = one(*cuts[0])
    for cut in cuts[1:]:
        factor_of = factor_of * one(*cut)
    return factor_of


def noise(own_key, shape, scale, reach, pieces=(), kind=jnp.bfloat16):
    loudness = block_scale(own_key, shape, pieces, -0.22, 0.18) if pieces else 1.0
    values = jax.random.normal(own_key, shape, jnp.float32) * scale * loudness
    return jnp.minimum(jnp.maximum(values, -reach), reach).astype(kind)


def setup_inputs(seed: int = 0) -> dict:
    arg_keys = jax.random.split(jax.random.key(seed), 12)
    tokens = noise(arg_keys[0], (TOKENS, D), 1.0, 6.0, ((0, 32),))
    qkv_weight = noise(arg_keys[1], (3, D, D), D ** -0.5, 0.1875, ((2, 8),))
    qv_bias = noise(arg_keys[2], (2, D), 0.2, 1.1953125, ((1, 8),))
    out_weight = noise(arg_keys[3], (D, D), (D // 16) ** -0.5, 0.75, ((0, 8),))
    up_weight = noise(arg_keys[4], (D, FF), D ** -0.5, 0.1875, ((1, 8),))
    up_bias = noise(arg_keys[5], (FF,), 0.2, 1.1953125, ((0, 8),))
    down_weight = noise(arg_keys[6], (FF, D), FF ** -0.5, 0.09375, ((0, 8),))
    norm_gains = jnp.clip(1.0 + 0.1 * jax.random.normal(arg_keys[7], (2, D), jnp.float32), 0.5, 1.5).astype(jnp.bfloat16)
    shift_vectors = noise(arg_keys[8], (4, D), 0.2, 1.1953125)
    lengths = draw_lengths(jax.random.fold_in(arg_keys[11], 71), 0)
    cotangent = noise(arg_keys[10], (TOKENS, D), 1.0, 6.0, ((0, 32),))
    return {"tokens": tokens, "qkv_weight": qkv_weight, "qv_bias": qv_bias, "out_weight": out_weight, "up_weight": up_weight, "up_bias": up_bias, "down_weight": down_weight, "norm_gains": norm_gains, "shift_vectors": shift_vectors, "lengths": lengths, "cotangent": cotangent}


@jax.custom_vjp
def low(v):
    return lax.optimization_barrier(v.astype(jnp.bfloat16)).astype(jnp.float32)

@jax.custom_vjp
def low_back(v):
    return v

def low_keep(v):
    return (low(v), None)

def low_pass(kept, grad):
    return (grad,)

def back_keep(v):
    return (v, None)

def back_low(kept, grad):
    return (low(grad),)
low.defvjp(low_keep, low_pass)
low_back.defvjp(back_keep, back_low)
PRECISE = lax.Precision.HIGHEST
EPSILON = 1e-05

def layer_norm(values, gain, shift):
    center = lax.optimization_barrier(jnp.mean(values, axis=-1, keepdims=True))
    spread = values - center
    variance = lax.optimization_barrier(jnp.mean(spread * spread, axis=-1, keepdims=True))
    return spread * lax.rsqrt(variance + EPSILON) * gain + shift

def document_ids(lengths):
    endings = jnp.cumsum(lengths, axis=1).astype(jnp.int32)
    position = jnp.arange(SLOTS, dtype=jnp.int32)
    segment = lax.optimization_barrier(jnp.sum((position[None, :, None] >= endings[:, None, :]).astype(jnp.int32), axis=2)).astype(jnp.int32)
    living = segment < DOCS
    identity = jnp.where(living, segment, DOCS + position[None, :]).astype(jnp.int32)
    return (identity, living)

def heads_of(tensor):
    return tensor.reshape(SLOTS, HEADS, HD)

def block_forward(inputs, identity, params):
    qkv_weight, qv_bias, out_weight, up_weight, up_bias, down_weight, gains, shifts = params
    factor = HD ** (-0.5)
    normed = low(layer_norm(inputs, gains[0], shifts[0]))
    queries = low_back(low((jnp.dot(normed, qkv_weight[0], precision=PRECISE) + qv_bias[0]) * factor))
    key_rows = low_back(low(jnp.dot(normed, qkv_weight[1], precision=PRECISE)))
    value_rows = low_back(low(jnp.dot(normed, qkv_weight[2], precision=PRECISE) + qv_bias[1]))
    scores = low_back(jnp.einsum('qhd,khd->hqk', heads_of(queries), heads_of(key_rows), precision=PRECISE))
    position = jnp.arange(SLOTS)
    allowed = (identity[:, None] == identity[None, :]) & (position[None, :] <= position[:, None])
    scores = jnp.where(allowed[None], scores, -1e+30)
    weights = low(jax.nn.softmax(scores, axis=-1))
    attended = jnp.einsum('hqk,khd->qhd', weights, heads_of(value_rows), precision=PRECISE).reshape(SLOTS, D)
    attended = low_back(low(attended))
    branch = low_back(jnp.dot(attended, out_weight, precision=PRECISE) + shifts[1])
    middle = inputs + branch
    normed_two = low(layer_norm(middle, gains[1], shifts[2]))
    hidden = low_back(jnp.dot(normed_two, up_weight, precision=PRECISE) + up_bias)
    active = low(jax.nn.gelu(hidden, approximate=True))
    feed = low_back(jnp.dot(active, down_weight, precision=PRECISE) + shifts[3])
    return middle + feed

def reference(tokens, qkv_weight, qv_bias, out_weight, up_weight, up_bias, down_weight, norm_gains, shift_vectors, lengths, cotangent):
    identity, living = document_ids(lengths)
    params = tuple((member.astype(jnp.float32) for member in (qkv_weight, qv_bias, out_weight, up_weight, up_bias, down_weight, norm_gains, shift_vectors)))
    inputs = tokens.astype(jnp.float32).reshape(BLOCKS, SLOTS, D)
    weighting = cotangent.astype(jnp.float32).reshape(BLOCKS, SLOTS, D) * living[:, :, None].astype(jnp.float32)
    checked = jax.checkpoint(block_forward)

    def forward(stacked, params_in):

        def advance(running, member):
            return (running, checked(member[0], member[1], params_in))
        _, result = lax.scan(advance, jnp.zeros((), jnp.float32), (stacked, identity))
        return result
    result, pullback = jax.vjp(forward, inputs, params)
    input_grad, param_grads = pullback(weighting)
    mixed = result.reshape(TOKENS, D).astype(jnp.bfloat16)
    block_loss = lax.optimization_barrier(jnp.sum(result * weighting, axis=(1, 2))) / math.sqrt(SLOTS * D)
    vector_grad = jnp.concatenate([param_grads[6], param_grads[7]], axis=0)
    return (mixed, block_loss, input_grad.reshape(TOKENS, D), param_grads[0], param_grads[1], param_grads[2], param_grads[3], param_grads[4], param_grads[5], vector_grad)
```

```python
import functools
import math

import jax
import jax.numpy as jnp
from jax import lax
from jax.experimental import pallas as pl
from jax.experimental.pallas import tpu as pltpu
from jax.sharding import PartitionSpec as P

HD = 64
PAIR = 128
PART = 32
PIECE = 112
TILE = 256
SLOTS = 1024
DOCS = 6
EPSILON = 1e-05
MASKED = -1e30
LOG2E = math.log2(math.e)
F32, BF16 = jnp.float32, jnp.bfloat16
NN = (((1,), (0,)), ((), ()))
NT = (((1,), (1,)), ((), ()))
TN = (((0,), (0,)), ((), ()))


def mm(a, b, dims):
    return lax.dot_general(a, b, dims, preferred_element_type=F32)


def whole(shape):
    return pl.BlockSpec(shape, lambda *_: (0,) * len(shape), pipeline_mode=pl.Buffered(1))


def call(kernel, grid, ins, outs, scratch=(), gflop=1.0, name=None):
    nbytes = sum(a.size * a.dtype.itemsize for a, _ in ins)
    nbytes += sum(math.prod(s) * jnp.dtype(d).itemsize for s, d, _ in outs)
    return pl.pallas_call(
        kernel,
        grid=grid,
        in_specs=[s for _, s in ins],
        out_specs=[s for _, _, s in outs],
        out_shape=[jax.ShapeDtypeStruct(s, d) for s, d, _ in outs],
        scratch_shapes=list(scratch),
        compiler_params=pltpu.CompilerParams(vmem_limit_bytes=56 << 20),
        cost_estimate=pl.CostEstimate(flops=int(gflop * 1e9), bytes_accessed=nbytes, transcendentals=0),
        name=name,
    )(*[a for a, _ in ins])


def prep_kernel(x_ref, cot_ref, live_ref, gain_ref, shift_ref, h_ref, gf_ref):
    v = x_ref[...].astype(F32)
    spread = v - jnp.mean(v, axis=1, keepdims=True)
    var = jnp.mean(spread * spread, axis=1, keepdims=True)
    h = spread * lax.rsqrt(var + EPSILON) * gain_ref[0:1, :] + shift_ref[0:1, :]
    h_ref[...] = h.astype(BF16)
    gf_ref[...] = (cot_ref[...].astype(F32) * live_ref[...]).astype(BF16)


def prep(x, cot, live, gains, shifts):
    n, d = x.shape
    rows = pl.BlockSpec((TILE, d), lambda i: (i, 0))
    return call(
        prep_kernel, (n // TILE,),
        [(x, rows), (cot, rows), (live, pl.BlockSpec((TILE, 1), lambda i: (i, 0))), (gains, whole(gains.shape)), (shifts, whole(shifts.shape))],
        [((n, d), BF16, rows), ((n, d), BF16, rows)], gflop=1.0, name="prep",
    )


def fill_mask(bias_ref, col_ref, row_ref, transposed):
    n = col_ref.shape[0]
    for i in range(n // TILE):
        part, upto = slice(i * TILE, (i + 1) * TILE), (i + 1) * TILE
        if transposed:
            same = col_ref[:upto, :] == row_ref[:, part]
            key = lax.broadcasted_iota(jnp.int32, (upto, TILE), 0)
            query = lax.broadcasted_iota(jnp.int32, (upto, TILE), 1) + i * TILE
            bias_ref[:upto, part] = jnp.where(same & (key <= query), 0.0, MASKED)
        else:
            same = col_ref[part, :] == row_ref[:, :upto]
            query = lax.broadcasted_iota(jnp.int32, (TILE, upto), 0) + i * TILE
            key = lax.broadcasted_iota(jnp.int32, (TILE, upto), 1)
            bias_ref[part, :upto] = jnp.where(same & (key <= query), 0.0, MASKED)


def pair_rows(w_ref, at):
    return jnp.concatenate([w_ref[j, 0, at : at + PART, :] for j in range(4)], axis=0)


def pair_bias(w_ref, at):
    lane = lax.broadcasted_iota(jnp.int32, (1, PAIR), 1) // PART
    row = jnp.zeros((1, PAIR), F32)
    for j in range(4):
        mine = w_ref[j, 0, 96:112, at : at + PAIR].astype(F32)[0:1, :]
        row = jnp.where(lane == j, mine, row)
    return row


def attend_kernel(col_ref, row_ref, h_ref, w_ref, q_ref, k_ref, v_ref, o_ref, lse_ref, bias_ref):
    n = h_ref.shape[0]

    @pl.when(pl.program_id(0) == 0)
    def _():
        fill_mask(bias_ref, col_ref, row_ref, False)

    wall = jnp.concatenate([pair_rows(w_ref, i * PART) for i in range(3)], axis=0)
    qkv = mm(h_ref[...], wall, NT)
    q_ref[...] = ((qkv[:, :PAIR] + pair_bias(w_ref, 128)) * HD**-0.5).astype(BF16)
    k_ref[...] = qkv[:, PAIR : 2 * PAIR].astype(BF16)
    v = (qkv[:, 2 * PAIR :] + pair_bias(w_ref, 256)).astype(BF16)
    v_ref[...] = v
    vx = jnp.concatenate([v, jnp.ones((n, PAIR), BF16)], axis=1)
    first = lax.broadcasted_iota(jnp.int32, (1, PAIR), 1) < HD
    zero = jnp.zeros((), BF16)
    for i in range(n // TILE):
        part, upto = slice(i * TILE, (i + 1) * TILE), (i + 1) * TILE
        q = q_ref[part, :]
        outs = []
        for h in range(2):
            mine = jnp.where(first, q, zero) if h == 0 else jnp.where(first, zero, q)
            s = mm(mine, k_ref[:upto, :], NT) + bias_ref[part, :upto]
            top = jnp.max(s, axis=1, keepdims=True)
            e = jnp.exp2((s - top) * LOG2E).astype(BF16)
            ov = mm(e, vx[:upto], NN)
            total = ov[:, PAIR:]
            outs.append(ov[:, :PAIR] / total)
            lse_ref[0, h : h + 1, part] = jnp.transpose(top + jnp.log(total))[0:1, :]
        o_ref[part, :] = jnp.where(first, outs[0], outs[1]).astype(BF16)


def attend(col, row, h, w, base=0, pairs=4):
    n, d = h.shape
    blk = pl.BlockSpec((n, PAIR), lambda p: (0, p))
    act = ((n, pairs * PAIR), BF16, blk)
    return call(
        attend_kernel, (pairs,),
        [(col, whole(col.shape)), (row, whole(row.shape)), (h, whole(h.shape)), (w, pl.BlockSpec((4, 1, PIECE, d), lambda p: (0, p + base, 0, 0)))],
        [act, act, act, act, ((pairs, 2, n), F32, pl.BlockSpec((1, 2, n), lambda p: (p, 0, 0)))],
        [pltpu.VMEM((n, n), F32)], gflop=4.0 * pairs, name="attend",
    )


def join_kernel(*refs):
    x_ref, o_refs, (wa_ref, wb_ref, gain_ref, shift_ref, r_ref, h_ref, wo_ref) = refs[0], refs[1:-7], refs[-7:]

    @pl.when(pl.program_id(0) == 0)
    def _():
        for half, w_ref in enumerate((wa_ref, wb_ref)):
            for z in range(4):
                for j in range(4):
                    lo = (half * 4 + z) * PAIR + j * PART
                    wo_ref[lo : lo + PART, :] = w_ref[j, z, :, :]

    branch, lo = shift_ref[1:2, :], 0
    for o_ref in o_refs:
        hi = lo + o_ref.shape[1]
        branch = branch + mm(o_ref[...], wo_ref[lo:hi, :], NN)
        lo = hi
    r = x_ref[...].astype(F32) + branch
    r_ref[...] = r
    spread = r - jnp.mean(r, axis=1, keepdims=True)
    var = jnp.mean(spread * spread, axis=1, keepdims=True)
    h_ref[...] = (spread * lax.rsqrt(var + EPSILON) * gain_ref[1:2, :] + shift_ref[2:3, :]).astype(BF16)


def join(x, os, wa, wb, gains, shifts):
    n, d = x.shape
    rows = pl.BlockSpec((TILE, d), lambda i: (i, 0))
    out = pl.BlockSpec((4, 4, PART, d), lambda i: (0, 0, PAIR // PART, 0), pipeline_mode=pl.Buffered(1))
    return call(
        join_kernel, (n // TILE,),
        [(x, rows)] + [(o, pl.BlockSpec((TILE, o.shape[1]), lambda i: (i, 0))) for o in os]
        + [(wa, out), (wb, out), (gains, whole(gains.shape)), (shifts, whole(shifts.shape))],
        [((n, d), F32, rows), ((n, d), BF16, rows)],
        [pltpu.VMEM((d, d), BF16)], gflop=4.0, name="join",
    )


UNITS = 512


def up_kernel(h_ref, w_ref, b_ref, act_ref, slope_ref):
    u = mm(h_ref[...], w_ref[0].reshape(UNITS, -1), NT) + b_ref[...].astype(F32)
    c0, c1 = math.sqrt(2 / math.pi), math.sqrt(2 / math.pi) * 0.044715
    square = u * u
    t = jnp.tanh(u * (c0 + c1 * square))
    half = 0.5 + 0.5 * t
    act_ref[...] = (u * half).astype(BF16)
    slope_ref[...] = (half + u * (0.5 - 0.5 * t * t) * (c0 + 3 * c1 * square)).astype(BF16)


def up(h, w, b):
    n, d = h.shape
    blk = pl.BlockSpec((n, UNITS), lambda i: (0, i))
    shape = (n, 4 * UNITS)
    return call(
        up_kernel, (4,),
        [(h, whole(h.shape)), (w, pl.BlockSpec((1, 4, PAIR, d), lambda i: (i, 0, 0, 0))), (b, pl.BlockSpec((1, UNITS), lambda i: (0, i)))],
        [(shape, BF16, blk), (shape, BF16, blk)], gflop=6.0, name="up",
    )


def down_kernel(aa_ref, ab_ref, wa_ref, wb_ref, r_ref, gf_ref, shift_ref, mixed_ref, loss_ref, acc_ref):
    t, last = pl.program_id(0), pl.num_programs(0) - 1
    half = pl.num_programs(0) // 2

    @pl.when(t == 0)
    def _():
        acc_ref[...] = mm(aa_ref[...], wa_ref[...], NN)

    @pl.when((t > 0) & (t < half))
    def _():
        acc_ref[...] += mm(aa_ref[...], wa_ref[...], NN)

    @pl.when(t >= half)
    def _():
        acc_ref[...] += mm(ab_ref[...], wb_ref[...], NN)

    @pl.when(t == last)
    def _():
        out = r_ref[...] + (acc_ref[...] + shift_ref[3:4, :])
        mixed_ref[...] = out.astype(BF16)
        loss = jnp.sum(out * gf_ref[...].astype(F32), axis=0, keepdims=True)
        loss_ref[...] = jnp.broadcast_to(jnp.sum(loss, axis=1, keepdims=True), loss_ref.shape)


def own(shape, steps, axis):
    at = lambda t: jnp.minimum(t, steps - 1)
    return pl.BlockSpec(shape, (lambda t: (at(t), 0)) if axis == 0 else (lambda t: (0, at(t))))


def oth(shape, steps, axis):
    at = lambda t: jnp.maximum(t - steps, 0)
    return pl.BlockSpec(shape, (lambda t: (at(t), 0)) if axis == 0 else (lambda t: (0, at(t))))


def down(aa, ab, wa, wb, r, gf, shifts):
    n, d = r.shape
    steps = wa.shape[0] // UNITS
    return call(
        down_kernel, (2 * steps,),
        [(aa, own((n, UNITS), steps, 1)), (ab, oth((n, UNITS), steps, 1)), (wa, own((UNITS, d), steps, 0)), (wb, oth((UNITS, d), steps, 0)),
         (r, whole(r.shape)), (gf, whole(gf.shape)), (shifts, whole(shifts.shape))],
        [((n, d), BF16, whole((n, d))), ((8, 128), F32, whole((8, 128)))],
        [pltpu.VMEM((n, d), F32)], gflop=9.0, name="down",
    )


def back_kernel(gf_ref, sa_ref, sb_ref, da_ref, db_ref, ua_ref, ub_ref, r_ref, gain_ref, ga_out, gb_out, gr_ref, br_ref, vec_ref, acc_ref):
    t, last = pl.program_id(0), pl.num_programs(0) - 1
    half = pl.num_programs(0) // 2

    @pl.when(t < half)
    def _():
        g = (mm(gf_ref[...], da_ref[...], NT) * sa_ref[...].astype(F32)).astype(BF16)
        ga_out[...] = g
        part = mm(g, ua_ref[0].reshape(UNITS, -1), NN)

        @pl.when(t == 0)
        def _():
            acc_ref[...] = part

        @pl.when(t > 0)
        def _():
            acc_ref[...] += part

    @pl.when(t >= half)
    def _():
        g = (mm(gf_ref[...], db_ref[...], NT) * sb_ref[...].astype(F32)).astype(BF16)
        gb_out[...] = g
        acc_ref[...] += mm(g, ub_ref[0].reshape(UNITS, -1), NN)

    @pl.when(t == last)
    def _():
        n, d = r_ref.shape
        sums = [jnp.zeros((1, d), F32) for _ in range(4)]
        for i in range(n // TILE):
            part = slice(i * TILE, (i + 1) * TILE)
            r, gy, c = r_ref[part, :], acc_ref[part, :], gf_ref[part, :].astype(F32)
            spread = r - jnp.mean(r, axis=1, keepdims=True)
            rstd = lax.rsqrt(jnp.mean(spread * spread, axis=1, keepdims=True) + EPSILON)
            norm = spread * rstd
            gn = gy * gain_ref[1:2, :]
            gv = rstd * (gn - jnp.mean(gn, axis=1, keepdims=True) - norm * jnp.mean(gn * norm, axis=1, keepdims=True))
            gr = c + gv
            gr_ref[part, :] = gr
            branch = gr.astype(BF16)
            br_ref[part, :] = branch
            for at, value in enumerate((gy * norm, gy, branch.astype(F32), c)):
                sums[at] += jnp.sum(value, axis=0, keepdims=True)
        vec_ref[...] = jnp.concatenate(sums + [jnp.zeros((4, d), F32)], axis=0)


def back(gf, sa, sb, da, db, ua, ub, r, gains):
    n, d = r.shape
    steps = da.shape[0] // UNITS
    wa, wb = own((UNITS, d), steps, 0), oth((UNITS, d), steps, 0)
    ta, tb = own((n, UNITS), steps, 1), oth((n, UNITS), steps, 1)
    pa = pl.BlockSpec((1, 4, PAIR, d), lambda t: (jnp.minimum(t, steps - 1), 0, 0, 0))
    pb = pl.BlockSpec((1, 4, PAIR, d), lambda t: (jnp.maximum(t - steps, 0), 0, 0, 0))
    return call(
        back_kernel, (2 * steps,),
        [(gf, whole(gf.shape)), (sa, ta), (sb, tb), (da, wa), (db, wb), (ua, pa), (ub, pb), (r, whole(r.shape)), (gains, whole(gains.shape))],
        [(sa.shape, BF16, ta), (sb.shape, BF16, tb), ((n, d), F32, whole((n, d))), ((n, d), BF16, whole((n, d))), ((8, d), F32, whole((8, d)))],
        [pltpu.VMEM((n, d), F32)], gflop=19.0, name="back",
    )


def halves(rows):
    return rows // 2 // 16 * 16


def outer_kernel(la_ref, lb_ref, ra_ref, rb_ref, *outs):
    g = (mm(la_ref[...], ra_ref[...], TN) + mm(lb_ref[...], rb_ref[...], TN)).astype(BF16)
    t = pl.program_id(0)
    for j in range(3):

        @pl.when(t == j)
        def _():
            outs[j][...] = g

    @pl.when(t == 3)
    def _():
        cut = outs[3].shape[0]
        outs[3][...] = g[:cut]
        outs[4][...] = g[cut:]

    outs[5][...] = jnp.sum(la_ref[...].astype(F32) + lb_ref[...].astype(F32), axis=0, keepdims=True)


def outer(la, lb, ra, rb):
    n, m = la.shape
    d = ra.shape[1]
    tile = pl.BlockSpec((n, UNITS), lambda i: (0, i))
    cut = halves(UNITS)
    rows = (UNITS, UNITS, UNITS, cut, UNITS - cut)
    *g, total = call(
        outer_kernel, (4,),
        [(la, tile), (lb, tile), (ra, whole(ra.shape)), (rb, whole(rb.shape))],
        [((k, d), BF16, whole((k, d))) for k in rows] + [((1, m), F32, pl.BlockSpec((1, UNITS), lambda i: (0, i)))],
        gflop=9.0, name="outer",
    )
    return g, total


def attend_back_kernel(col_ref, row_ref, ga_ref, wo_ref, q_ref, k_ref, v_ref, o_ref, lse_ref, gq_ref, gk_ref, gv_ref, bias_ref, ka_ref, va_ref, go_ref):
    n = q_ref.shape[0]

    @pl.when(pl.program_id(0) == 0)
    def _():
        fill_mask(bias_ref, col_ref, row_ref, True)

    w = jnp.concatenate([wo_ref[j, 0, :, :] for j in range(4)], axis=0)
    go_ref[...] = mm(ga_ref[...], w, NT).astype(BF16)
    first = lax.broadcasted_iota(jnp.int32, (1, PAIR), 1) < HD
    zero = jnp.zeros((), BF16)
    split = lambda a: (jnp.where(first, a, zero), jnp.where(first, zero, a))
    ks = split(k_ref[...])
    for i in range(n // TILE):
        part, upto = slice(i * TILE, (i + 1) * TILE), (i + 1) * TILE
        qs, gs = split(q_ref[part, :]), split(go_ref[part, :])
        prod = jnp.transpose(go_ref[part, :].astype(F32) * o_ref[part, :].astype(F32))
        ps, ds = [], []
        for h in range(2):
            delta = jnp.sum(prod[h * HD : (h + 1) * HD, :], axis=0, keepdims=True)
            s = mm(k_ref[:upto, :], qs[h], NT) + bias_ref[:upto, part]
            p = jnp.exp2((s - lse_ref[0, h : h + 1, part]) * LOG2E)
            dp = mm(v_ref[:upto, :], gs[h], NT)
            ds.append((p * (dp - delta)).astype(BF16))
            ps.append(p.astype(BF16))
        gv = mm(jnp.concatenate(ps, 1), jnp.concatenate(gs, 0), NN)
        gk = mm(jnp.concatenate(ds, 1), jnp.concatenate(qs, 0), NN)
        gq = mm(ds[0], ks[0][:upto], TN) + mm(ds[1], ks[1][:upto], TN)
        gq_ref[part, :] = (gq.astype(BF16).astype(F32) * HD**-0.5).astype(BF16)
        lo = i * TILE
        if i:
            va_ref[:lo, :] += gv[:lo]
            ka_ref[:lo, :] += gk[:lo]
        va_ref[part, :] = gv[lo:]
        ka_ref[part, :] = gk[lo:]
    gk_ref[...] = ka_ref[...].astype(BF16)
    gv_ref[...] = va_ref[...].astype(BF16)


def attend_back(col, row, ga, wo, base, q, k, v, o, lse):
    n, d = ga.shape
    pairs = lse.shape[0]
    blk = pl.BlockSpec((n, PAIR), lambda p: (0, p))
    act = ((n, pairs * PAIR), BF16, blk)
    return call(
        attend_back_kernel, (pairs,),
        [(col, whole(col.shape)), (row, whole(row.shape)), (ga, whole(ga.shape)), (wo, pl.BlockSpec((4, 1, PART, d), lambda p: (0, p + base, PAIR // PART, 0))),
         (q, blk), (k, blk), (v, blk), (o, blk), (lse, pl.BlockSpec((1, 2, n), lambda p: (p, 0, 0)))],
        [act, act, act],
        [pltpu.VMEM((n, n), F32), pltpu.VMEM((n, PAIR), F32), pltpu.VMEM((n, PAIR), F32), pltpu.VMEM((n, PAIR), BF16)],
        gflop=5.0 * pairs, name="attend_back",
    )


ATTN = PIECE + PART


def outer_attn_kernel(qa_ref, qb_ref, ka_ref, kb_ref, va_ref, vb_ref, oa_ref, ob_ref, ha_ref, hb_ref, ga_ref, gb_ref, up_ref, *outs):
    p, pairs = pl.program_id(0), pl.num_programs(0)
    rows = []
    for a_ref, b_ref, c_ref, d_ref in ((qa_ref, qb_ref, ha_ref, hb_ref), (ka_ref, kb_ref, ha_ref, hb_ref), (va_ref, vb_ref, ha_ref, hb_ref), (oa_ref, ob_ref, ga_ref, gb_ref)):
        rows.append((mm(a_ref[...], c_ref[...], TN) + mm(b_ref[...], d_ref[...], TN)).astype(BF16))
    total = lambda a_ref, b_ref: jnp.sum(a_ref[...].astype(F32) + b_ref[...].astype(F32), axis=0, keepdims=True)
    qsum, vsum = total(qa_ref, qb_ref), total(va_ref, vb_ref)
    d = ha_ref.shape[1]
    for j in range(4):
        turn = lambda a: jnp.concatenate([a[:, j * PART :], a[:, : j * PART]], axis=1) if j else a
        line = jnp.concatenate([up_ref[j, 0, 0:1, :], turn(qsum), turn(vsum), jnp.zeros((1, d - 3 * PAIR), F32)], axis=1)
        line = jnp.concatenate([line, jnp.zeros((15, d), F32)], axis=0).astype(BF16)
        part = [rows[i][j * PART : (j + 1) * PART, :] for i in range(4)]
        outs[j][...] = jnp.concatenate(part[:3] + [line] + part[3:], axis=0)


def outer_attn(qs, ks, vs, os, hs, gs, upsum):
    n, m = qs[0].shape
    d = hs[0].shape[1]
    pairs = m // PAIR
    tile = pl.BlockSpec((n, PAIR), lambda p: (0, p))
    return call(
        outer_attn_kernel, (pairs,),
        [(a, tile) for a in (*qs, *ks, *vs, *os)] + [(a, whole(a.shape)) for a in (*hs, *gs)]
        + [(upsum, pl.BlockSpec((4, 1, 8, PAIR), lambda p: (0, p, 0, 0)))],
        [((pairs * ATTN, d), BF16, pl.BlockSpec((ATTN, d), lambda p: (p, 0)))] * 4,
        gflop=2.5 * pairs, name="outer_attn",
    )


def finish_kernel(*refs, spans):
    grads, (wa_ref, wb_ref, x_ref, gr_ref, gain_ref, out_ref, vec_ref, acc_ref) = refs[:-8], refs[-8:]
    t, last = pl.program_id(0), pl.num_programs(0) - 1
    for at, (lo, hi, half) in enumerate(spans):

        @pl.when((t >= lo) & (t < hi))
        def _():
            w_ref = wb_ref if half else wa_ref
            wall = jnp.concatenate([pair_rows(w_ref, i * PART) for i in range(3)], axis=0)
            part = mm(jnp.concatenate([ref[...] for ref in grads[3 * at : 3 * at + 3]], axis=1), wall, NN)
            if lo == 0:
                acc_ref[...] = jnp.where(t == 0, part, acc_ref[...] + part)
            else:
                acc_ref[...] += part

    @pl.when(t == last)
    def _():
        n, d = x_ref.shape
        sums = [jnp.zeros((1, d), F32) for _ in range(2)]
        for i in range(n // TILE):
            rows = slice(i * TILE, (i + 1) * TILE)
            x, gy = x_ref[rows, :].astype(F32), acc_ref[rows, :]
            spread = x - jnp.mean(x, axis=1, keepdims=True)
            rstd = lax.rsqrt(jnp.mean(spread * spread, axis=1, keepdims=True) + EPSILON)
            norm = spread * rstd
            gn = gy * gain_ref[0:1, :]
            gv = rstd * (gn - jnp.mean(gn, axis=1, keepdims=True) - norm * jnp.mean(gn * norm, axis=1, keepdims=True))
            out_ref[rows, :] = gr_ref[rows, :] + gv
            for at, value in enumerate((gy * norm, gy)):
                sums[at] += jnp.sum(value, axis=0, keepdims=True)
        vec_ref[...] = jnp.concatenate(sums + [jnp.zeros((6, d), F32)], axis=0)


def finish(grads, wa, wb, x, gr, gains):
    n, d = x.shape
    ins, spans, lo = [], [], 0
    firsts = {0: [], 1: []}
    for gq, gk, gv, base, half in grads:
        count = gq.shape[1] // PAIR
        spec = pl.BlockSpec((n, PAIR), lambda t, lo=lo, count=count: (0, jnp.clip(t - lo, 0, count - 1)))
        ins += [(gq, spec), (gk, spec), (gv, spec)]
        spans.append((lo, lo + count, half))
        firsts[half].append((lo, base))
        lo += count

    def pick(half):
        def at(t):
            pair = firsts[half][0][1]
            for lo, hi, which in spans:
                if which == half:
                    base = dict(firsts[half])[lo]
                    pair = jnp.where(t >= lo, base + jnp.minimum(t - lo, hi - lo - 1), pair)
            return (0, pair, 0, 0)

        return pl.BlockSpec((4, 1, PIECE, d), at)

    return call(
        functools.partial(finish_kernel, spans=spans), (lo,),
        ins + [(wa, pick(0)), (wb, pick(1)), (x, whole(x.shape)), (gr, whole(gr.shape)), (gains, whole(gains.shape))],
        [((n, d), F32, whole((n, d))), ((8, d), F32, whole((8, d)))],
        [pltpu.VMEM((n, d), F32)], gflop=10.0, name="finish",
    )


def pack_kernel(r_ref, *refs, plan, bands):
    srcs, (out_ref, held_ref, in_sem, out_sem) = refs[:-4], refs[-4:]
    copies = []
    for at, (src, quarter, count, dst) in enumerate(plan):
        source = srcs[src] if quarter is None else srcs[src].at[r_ref[0] ^ quarter]
        copies.append(pltpu.make_async_copy(source, held_ref.at[pl.ds(dst, count)], in_sem.at[at]))
    for copy in copies:
        copy.start()
    band = held_ref.shape[0] // bands
    outs = []
    for b in range(bands):
        for copy, (_, _, _, dst) in zip(copies, plan):
            if dst // band == b:
                copy.wait()
        span = pl.ds(b * band, band)
        outs.append(pltpu.make_async_copy(held_ref.at[span], out_ref.at[span], out_sem.at[b]))
        outs[-1].start()
    for out in outs:
        out.wait()


def pack(r, arrays, plan, bands=1):
    rows = sum(count for _, _, count, _ in plan)
    d = arrays[0].shape[-1]
    anywhere = pl.BlockSpec(memory_space=pl.ANY)
    return pl.pallas_call(
        functools.partial(pack_kernel, plan=plan, bands=bands),
        in_specs=[pl.BlockSpec(memory_space=pltpu.SMEM)] + [anywhere] * len(arrays),
        out_specs=anywhere,
        out_shape=jax.ShapeDtypeStruct((rows, d), BF16),
        scratch_shapes=[pltpu.VMEM((rows, d), BF16), pltpu.SemaphoreType.DMA((len(plan),)), pltpu.SemaphoreType.DMA((bands,))],
        compiler_params=pltpu.CompilerParams(vmem_limit_bytes=56 << 20),
        cost_estimate=pl.CostEstimate(flops=0, bytes_accessed=4 * rows * d, transcendentals=0),
        name="pack",
    )(r, *arrays)


def moved(array, axis, mask):
    size = lax.axis_size(axis)
    return lax.ppermute(array, axis, [(i, i ^ mask) for i in range(size)])


def across(array):
    return moved(array, "mp", 1)


def beside_x(a):
    return moved(a, "rows", 1)


def beside_y(a):
    return moved(a, "rows", 2)


def along_z(a, z):
    return moved(a, "mp", 2 * z)


def fence(*trees):
    return lax.optimization_barrier(trees)


def relative(a):
    r = lax.axis_index("rows")
    low = [jnp.where(r & 1, a[i ^ 1], a[i]) for i in range(4)]
    return [jnp.where(r & 2, low[i ^ 2], low[i]) for i in range(4)]


def added(*terms):
    total = terms[0].astype(F32)
    for term in terms[1:]:
        total = total + term.astype(F32)
    return total.astype(BF16)


def stack_z(r, parts):
    n = parts[0].shape[0]
    return pack(r, parts, [(i, None, n, i * n) for i in range(3)])


def stack_all(r, quarters, s, x, y, dx, dy):
    n, cut = quarters.shape[1], dx.shape[0]
    plan = [(0, j, n, 4 * n * j) for j in range(4)]
    plan += [(1, None, 3 * n, n), (2, None, 3 * n, 5 * n), (3, None, 3 * n, 9 * n), (4, None, cut, 13 * n), (5, None, 3 * n - cut, 13 * n + cut)]
    return pack(r, [quarters, s, x, y, dx, dy], plan, 4).reshape(4, 4, n, -1)


def second_hop(g, ax, ay):
    cut = ax.shape[0]
    to_x = jnp.concatenate([g[1][:cut], added(g[1][cut:], ay)], axis=0)
    to_y = jnp.concatenate([added(g[2][:cut], ax), g[2][cut:]], axis=0)
    return to_x, to_y


def shard_of(f, fx, fy, fd):
    return jnp.stack(relative([f, fx, fy, fd])).astype(F32)


def any_spread(parts):
    core = lax.axis_index("mp") % 2
    return [lax.dynamic_index_in_dim(parts, c, 0, False) for c in (core, 1 - core)]


def any_reduced(full, axis):
    return lax.psum(lax.psum_scatter(full, "mp", scatter_dimension=axis, tiled=True), "rows")


def up_biases(w):
    return w[:, :, 96, :PAIR].reshape(1, -1)


def up_sums(total, pairs):
    return jnp.pad(total.reshape(4, 4, 1, PAIR)[:, pairs], ((0, 0), (0, 0), (0, 7), (0, 0)))


def stacked_vectors(one, two, loss):
    d = one.shape[1]
    at = lax.axis_index("rows") * lax.axis_size("mp") + lax.axis_index("mp")
    losses = jnp.where(jnp.arange(d, dtype=jnp.int32) == at, loss[0, 0] / math.sqrt(SLOTS * d), 0.0)
    return jnp.stack([one[0], two[0], one[1], two[2], two[1], two[3], losses, jnp.zeros_like(losses)])


def any_mesh(tokens, qkv_rows, qv_bias, out_weight, up_rows, up_bias, down_weight, gains, shifts, live, col, line, cotangent):
    d = tokens.shape[1]
    every = lambda a, axis=0: lax.all_gather(a, "mp", axis=axis, tiled=True)
    heads = lambda a: a.reshape(2, 4, 4, PART, d).swapaxes(1, 2)
    qkv_all, qvb_all = every(qkv_rows, 1), every(qv_bias, 1)
    small = lambda a: jnp.tile(a.reshape(2, 4, 4, PART).swapaxes(1, 2), (1, 1, 1, 4))
    bias = jnp.concatenate([every(up_bias).reshape(2, 4, 4, PAIR), small(qvb_all[0]), small(qvb_all[1])], axis=3)
    bias = jnp.pad(bias[:, :, :, None, :], ((0, 0), (0, 0), (0, 0), (0, PIECE - 97), (0, d - 3 * PAIR)))
    wa, wb = any_spread(jnp.concatenate([heads(qkv_all[0]), heads(qkv_all[1]), heads(qkv_all[2]), bias], axis=3))
    ua, ub = any_spread(jnp.concatenate([every(up_rows).reshape(2, 4, 4, PAIR, d), heads(every(out_weight))], axis=3))
    da, db = [w.reshape(-1, d) for w in any_spread(every(down_weight).reshape(2, 4, 4, PAIR, d))]
    h1, gf = prep(tokens, cotangent, live, gains, shifts)
    *qkv_a, oa, la = attend(col, line, h1, wa)
    *qkv_b, ob, lb = attend(col, line, h1, wb)
    r, h2 = join(tokens, [oa, ob], ua, ub, gains, shifts)
    aa, sa = up(h2, ua, up_biases(wa))
    ab, sb = up(h2, ub, up_biases(wb))
    g_down, _ = outer(aa, across(ab), gf, across(gf))
    mixed, loss = down(aa, ab, da, db, r, gf, shifts)
    ga, gb, gr, branch, two = back(gf, sa, sb, da, db, ua, ub, r, gains)
    g_up, total = outer(ga, across(gb), h2, across(h2))
    back_b = attend_back(col, line, branch, ub, 0, *qkv_b, ob, lb)
    back_a = attend_back(col, line, branch, ua, 0, *qkv_a, oa, la)
    pairs = [(a, across(b)) for a, b in zip(back_a, back_b)]
    g_attn = outer_attn(*pairs, (oa, across(ob)), (h1, across(h1)), (branch, across(branch)), up_sums(total, slice(0, 4)))
    g_attn = jnp.stack(g_attn).reshape(4, 4, ATTN, d)
    input_grad, one = finish([(*back_a, 0, 0), (*back_b, 0, 1)], wa, wb, tokens, gr, gains)
    vectors = lax.psum(stacked_vectors(one, two, loss), ("rows", "mp"))
    core = lax.axis_index("mp") % 2
    full = lambda g: lax.dynamic_update_index_in_dim(jnp.zeros((2,) + g.shape, F32), g.astype(F32), core, 0)
    down_grad, up_grad = [any_reduced(full(jnp.concatenate(g)).reshape(-1, d), 0) for g in (g_down, g_up)]
    ordered = lambda g: full(g).swapaxes(1, 2).reshape(-1, g.shape[-1])
    out_grad = any_reduced(ordered(g_attn[:, :, PIECE:]), 0)
    qkv_grad = any_reduced(jnp.stack([ordered(g_attn[:, :, i * PART : (i + 1) * PART]) for i in range(3)]), 1)
    up_bias_grad = any_reduced(full(g_attn[:, :, 96, :PAIR]).reshape(-1), 0)
    ordered = lambda g: full(g).swapaxes(1, 2).reshape(-1)
    qv_bias_grad = any_reduced(jnp.stack([ordered(g_attn[:, :, 96, at : at + PART]) for at in (PAIR, 2 * PAIR)]), 1)
    return mixed, input_grad, qkv_grad, qv_bias_grad, out_grad, up_grad, up_bias_grad, down_grad, vectors


def small_mesh(tokens, qkv_rows, qv_bias, out_weight, up_rows, up_bias, down_weight, gains, shifts, live, col, line, cotangent):
    d = tokens.shape[1]
    row = lax.axis_index("rows")
    r = row.reshape(1).astype(jnp.int32)
    mine = lambda a: lax.dynamic_index_in_dim(a, row, 0, False)
    xy = lambda s: (beside_x(s), beside_y(s))
    zs = lambda p, which=(1, 2, 3): [along_z(p, z) for z in which]

    def corner(x, y):
        cut = halves(x.shape[0])
        return beside_x(y[:cut]), beside_y(x[cut:])

    bias = jnp.concatenate(
        [up_bias.reshape(4, PAIR), jnp.tile(qv_bias[0].reshape(4, PART), (1, 4)), jnp.tile(qv_bias[1].reshape(4, PART), (1, 4))], axis=1
    )
    bias = jnp.pad(bias[:, None, :], ((0, 0), (0, PIECE - 97), (0, d - 3 * PAIR)))
    a4 = jnp.concatenate([qkv_rows.reshape(3, 4, PART, d).swapaxes(0, 1).reshape(4, 3 * PART, d), bias], axis=1)
    za = zs(mine(a4))
    b4 = jnp.concatenate([up_rows.reshape(4, PAIR, d), out_weight.reshape(4, PART, d)], axis=1)
    c4 = down_weight.reshape(4, PAIR, d)
    pb, pc = mine(b4), mine(c4)
    h1, gf = prep(tokens, cotangent, live, gains, shifts)
    a0 = pack(r, [a4], [(0, j, PIECE, j * PIECE) for j in range(4)]).reshape(4, 1, PIECE, d)
    *qkv_a0, oa0, la0 = attend(col, line, h1, a0, 0, 1)
    za, b4, c4, pb, pc, h1, gf, oa0 = fence(za, b4, c4, pb, pc, h1, gf, oa0)
    s_a = stack_z(r, za)
    x_a, y_a = xy(s_a)
    zb = zs(pb, (1, 2))
    h1_x, gf_x = across(h1), across(gf)
    x_a, y_a, zb, pb, h1_x, gf_x = fence(x_a, y_a, zb, pb, h1_x, gf_x)
    dx, dy = corner(x_a, y_a)
    zb = zb + zs(pb, (3,))
    dx, dy, zb, pc = fence(dx, dy, zb, pc)
    wa = stack_all(r, a4, s_a, x_a, y_a, dx, dy)
    wb = across(wa)
    s_b = stack_z(r, zb)
    x_b, y_b = xy(s_b)
    zc = zs(pc, (1, 2))
    *qkv_a1, oa1, la1 = attend(col, line, h1, wa, 1, 3)
    wb, x_b, y_b, zc, oa1, pc = fence(wb, x_b, y_b, zc, oa1, pc)
    dx, dy = corner(x_b, y_b)
    zc = zc + zs(pc, (3,))
    *qkv_b1, ob1, lb1 = attend(col, line, h1, wb, 1, 3)
    dx, dy, zc, ob1, wb = fence(dx, dy, zc, ob1, wb)
    ua = stack_all(r, b4, s_b, x_b, y_b, dx, dy)
    ub = across(ua)
    s_c = stack_z(r, zc)
    x_c, y_c = xy(s_c)
    *qkv_b0, ob0, lb0 = attend(col, line, h1, wb, 0, 1)
    res, h2 = join(tokens, [oa0, oa1, ob0, ob1], ua, ub, gains, shifts)
    x_c, y_c, ub, res, h2 = fence(x_c, y_c, ub, res, h2)
    dx, dy = corner(x_c, y_c)
    ab, sb = up(h2, ub, up_biases(wb))
    dx, dy, ab, h2 = fence(dx, dy, ab, h2)
    da = stack_all(r, c4, s_c, x_c, y_c, dx, dy).reshape(-1, d)
    db = across(da)
    ab_x, h2_x = across(ab), across(h2)
    ob0_x, ob1_x = across(ob0), across(ob1)
    aa, sa = up(h2, ua, up_biases(wa))
    db, ab_x, h2_x, ob0_x, ob1_x, aa = fence(db, ab_x, h2_x, ob0_x, ob1_x, aa)
    g, _ = outer(aa, ab_x, gf, gf_x)
    g, db = fence(g, db)
    ax, ay = beside_x(g[3]), beside_y(g[4])
    mixed, loss = down(aa, ab, da, db, res, gf, shifts)
    ax, ay, mixed, loss, db = fence(ax, ay, mixed, loss, db)
    to_x, to_y = second_hop(g, ax, ay)
    fx, fy = beside_x(to_x), beside_y(to_y)
    ga, gb, gr, branch, two = back(gf, sa, sb, da, db, ua, ub, res, gains)
    fx, fy, ga, gb, gr, branch = fence(fx, fy, ga, gb, gr, branch)
    t = added(g[0], fx, fy).reshape(4, PAIR, d)
    zr = [along_z(t[z], z) for z in (1, 2, 3)]
    gb_x, branch_x = across(gb), across(branch)
    back_b1 = attend_back(col, line, branch, ub, 1, *qkv_b1, ob1, lb1)
    zr, gb_x, branch_x, back_b1 = fence(zr, gb_x, branch_x, back_b1)
    f = added(t[0], *zr)
    fx, fy = beside_x(f), beside_y(f)
    back_b1_x = [across(a) for a in back_b1]
    g, total = outer(ga, gb_x, h2, h2_x)
    fx, fy, back_b1_x, g, branch = fence(fx, fy, back_b1_x, g, branch)
    ax, ay, fd = beside_x(g[3]), beside_y(g[4]), beside_x(fy)
    back_a1 = attend_back(col, line, branch, ua, 1, *qkv_a1, oa1, la1)
    ax, ay, fd, back_a1, h1 = fence(ax, ay, fd, back_a1, h1)
    down_grad = shard_of(f, fx, fy, fd).reshape(-1, d)
    to_x, to_y = second_hop(g, ax, ay)
    fx, fy = beside_x(to_x), beside_y(to_y)
    pairs = list(zip(back_a1, back_b1_x))
    n1 = outer_attn(*pairs, (oa1, ob1_x), (h1, h1_x), (branch, branch_x), up_sums(total, slice(1, 4)))
    back_b0 = attend_back(col, line, branch, ub, 0, *qkv_b0, ob0, lb0)
    fx, fy, n1, back_b0, branch = fence(fx, fy, n1, back_b0, branch)
    t = added(g[0], fx, fy).reshape(4, PAIR, d)
    zr = [along_z(t[z], z) for z in (1, 2, 3)]
    cut = halves(n1[3].shape[0])
    ax, ay = beside_x(n1[3][:cut]), beside_y(n1[3][cut:])
    back_b0_x = [across(a) for a in back_b0]
    back_a0 = attend_back(col, line, branch, ua, 0, *qkv_a0, oa0, la0)
    zr, ax, ay, back_b0_x, back_a0, h1 = fence(zr, ax, ay, back_b0_x, back_a0, h1)
    f = added(t[0], *zr)
    fx, fy = beside_x(f), beside_y(f)
    to_x, to_y = second_hop(n1, ax, ay)
    ex, ey = beside_x(to_x), beside_y(to_y)
    pairs = list(zip(back_a0, back_b0_x))
    n0 = outer_attn(*pairs, (oa0, ob0_x), (h1, h1_x), (branch, branch_x), up_sums(total, slice(0, 1)))
    fx, fy, ex, ey, n0, wa = fence(fx, fy, ex, ey, n0, wa)
    fd = beside_x(fy)
    t = added(n1[0], ex, ey).reshape(3, ATTN, d)
    zr = [along_z(t[z - 1], z) for z in (1, 2, 3)]
    cut = halves(n0[3].shape[0])
    ax, ay = beside_x(n0[3][:cut]), beside_y(n0[3][cut:])
    grads = [(*back_a0, 0, 0), (*back_a1, 1, 0), (*back_b0, 0, 1), (*back_b1, 1, 1)]
    input_grad, one = finish(grads, wa, wb, tokens, gr, gains)
    fd, zr, ax, ay, input_grad, one = fence(fd, zr, ax, ay, input_grad, one)
    to_x, to_y = second_hop(n0, ax, ay)
    ex, ey = beside_x(to_x), beside_y(to_y)
    vectors = stacked_vectors(one, two, loss)
    vx = beside_x(vectors)
    up_grad = shard_of(f, fx, fy, fd).reshape(-1, d)
    ex, ey, vx, up_grad = fence(ex, ey, vx, up_grad)
    f = added(n0[0], ex, ey, *zr)
    fx, fy = beside_x(f), beside_y(f)
    vectors = vectors + vx
    vy = beside_y(vectors)
    fx, fy, vy = fence(fx, fy, vy)
    fd = beside_x(fy)
    vectors = vectors + vy
    vc = across(vectors)
    fd, vc = fence(fd, vc)
    vectors = vectors + vc
    vz = zs(vectors)
    vectors = (vectors + vz[0]) + (vz[1] + vz[2])
    last = shard_of(f, fx, fy, fd)
    qkv_grad = last[:, : 3 * PART].reshape(4, 3, PART, d).swapaxes(0, 1).reshape(3, -1, d)
    up_bias_grad = last[:, 96, :PAIR].reshape(-1)
    qv_bias_grad = jnp.stack([last[:, 96, at : at + PART].reshape(-1) for at in (PAIR, 2 * PAIR)])
    out_grad = last[:, PIECE:].reshape(-1, d)
    return mixed, input_grad, qkv_grad, qv_bias_grad, out_grad, up_grad, up_bias_grad, down_grad, vectors


def body(tokens, qkv_weight, qv_bias, out_weight, up_weight, up_bias, down_weight, norm_gains, shift_vectors, lengths, cotangent):
    n, d = tokens.shape
    place, row = lax.axis_index("mp"), lax.axis_index("rows")
    endings = jnp.cumsum(lax.dynamic_slice_in_dim(lengths, place, 1, 0)[0])
    position = jnp.arange(SLOTS, dtype=jnp.int32)
    segment = jnp.sum((position[:, None] >= endings[None, :]).astype(jnp.int32), axis=1)
    live = (segment < DOCS).astype(F32)[:, None]
    ident = jnp.where(segment < DOCS, segment, DOCS + position).astype(jnp.int32)
    layer = small_mesh if (lax.axis_size("rows"), lax.axis_size("mp")) == (4, 8) else any_mesh
    mixed, input_grad, qkv_grad, qv_bias_grad, out_grad, up_grad, up_bias_grad, down_grad, vectors = layer(
        tokens, jnp.swapaxes(qkv_weight, 1, 2), qv_bias, out_weight, up_weight.T, up_bias, down_weight,
        norm_gains.astype(F32), shift_vectors.astype(F32), live, ident.reshape(n, 1), ident.reshape(1, n), cotangent,
    )
    share = d // lax.axis_size("mp")
    vector_grad = lax.dynamic_slice_in_dim(vectors[:6], place * share, share, 1)
    block_loss = lax.dynamic_slice_in_dim(vectors[6], row * lax.axis_size("mp"), lax.axis_size("mp"), 0)
    return (
        mixed, block_loss, input_grad, jnp.swapaxes(qkv_grad, 1, 2), qv_bias_grad, out_grad,
        up_grad.T, up_bias_grad, down_grad, vector_grad,
    )


def solution(mesh):
    placed = (
        P(("rows", "mp"), None),
        P(None, None, "mp"),
        P(None, "mp"),
        P("mp", None),
        P(None, "mp"),
        P("mp"),
        P("mp", None),
        P(),
        P(),
        P("rows", None),
        P(("rows", "mp"), None),
    )
    return jax.shard_map(
        body,
        mesh=mesh,
        in_specs=placed,
        out_specs=(
            P(("rows", "mp"), None),
            P("rows"),
            P(("rows", "mp"), None),
            P(None, None, "mp"),
            P(None, "mp"),
            P("mp", None),
            P(None, "mp"),
            P("mp"),
            P("mp", None),
            P(None, "mp"),
        ),
        check_vma=False,
    )
```

```python
import functools
import math

import jax
import jax.numpy as jnp
from jax import lax
from jax.experimental import pallas as pl
from jax.experimental.pallas import tpu as pltpu
from jax.sharding import PartitionSpec as P

HD = 64
PAIR = 128
PART = 32
ATTN = 144
TILE = 256
UNITS = 512
SCALE = 0.4e9
SLOTS = 1024
DOCS = 6
EPSILON = 1e-05
MASKED = -1e30
LOG2E = math.log2(math.e)
F32, BF16 = jnp.float32, jnp.bfloat16
NN = (((1,), (0,)), ((), ()))
NT = (((1,), (1,)), ((), ()))
TN = (((0,), (0,)), ((), ()))


def mm(a, b, dims):
    return lax.dot_general(a, b, dims, preferred_element_type=F32)


def whole(shape):
    return pl.BlockSpec(shape, lambda *_: (0,) * len(shape), pipeline_mode=pl.Buffered(1))


ANYWHERE = pl.BlockSpec(memory_space=pl.ANY)
FAR = pl.BlockSpec(memory_space=pltpu.HBM)
SCALARS = pl.BlockSpec(memory_space=pltpu.SMEM)


def call(kernel, grid, ins, outs, scratch=(), gflop=1.0, name=None, limit=56, aliases=None, far=()):
    nbytes = sum(a.size * a.dtype.itemsize for a, _ in ins)
    nbytes += sum(math.prod(s) * jnp.dtype(d).itemsize for s, d, _ in outs)
    return pl.pallas_call(
        kernel,
        grid=grid,
        in_specs=[s for _, s in ins],
        out_specs=[s for _, _, s in outs],
        out_shape=[pltpu.HBM(s, d) if i in far else jax.ShapeDtypeStruct(s, d) for i, (s, d, _) in enumerate(outs)],
        scratch_shapes=list(scratch),
        input_output_aliases=aliases or {},
        compiler_params=pltpu.CompilerParams(vmem_limit_bytes=limit << 20),
        cost_estimate=pl.CostEstimate(flops=int(gflop * SCALE), bytes_accessed=nbytes, transcendentals=0),
        name=name,
    )(*[a for a, _ in ins])


def normed(v):
    spread = v - jnp.mean(v, axis=1, keepdims=True)
    rstd = lax.rsqrt(jnp.mean(spread * spread, axis=1, keepdims=True) + EPSILON)
    return spread * rstd, rstd


def norm_back(v, gy, gain):
    norm, rstd = normed(v)
    gn = gy * gain
    gv = rstd * (gn - jnp.mean(gn, axis=1, keepdims=True) - norm * jnp.mean(gn * norm, axis=1, keepdims=True))
    return gv, gy * norm


def column_sums(*values):
    d = values[0].shape[1]
    rows = [jnp.sum(v, axis=0, keepdims=True) for v in values]
    return jnp.concatenate(rows + [jnp.zeros((8 - len(rows), d), F32)], axis=0)


def prep_kernel(x_ref, cot_ref, live_ref, gain_ref, shift_ref, h_ref, gf_ref):
    norm, _ = normed(x_ref[...].astype(F32))
    h_ref[...] = (norm * gain_ref[0:1, :] + shift_ref[0:1, :]).astype(BF16)
    gf_ref[...] = (cot_ref[...].astype(F32) * live_ref[...]).astype(BF16)


def prep(x, cot, live, gains, shifts):
    n, d = x.shape
    rows = pl.BlockSpec((TILE, d), lambda i: (i, 0))
    return call(
        prep_kernel, (n // TILE,),
        [(x, rows), (cot, rows), (live, pl.BlockSpec((TILE, 1), lambda i: (i, 0))), (gains, whole(gains.shape)), (shifts, whole(shifts.shape))],
        [((n, d), BF16, rows), ((n, d), BF16, rows)], gflop=1.0, name="prep", limit=20,
    )


def fill_mask(bias_ref, col_ref, row_ref, transposed):
    n = col_ref.shape[0]
    for i in range(n // TILE):
        part, upto = slice(i * TILE, (i + 1) * TILE), (i + 1) * TILE
        if transposed:
            same = col_ref[:upto, :] == row_ref[:, part]
            key = lax.broadcasted_iota(jnp.int32, (upto, TILE), 0)
            query = lax.broadcasted_iota(jnp.int32, (upto, TILE), 1) + i * TILE
            bias_ref[:upto, part] = jnp.where(same & (key <= query), 0.0, MASKED)
        else:
            same = col_ref[part, :] == row_ref[:, :upto]
            query = lax.broadcasted_iota(jnp.int32, (TILE, upto), 0) + i * TILE
            key = lax.broadcasted_iota(jnp.int32, (TILE, upto), 1)
            bias_ref[part, :upto] = jnp.where(same & (key <= query), 0.0, MASKED)


def pair_bias(pieces, at):
    lane = lax.broadcasted_iota(jnp.int32, (1, PAIR), 1) // PART
    row = jnp.zeros((1, PAIR), F32)
    for j in range(4):
        row = jnp.where(lane == j, pieces[j][4 * PART : ATTN, at : at + PAIR].astype(F32)[0:1, :], row)
    return row


def split_heads(a):
    first = lax.broadcasted_iota(jnp.int32, (1, PAIR), 1) < HD
    zero = jnp.zeros((), a.dtype)
    return jnp.where(first, a, zero), jnp.where(first, zero, a)


def attend_kernel(r_ref, col_ref, row_ref, h_ref, *refs, mode, stacked, count):
    w_refs, refs = refs[:count], refs[count + (STACKS if stacked else 0) :]
    qkv_ref, o_ref, lse_ref, up_ref = refs[:STACKS]
    bias_ref, held_ref = refs[-2:]
    n = h_ref.shape[0]

    @pl.when(pl.program_id(0) == 0)
    def _():
        fill_mask(bias_ref, col_ref, row_ref, False)

    if mode == "packed":
        for p in range(count):

            @pl.when(pl.program_id(0) == p)
            def _():
                held_ref[...] = w_refs[p][...]
    else:
        for j in range(4):
            piece = w_refs[0][r_ref[0] ^ j] if mode == "quarters" else w_refs[j][...]
            held_ref[j] = piece
            refs[STACKS][j] = piece
    pieces = [held_ref[j] for j in range(4)]
    up_ref[0] = jnp.concatenate([piece[4 * PART :, :PAIR].astype(F32)[0:1] for piece in pieces], axis=0)
    wall = jnp.concatenate([pieces[j][i * PART : (i + 1) * PART] for i in (1, 2, 3) for j in range(4)], axis=0)
    qkv = mm(h_ref[...], wall, NT)
    qkv_ref[:, :PAIR] = ((qkv[:, :PAIR] + pair_bias(pieces, 128)) * HD**-0.5).astype(BF16)
    qkv_ref[:, PAIR : 2 * PAIR] = qkv[:, PAIR : 2 * PAIR].astype(BF16)
    v = (qkv[:, 2 * PAIR :] + pair_bias(pieces, 256)).astype(BF16)
    qkv_ref[:, 2 * PAIR :] = v
    vx = jnp.concatenate([v, jnp.ones((n, PAIR), BF16)], axis=1)
    first = lax.broadcasted_iota(jnp.int32, (1, PAIR), 1) < HD
    work = [(i, h) for i in range(n // TILE) for h in range(2)]
    outs = {}

    def scores(i, h):
        q = split_heads(qkv_ref[i * TILE : (i + 1) * TILE, :PAIR])[h]
        return mm(q, qkv_ref[: (i + 1) * TILE, PAIR : 2 * PAIR], NT)

    def weigh(i, h, e, top):
        part = slice(i * TILE, (i + 1) * TILE)
        ov = mm(e, vx[: (i + 1) * TILE], NN)
        total = ov[:, PAIR:]
        outs[h] = ov[:, :PAIR] / total
        lse_ref[0, h : h + 1, part] = jnp.transpose(top + jnp.log(total))[0:1, :]
        if h:
            o_ref[part, :] = jnp.where(first, outs[0], outs[1]).astype(BF16)

    s, held = scores(*work[0]), None
    for t, (i, h) in enumerate(work):
        ahead = scores(*work[t + 1]) if t + 1 < len(work) else None
        s = s + bias_ref[i * TILE : (i + 1) * TILE, : (i + 1) * TILE]
        top = jnp.max(s, axis=1, keepdims=True)
        e = jnp.exp2((s - top) * LOG2E).astype(BF16)
        if held is not None:
            weigh(*work[t - 1], *held)
        s, held = ahead, (e, top)
    weigh(*work[-1], *held)


STACKS = 4


def attend(r, col, row, h, w, mode, z, stacks=None):
    n, d = h.shape
    pairs = len(w) if mode == "packed" else 1
    outs = [
        ((n, 12 * PAIR), BF16, pl.BlockSpec((n, 3 * PAIR), lambda p: (0, z + p))),
        ((n, 4 * PAIR), BF16, pl.BlockSpec((n, PAIR), lambda p: (0, z + p))),
        ((4, 2, n), F32, pl.BlockSpec((1, 2, n), lambda p: (z + p, 0, 0))),
        ((4, 4, PAIR), F32, pl.BlockSpec((1, 4, PAIR), lambda p: (z + p, 0, 0))),
    ]
    if mode != "packed":
        outs.append(((4, ATTN, d), BF16, whole((4, ATTN, d))))
    ins = [(r, SCALARS), (col, whole(col.shape)), (row, whole(row.shape)), (h, whole(h.shape))] + [(a, whole(a.shape)) for a in w]
    aliases = {len(ins) + i: i for i in range(STACKS)} if stacks else None
    ins += [(a, FAR) for a in stacks or ()]
    *stacks, last = *call(
        functools.partial(attend_kernel, mode=mode, stacked=bool(aliases), count=len(w)), (pairs,), ins, outs,
        [pltpu.VMEM((n, n), F32), pltpu.VMEM((4, ATTN, d), BF16)], gflop=5.0 * pairs, name="attend", limit=28, aliases=aliases, far=range(STACKS),
    ), *([None] if mode == "packed" else [])
    return stacks, last


def out_copies(refs, held_ref, sem):
    return [[pltpu.make_async_copy(ref.at[:, pl.ds(0, PART)], held_ref.at[i], sem.at[i]) for i, ref in enumerate(refs)]]


def join_kernel(x_ref, oa_ref, ob_ref, gain_ref, shift_ref, *refs):
    r_ref, h_ref, held_ref, sem = refs[8:]

    @pl.when(pl.program_id(0) == 0)
    def _():
        copies = out_copies(refs[:8], held_ref, sem)
        begin(copies)
        end(copies[0])

    half = lambda a: held_ref[a : a + 4].reshape(4 * PAIR, -1)
    branch = mm(oa_ref[...], half(0), NN) + mm(ob_ref[...], half(4), NN)
    r = x_ref[...].astype(F32) + (branch + shift_ref[1:2, :])
    r_ref[...] = r
    norm, _ = normed(r)
    h_ref[...] = (norm * gain_ref[1:2, :] + shift_ref[2:3, :]).astype(BF16)


def join(x, oa, ob, ws, gains, shifts):
    n, d = x.shape
    rows = pl.BlockSpec((TILE, d), lambda i: (i, 0))
    half = pl.BlockSpec((TILE, 4 * PAIR), lambda i: (i, 0))
    return call(
        join_kernel, (n // TILE,),
        [(x, rows), (oa, half), (ob, half), (gains, whole(gains.shape)), (shifts, whole(shifts.shape))] + [(w, FAR) for w in ws],
        [((n, d), F32, rows), ((n, d), BF16, rows)], [pltpu.VMEM((8, 4, PART, d), BF16), pltpu.SemaphoreType.DMA((8,))],
        gflop=4.0, name="join", limit=24, far=(0,),
    )


def unit_copies(w_ref, held_ref, sem, first):
    spans = [(j * UNITS, first + j * UNITS) for j in range(4)]
    return [[pltpu.make_async_copy(w_ref.at[pl.ds(a, UNITS)], held_ref.at[pl.ds(b, UNITS)], sem.at[b // UNITS])] for a, b in spans]


def gathered_copies(place_ref, w_ref, held_ref, sem, half, first):
    r, at, core = place_ref[0], place_ref[1], place_ref[2]
    copies = []
    for j in range(4):
        lo = first + j * UNITS
        source = lambda z: w_ref.at[((r ^ j) * 4 + (at ^ z)) * 2 + (core ^ half)]
        copies.append([pltpu.make_async_copy(source(z), held_ref.at[pl.ds(lo + z * PAIR, PAIR)], sem.at[lo // PAIR + z]) for z in range(4)])
    return copies


def begin(copies):
    for pair in copies:
        for copy in pair:
            copy.start()


def end(pair):
    for copy in pair:
        copy.wait()


def up_kernel(place_ref, h_ref, bias_ref, w_ref, act_ref, slope_ref, held_ref, sem, *, half):
    copies = gathered_copies(place_ref, w_ref, held_ref, sem, half, 0)
    step = pl.program_id(0)

    @pl.when(step == 0)
    def _():
        begin(copies)

    for j in range(4):

        @pl.when(step == j)
        def _():
            end(copies[j])
            u = mm(h_ref[...], held_ref[j * UNITS : (j + 1) * UNITS, :], NT)
            u = u + jnp.concatenate([bias_ref[z, j : j + 1, :] for z in range(4)], axis=1)
            c0, c1 = math.sqrt(2 / math.pi), math.sqrt(2 / math.pi) * 0.044715
            square = u * u
            s = 0.5 + 0.5 * jnp.tanh(u * (c0 + c1 * square))
            us = u * s
            act_ref[...] = us.astype(BF16)
            slope_ref[...] = (s + (us - us * s) * (2 * c0 + 6 * c1 * square)).astype(BF16)


def up(place, h, w, bias, half):
    n, d = h.shape
    blk = pl.BlockSpec((n, UNITS), lambda i: (0, i))
    shape = (n, 4 * UNITS)
    return call(
        functools.partial(up_kernel, half=half), (4,),
        [(place, SCALARS), (h, whole(h.shape)), (bias, whole(bias.shape)), (w, FAR)],
        [(shape, BF16, blk), (shape, BF16, blk)],
        [pltpu.VMEM((4 * UNITS, d), BF16), pltpu.SemaphoreType.DMA((16,))], gflop=6.0, name="up", limit=28, far=(0, 1),
    )


def down_kernel(aa_ref, ab_ref, res_ref, gf_ref, shift_ref, wa_ref, wb_ref, mixed_ref, loss_ref, held_ref, sem):
    half = 4 * UNITS
    copies = unit_copies(wa_ref, held_ref, sem, 0) + unit_copies(wb_ref, held_ref, sem, half)
    step = pl.program_id(0)

    def rest(feed):
        out = res_ref[...] + (feed + shift_ref[3:4, :])
        mixed_ref[...] = out.astype(BF16)
        loss = jnp.sum(out * gf_ref[...].astype(F32), axis=0, keepdims=True)
        loss = jnp.broadcast_to(jnp.sum(loss, axis=1, keepdims=True), loss_ref.shape)
        loss_ref[...] = jnp.where(step == 0, loss, loss_ref[...] + loss)

    @pl.when(step == 0)
    def _():
        begin(copies)
        feed = None
        for c in range(8):
            end(copies[c])
            a_ref, lo = (aa_ref, c * UNITS) if c < 4 else (ab_ref, (c - 4) * UNITS)
            part = mm(a_ref[:, lo : lo + UNITS], held_ref[c * UNITS : (c + 1) * UNITS, :], NN)
            feed = part if feed is None else feed + part
        rest(feed)

    @pl.when(step > 0)
    def _():
        rest(mm(aa_ref[...], held_ref[:half, :], NN) + mm(ab_ref[...], held_ref[half:, :], NN))


def down(aa, ab, wa, wb, res, gf, shifts):
    n, d = res.shape
    rows = pl.BlockSpec((TILE, d), lambda i: (i, 0))
    units = pl.BlockSpec((TILE, 4 * UNITS), lambda i: (i, 0))
    return call(
        down_kernel, (n // TILE,),
        [(aa, units), (ab, units), (res, rows), (gf, rows), (shifts, whole(shifts.shape)), (wa, ANYWHERE), (wb, ANYWHERE)],
        [((n, d), BF16, rows), ((8, 128), F32, whole((8, 128)))],
        [pltpu.VMEM((8 * UNITS, d), BF16), pltpu.SemaphoreType.DMA((8,))], gflop=9.0, name="down", limit=50,
    )


def slope_kernel(gf_ref, sa_ref, sb_ref, wa_ref, wb_ref, ga_ref, gb_ref, held_ref, sem):
    copies = unit_copies(wa_ref, held_ref, sem, 0) + unit_copies(wb_ref, held_ref, sem, 4 * UNITS)
    step = pl.program_id(0)

    def tile(first):
        def product(c):
            if first:
                end(copies[c])
            return mm(gf_ref[...], held_ref[c * UNITS : (c + 1) * UNITS, :], NT)

        g = product(0)
        for c in range(8):
            ahead = product(c + 1) if c < 7 else None
            s_ref, g_ref, lo = (sa_ref, ga_ref, c * UNITS) if c < 4 else (sb_ref, gb_ref, (c - 4) * UNITS)
            g_ref[:, lo : lo + UNITS] = (g * s_ref[:, lo : lo + UNITS].astype(F32)).astype(BF16)
            g = ahead

    @pl.when(step == 0)
    def _():
        begin(copies)
        tile(True)

    @pl.when(step > 0)
    def _():
        tile(False)


def slope(gf, sa, sb, wa, wb):
    n, d = gf.shape
    units = pl.BlockSpec((TILE, 4 * UNITS), lambda i: (i, 0))
    return call(
        slope_kernel, (n // TILE,),
        [(gf, pl.BlockSpec((TILE, d), lambda i: (i, 0))), (sa, units), (sb, units), (wa, ANYWHERE), (wb, ANYWHERE)],
        [(sa.shape, BF16, units), (sb.shape, BF16, units)],
        [pltpu.VMEM((8 * UNITS, d), BF16), pltpu.SemaphoreType.DMA((8,))], gflop=9.0, name="slope", limit=50, far=(0, 1),
    )


def back_kernel(place_ref, ga_ref, gb_ref, gf_ref, res_ref, gain_ref, w_ref, *refs):
    gr_ref, br_ref, oa_ref, ob_ref, vec_ref, held_ref, out_ref, sem, out_sem = refs[8:]
    half = 4 * UNITS
    copies = [c for i in range(2) for c in gathered_copies(place_ref, w_ref, held_ref, sem, i, i * half)]
    outs = out_copies(refs[:8], out_ref, out_sem)
    step = pl.program_id(0)

    def rest(gy, first):
        c = gf_ref[...].astype(F32)
        gv, terms = norm_back(res_ref[...], gy, gain_ref[1:2, :])
        gr = c + gv
        gr_ref[...] = gr
        branch = gr.astype(BF16)
        br_ref[...] = branch
        if first:
            end(outs[0])
        go = mm(branch, out_ref[...].reshape(8 * PAIR, -1), NT).astype(BF16)
        oa_ref[...] = go[:, : 4 * PAIR]
        ob_ref[...] = go[:, 4 * PAIR :]
        sums = column_sums(terms, gy, branch.astype(F32), c)
        vec_ref[...] = sums if first else vec_ref[...] + sums

    @pl.when(step == 0)
    def _():
        begin(copies)
        begin(outs)
        gy = None
        for c in range(8):
            end(copies[c])
            g_ref, lo = (ga_ref, c * UNITS) if c < 4 else (gb_ref, (c - 4) * UNITS)
            part = mm(g_ref[:, lo : lo + UNITS], held_ref[c * UNITS : (c + 1) * UNITS, :], NN)
            gy = part if gy is None else gy + part
        rest(gy, True)

    @pl.when(step > 0)
    def _():
        rest(mm(ga_ref[...], held_ref[:half, :], NN) + mm(gb_ref[...], held_ref[half:, :], NN), False)


def back(place, ga, gb, gf, w, ws, res, gains):
    n, d = res.shape
    rows = pl.BlockSpec((TILE, d), lambda i: (i, 0))
    units = pl.BlockSpec((TILE, 4 * UNITS), lambda i: (i, 0))
    heads = pl.BlockSpec((TILE, 4 * PAIR), lambda i: (i, 0))
    return call(
        back_kernel, (n // TILE,),
        [(place, SCALARS), (ga, units), (gb, units), (gf, rows), (res, rows), (gains, whole(gains.shape)), (w, FAR)] + [(w, FAR) for w in ws],
        [((n, d), F32, rows), ((n, d), BF16, rows), ((n, 4 * PAIR), BF16, heads), ((n, 4 * PAIR), BF16, heads), ((8, d), F32, whole((8, d)))],
        [pltpu.VMEM((8 * UNITS, d), BF16), pltpu.VMEM((8, 4, PART, d), BF16), pltpu.SemaphoreType.DMA((32,)), pltpu.SemaphoreType.DMA((8,))],
        gflop=12.0, name="back", limit=50, far=(0,),
    )


def outer_kernel(la_ref, lb_ref, ra_ref, rb_ref, *refs):
    outs, sum_ref, held_ref, sem = refs[:4], refs[4], refs[5], refs[6]
    step = pl.program_id(0)
    copies = [[pltpu.make_async_copy(held_ref.at[j % 2], outs[j], sem.at[j])] for j in range(4)]
    for j in (2, 3):

        @pl.when(step == j)
        def _():
            end(copies[j - 2])

    held_ref[step % 2] = (mm(la_ref[...], ra_ref[...], TN) + mm(lb_ref[...], rb_ref[...], TN)).astype(BF16)
    for j in range(4):

        @pl.when(step == j)
        def _():
            begin((copies[j],))

    sum_ref[...] = jnp.sum(la_ref[...].astype(F32) + lb_ref[...].astype(F32), axis=0, keepdims=True)

    @pl.when(step == 3)
    def _():
        end(copies[2])
        end(copies[3])


def outer_all_kernel(lb_ref, la_ref, r_ref, gb_ref, ga_ref):
    for half, (l_ref, g_ref) in enumerate(((lb_ref, gb_ref), (la_ref, ga_ref))):

        @pl.when((pl.program_id(0) >= 4) == (half == 1))
        def _():
            g_ref[0] = mm(l_ref[...], r_ref[...], TN).astype(BF16)


def outer_all(lb, la, right):
    n, d = right.shape
    low, high = (lambda p: jnp.minimum(p, 3)), (lambda p: jnp.maximum(p - 4, 0))
    tile = lambda at: pl.BlockSpec((n, UNITS), lambda p: (0, at(p)))
    out = lambda at: ((4, UNITS, d), BF16, pl.BlockSpec((1, UNITS, d), lambda p: (at(p), 0, 0)))
    return call(
        outer_all_kernel, (8,), [(lb, tile(low)), (la, tile(high)), (right, whole(right.shape))], [out(low), out(high)],
        gflop=9.0, name="outer_all", limit=30, far=(0, 1),
    )


def outer(la, lb, ra, rb):
    n, m = la.shape
    d = ra.shape[1]
    tile = pl.BlockSpec((n, UNITS), lambda i: (0, i))
    *g, total = call(
        outer_kernel, (4,),
        [(la, tile), (lb, tile), (ra, whole(ra.shape)), (rb, whole(rb.shape))],
        [((UNITS, d), BF16, ANYWHERE)] * 4 + [((1, m), F32, pl.BlockSpec((1, UNITS), lambda i: (0, i)))],
        [pltpu.VMEM((2, UNITS, d), BF16), pltpu.SemaphoreType.DMA((4,))], gflop=9.0, name="outer", limit=40,
    )
    return g, total


def attend_back_kernel(col_ref, row_ref, go_ref, qkv_ref, o_ref, lse_ref, g_ref, bias_ref, p_ref, d_ref):
    n = go_ref.shape[0]

    @pl.when(pl.program_id(0) == 0)
    def _():
        fill_mask(bias_ref, col_ref, row_ref, True)

    q_at, k_at, v_at = slice(0, PAIR), slice(PAIR, 2 * PAIR), slice(2 * PAIR, 3 * PAIR)
    k_turned = jnp.transpose(qkv_ref[:, k_at])
    work = [(i, h) for i in range(n // TILE) for h in range(2)]
    qs, gs, deltas, halves = {}, {}, {}, {}

    def products(i, h):
        part, upto = slice(i * TILE, (i + 1) * TILE), (i + 1) * TILE
        if h == 0:
            go = go_ref[part, :]
            qs[i], gs[i] = split_heads(qkv_ref[part, q_at]), split_heads(go)
            both = jnp.transpose(go.astype(F32) * o_ref[part, :].astype(F32))
            deltas[i] = [jnp.sum(both[k * HD : (k + 1) * HD], axis=0, keepdims=True) for k in range(2)]
        return mm(qkv_ref[:upto, k_at], qs[i][h], NT), mm(qkv_ref[:upto, v_at], gs[i][h], NT)

    def query_grad(i, h, ds):
        part, upto = slice(i * TILE, (i + 1) * TILE), (i + 1) * TILE
        halves[h] = mm(k_turned[h * HD : (h + 1) * HD, :upto], ds, NN)
        if h:
            gq = jnp.transpose(jnp.concatenate([halves[0], halves[1]], axis=0))
            g_ref[part, q_at] = (gq.astype(BF16).astype(F32) * HD**-0.5).astype(BF16)

    now, held = products(*work[0]), None
    for t, (i, h) in enumerate(work):
        part, upto = slice(i * TILE, (i + 1) * TILE), (i + 1) * TILE
        ahead = products(*work[t + 1]) if t + 1 < len(work) else None
        p = jnp.exp2((now[0] + bias_ref[:upto, part] - lse_ref[0, h : h + 1, part]) * LOG2E)
        ds = (p * (now[1] - deltas[i][h])).astype(BF16)
        p_ref[h, :upto, part] = p.astype(BF16)
        d_ref[h, :upto, part] = ds
        if held is not None:
            query_grad(*work[t - 1], held)
        now, held = ahead, ds
    query_grad(*work[-1], held)
    qa, qb = split_heads(qkv_ref[:, q_at])
    ga, gb = split_heads(go_ref[...])
    for i in range(n // TILE):
        part, lo = slice(i * TILE, (i + 1) * TILE), i * TILE
        g_ref[part, k_at] = (mm(d_ref[0, part, lo:], qa[lo:], NN) + mm(d_ref[1, part, lo:], qb[lo:], NN)).astype(BF16)
        g_ref[part, v_at] = (mm(p_ref[0, part, lo:], ga[lo:], NN) + mm(p_ref[1, part, lo:], gb[lo:], NN)).astype(BF16)


def attend_back(col, row, go, stacks, base, pairs):
    qkv, o, lse = stacks[:3]
    n = go.shape[0]
    pair = pl.BlockSpec((n, PAIR), lambda p: (0, p + base))
    return call(
        attend_back_kernel, (pairs,),
        [(col, whole(col.shape)), (row, whole(row.shape)), (go, pair), (qkv, pl.BlockSpec((n, 3 * PAIR), lambda p: (0, p + base))), (o, pair),
         (lse, pl.BlockSpec((1, 2, n), lambda p: (p + base, 0, 0)))],
        [((n, 3 * PAIR * pairs), BF16, pl.BlockSpec((n, 3 * PAIR), lambda p: (0, p)))],
        [pltpu.VMEM((n, n), F32), pltpu.VMEM((2, n, n), BF16), pltpu.VMEM((2, n, n), BF16)],
        gflop=5.0 * pairs, name="attend_back", limit=32,
    )[0]


def outer_attn_kernel(gb_ref, ga_ref, ob_ref, oa_ref, h_ref, branch_ref, up_ref, nb_ref, na_ref, *, pairs):
    d = h_ref.shape[1]
    for half, (g_ref, o_ref, n_ref) in enumerate(((gb_ref, ob_ref, nb_ref), (ga_ref, oa_ref, na_ref))):

        @pl.when((pl.program_id(0) >= pairs) == (half == 1))
        def _():
            out = mm(o_ref[...], branch_ref[...], TN).astype(BF16)
            qkv = mm(g_ref[...], h_ref[...], TN).astype(BF16)
            sums = jnp.sum(g_ref[...].astype(F32), axis=0, keepdims=True)
            qsum, vsum = sums[:, :PAIR], sums[:, 2 * PAIR :]
            for j in range(4):
                turn = lambda a: jnp.concatenate([a[:, j * PART :], a[:, : j * PART]], axis=1) if j else a
                up = up_ref[j, 0, 0:1, :] if half else jnp.zeros((1, PAIR), F32)
                line = jnp.concatenate([up, turn(qsum), turn(vsum), jnp.zeros((1, d - 3 * PAIR), F32)], axis=1)
                line = jnp.concatenate([line, jnp.zeros((15, d), F32)], axis=0).astype(BF16)
                rows = [out[j * PART : (j + 1) * PART]] + [qkv[i * PAIR + j * PART : i * PAIR + (j + 1) * PART] for i in range(3)]
                n_ref[j] = jnp.concatenate(rows + [line], axis=0)


def outer_attn(gb, ga, ob, oa, base, h, branch, upsum):
    n, m = ga.shape
    d = h.shape[1]
    pairs = m // (3 * PAIR)
    low, high = (lambda p: jnp.minimum(p, pairs - 1)), (lambda p: jnp.maximum(p - pairs, 0))
    grad = lambda at: pl.BlockSpec((n, 3 * PAIR), lambda p: (0, at(p)))
    head = lambda at: pl.BlockSpec((n, PAIR), lambda p: (0, at(p) + base))
    out = lambda at: ((4, pairs * ATTN, d), BF16, pl.BlockSpec((4, ATTN, d), lambda p: (0, at(p), 0)))
    return call(
        functools.partial(outer_attn_kernel, pairs=pairs), (2 * pairs,),
        [(gb, grad(low)), (ga, grad(high)), (ob, head(low)), (oa, head(high)), (h, whole(h.shape)), (branch, whole(branch.shape)),
         (upsum, pl.BlockSpec((4, 1, 8, PAIR), lambda p: (0, high(p), 0, 0)))],
        [out(low), out(high)], gflop=2.5 * pairs, name="outer_attn", limit=30,
    )


def combine_kernel(a_ref, b_ref, *outs):
    for j in range(4):

        @pl.when(pl.program_id(0) == j)
        def _():
            outs[j][...] = (a_ref[0].astype(F32) + b_ref[0].astype(F32)).astype(BF16)


def combine(a, b):
    _, m, d = a.shape
    block = pl.BlockSpec((1, m, d), lambda j: (j, 0, 0))
    return call(combine_kernel, (4,), [(a, block), (b, block)], [((m, d), BF16, whole((m, d)))] * 4, gflop=0.1, name="combine", limit=20)


def finish_kernel(*refs, plan):
    grads, w_refs = refs[: len(plan)], refs[len(plan) : len(plan) + 8]
    x_ref, gr_ref, gain_ref, out_ref, vec_ref, held_ref, sem = refs[len(plan) + 8 :]
    step = pl.program_id(0)
    copies, spans, lo = [], [], 0
    for half, base, count in plan:
        spans.append(slice(3 * lo, 3 * (lo + count)))
        mine = []
        for z in range(base, base + count):
            for i in range(3):
                at = 3 * lo + i
                mine.append(pltpu.make_async_copy(w_refs[4 * half + z].at[:, pl.ds((1 + i) * PART, PART)], held_ref.at[at], sem.at[at]))
            lo += 1
        copies.append(mine)

    def tile(first):
        gy = None
        for g_ref, span, mine in zip(grads, spans, copies):
            if first:
                end(mine)
            part = mm(g_ref[...], held_ref[span].reshape(g_ref.shape[1], -1), NN)
            gy = part if gy is None else gy + part
        gv, terms = norm_back(x_ref[...].astype(F32), gy, gain_ref[0:1, :])
        out_ref[...] = gr_ref[...] + gv
        sums = column_sums(terms, gy)
        vec_ref[...] = sums if first else vec_ref[...] + sums

    @pl.when(step == 0)
    def _():
        begin(copies)
        tile(True)

    @pl.when(step > 0)
    def _():
        tile(False)


def finish(grads, ws, x, gr, gains):
    n, d = x.shape
    rows = pl.BlockSpec((TILE, d), lambda i: (i, 0))
    plan = tuple((half, base, g.shape[1] // (3 * PAIR)) for g, half, base in grads)
    return call(
        functools.partial(finish_kernel, plan=plan), (n // TILE,),
        [(g, pl.BlockSpec((TILE, g.shape[1]), lambda i: (i, 0))) for g, _, _ in grads]
        + [(w, FAR) for w in ws] + [(x, rows), (gr, rows), (gains, whole(gains.shape))],
        [((n, d), F32, rows), ((8, d), F32, whole((8, d)))],
        [pltpu.VMEM((24, 4, PART, d), BF16), pltpu.SemaphoreType.DMA((24,))], gflop=10.0, name="finish", limit=56,
    )


def pack_kernel(r_ref, *refs, plan, bands):
    srcs, (out_ref, held_ref, in_sem, out_sem) = refs[:-4], refs[-4:]
    copies = []
    for at, (src, quarter, count, dst) in enumerate(plan):
        source = srcs[src] if quarter is None else srcs[src].at[r_ref[0] ^ quarter]
        copies.append(pltpu.make_async_copy(source, held_ref.at[pl.ds(dst, count)], in_sem.at[at]))
    begin((copies,))
    band = held_ref.shape[0] // bands
    outs = []
    for b in range(bands):
        end([copy for copy, (_, _, _, dst) in zip(copies, plan) if dst // band == b])
        outs.append(pltpu.make_async_copy(held_ref.at[pl.ds(b * band, band)], out_ref.at[pl.ds(b * band, band)], out_sem.at[b]))
        begin((outs[-1:],))
    end(outs)


def pack(r, arrays, plan, bands):
    rows = sum(count for _, _, count, _ in plan)
    d = arrays[0].shape[-1]
    return call(
        functools.partial(pack_kernel, plan=plan, bands=bands), (), [(r, SCALARS)] + [(a, ANYWHERE) for a in arrays], [((rows, d), BF16, ANYWHERE)],
        [pltpu.VMEM((rows, d), BF16), pltpu.SemaphoreType.DMA((len(plan),)), pltpu.SemaphoreType.DMA((bands,))], gflop=0.0, name="pack", limit=14,
    )[0]


def stack_z(r, parts):
    n = parts[0].shape[0]
    return pack(r, parts, [(i, None, n, i * n) for i in range(3)], 3)


def stack_units(r, quarters, sides):
    n = quarters.shape[1]
    plan = [(0, j, n, 4 * n * j) for j in range(4)] + [(1 + j, None, 3 * n, 4 * n * j + n) for j in range(4)]
    return pack(r, [quarters, *sides], plan, 4)


def settle_kernel(r_ref, *refs):
    qkv_ref, bias_ref, out_ref, up_ref, held_ref = refs[4:]
    for j in range(4):
        held_ref[j] = refs[j][...]
    quarters = [held_ref[r_ref[0] ^ q].astype(F32) for q in range(4)]
    for i in range(3):
        qkv_ref[i] = jnp.transpose(jnp.concatenate([a[(1 + i) * PART : (2 + i) * PART] for a in quarters], axis=0))
    bias_ref[...] = jnp.concatenate([a[4 * PART : 4 * PART + 1, : 3 * PAIR] for a in quarters] + [jnp.zeros((4, 3 * PAIR), F32)], axis=0)
    out_ref[...] = jnp.concatenate([a[:PART] for a in quarters], axis=0)
    for q in range(4):
        up_ref[:, q * PAIR : (q + 1) * PAIR] = jnp.transpose(quarters[q][ATTN:])


def settle(r, pieces):
    d = pieces[0].shape[1]
    shapes = [(3, d, PAIR), (8, 3 * PAIR), (PAIR, d), (d, 4 * PAIR)]
    return call(
        settle_kernel, (), [(r, SCALARS)] + [(a, whole(a.shape)) for a in pieces], [(shape, F32, whole(shape)) for shape in shapes],
        [pltpu.VMEM((4, ATTN + PAIR, d), BF16)], gflop=0.1, name="settle", limit=24,
    )


def moved(array, axis, mask):
    size = lax.axis_size(axis)
    return lax.ppermute(array, axis, [(i, i ^ mask) for i in range(size)])


def across(array):
    return moved(array, "mp", 1)


def beside(array, j):
    return moved(array, "rows", j)


def along_z(array, z):
    return moved(array, "mp", 2 * z)


def fence(*trees):
    return lax.optimization_barrier(trees)


def by_z(a):
    z = lax.axis_index("mp") // 2
    low = [jnp.where(z & 1, a[i ^ 1], a[i]) for i in range(4)]
    return [jnp.where(z & 2, low[i ^ 2], low[i]) for i in range(4)]


def added(*terms):
    total = terms[0].astype(F32)
    for term in terms[1:]:
        total = total + term.astype(F32)
    return total.astype(BF16)


def any_spread(parts):
    core = lax.axis_index("mp") % 2
    return [lax.dynamic_index_in_dim(parts, c, 0, False) for c in (core, 1 - core)]


def any_reduced(full, axis):
    return lax.psum(lax.psum_scatter(full, "mp", scatter_dimension=axis, tiled=True), "rows")


def up_sums(total, first, last):
    return jnp.pad(total.reshape(4, 4, 1, PAIR)[:, first:last], ((0, 0), (0, 0), (0, 7), (0, 0)))


def stacked_vectors(one, two, loss):
    d = one.shape[1]
    at = lax.axis_index("rows") * lax.axis_size("mp") + lax.axis_index("mp")
    losses = jnp.where(jnp.arange(d, dtype=jnp.int32) == at, loss[0, 0] / math.sqrt(SLOTS * d), 0.0)
    return jnp.stack([one[0], two[0], one[1], two[2], two[1], two[3], losses, jnp.zeros_like(losses)])


def any_mesh(tokens, qkv_rows, qv_bias, out_weight, up_rows, up_bias, down_weight, gains, shifts, live, col, line, cotangent):
    d = tokens.shape[1]
    r = jnp.zeros((1,), jnp.int32)
    every = lambda a, axis=0: lax.all_gather(a, "mp", axis=axis, tiled=True)
    heads = lambda a: a.reshape(2, 4, 4, PART, d)
    qkv_all, qvb_all = every(qkv_rows, 1), every(qv_bias, 1)
    small = lambda a: jnp.tile(a.reshape(2, 4, 4, PART), (1, 1, 1, 4))
    ups = every(up_bias).reshape(2, 4, 4, PAIR).swapaxes(1, 2)
    bias = jnp.concatenate([ups, small(qvb_all[0]), small(qvb_all[1])], axis=3)
    bias = jnp.pad(bias[:, :, :, None, :], ((0, 0), (0, 0), (0, 0), (0, 15), (0, d - 3 * PAIR)))
    wa, wb = any_spread(jnp.concatenate([heads(every(out_weight)), heads(qkv_all[0]), heads(qkv_all[1]), heads(qkv_all[2]), bias], axis=3))

    place = jnp.zeros((3,), jnp.int32)
    da, db = any_spread(every(down_weight).reshape(2, 16 * PAIR, d))
    by_half = jnp.stack(any_spread(every(up_rows).reshape(2, 4, 4, PAIR, d)))
    up_all = jnp.moveaxis(by_half, 0, 2).reshape(32, PAIR, d)
    h1, gf = prep(tokens, cotangent, live, gains, shifts)
    stacks, ws = [], [w[z] for w in (wa, wb) for z in range(4)]
    for w in (wa, wb):
        stacks.append(attend(r, col, line, h1, [w[0], w[1], w[2], w[3]], "packed", 0)[0])
    stack_a, stack_b = stacks
    res, h2 = join(tokens, stack_a[1], stack_b[1], ws, gains, shifts)
    aa, sa = up(place, h2, up_all, stack_a[3], 0)
    ab, sb = up(place, h2, up_all, stack_b[3], 1)
    down_b, down_a = outer_all(ab, aa, gf)
    g_down = added(down_a, across(down_b))
    mixed, loss = down(aa, ab, da, db, res, gf, shifts)
    ga, gb = slope(gf, sa, sb, da, db)
    gr, branch, go_a, go_b, two = back(place, ga, gb, gf, up_all, ws, res, gains)
    g_up, total = outer(ga, across(gb), h2, across(h2))
    back_b = attend_back(col, line, go_b, stack_b, 0, 4)
    back_a = attend_back(col, line, go_a, stack_a, 0, 4)
    nb, na = outer_attn(back_b, back_a, stack_b[1], stack_a[1], 0, h1, branch, up_sums(total, 0, 4))
    g_attn = added(na, across(nb)).reshape(4, 4, ATTN, d)
    input_grad, one = finish([(back_a, 0, 0), (back_b, 1, 0)], ws, tokens, gr, gains)
    vectors = lax.psum(stacked_vectors(one, two, loss), ("rows", "mp"))
    core = lax.axis_index("mp") % 2
    full = lambda g: lax.dynamic_update_index_in_dim(jnp.zeros((2,) + g.shape, F32), g.astype(F32), core, 0)
    ordered = lambda g: full(g).swapaxes(1, 2).reshape(-1, g.shape[-1])
    down_grad, up_grad = any_reduced(full(g_down).reshape(-1, d), 0), any_reduced(full(jnp.concatenate(g_up)).reshape(-1, d), 0)
    out_grad = any_reduced(ordered(g_attn[:, :, :PART]), 0)
    qkv_grad = any_reduced(jnp.stack([ordered(g_attn[:, :, i * PART : (i + 1) * PART]) for i in (1, 2, 3)]), 1)
    lines = g_attn[:, :, 4 * PART]
    up_bias_grad = any_reduced(full(lines[:, :, :PAIR]).reshape(-1), 0)
    ordered = lambda g: full(g).swapaxes(1, 2).reshape(-1)
    qv_bias_grad = any_reduced(jnp.stack([ordered(lines[:, :, at : at + PART]) for at in (PAIR, 2 * PAIR)]), 1)
    qkv_grad, up_grad = jnp.swapaxes(qkv_grad, 1, 2), up_grad.T
    return mixed, input_grad, qkv_grad, qv_bias_grad, out_grad, up_grad, up_bias_grad, down_grad, vectors


def small_mesh(tokens, qkv_rows, qv_bias, out_weight, up_rows, up_bias, down_weight, gains, shifts, live, col, line, cotangent):
    d = tokens.shape[1]
    row = lax.axis_index("rows")
    r = row.reshape(1).astype(jnp.int32)
    mine = lambda a: lax.dynamic_index_in_dim(a, row, 0, False)
    sides = lambda a: [beside(a, j) for j in (1, 2, 3)]
    sides3 = lambda g: [beside(g[j], j) for j in (1, 2, 3)]

    bias = jnp.concatenate(
        [up_bias.reshape(4, PAIR), jnp.tile(qv_bias[0].reshape(4, PART), (1, 4)), jnp.tile(qv_bias[1].reshape(4, PART), (1, 4))], axis=1
    )
    bias = jnp.pad(bias[:, None, :], ((0, 0), (0, 15), (0, d - 3 * PAIR)))
    qkv4 = qkv_rows.reshape(3, 4, PART, d).swapaxes(0, 1).reshape(4, 3 * PART, d)
    a4 = jnp.concatenate([out_weight.reshape(4, PART, d), qkv4, bias], axis=1)
    pa = mine(a4)
    c4 = down_weight.reshape(4, PAIR, d)
    pc = mine(c4)
    index = lax.axis_index("mp").astype(jnp.int32)
    place = jnp.stack([row.astype(jnp.int32), index // 2, index % 2])
    up_all = lax.all_gather(mine(up_rows.reshape(4, PAIR, d)), ("rows", "mp"))
    p1, c2 = along_z(pa, 1), along_z(pc, 2)
    h1, gf = prep(tokens, cotangent, live, gains, shifts)
    p1, c2, h1, gf, pa, pc = fence(p1, c2, h1, gf, pa, pc)
    s1, p2 = sides(p1), along_z(pa, 2)
    sa, w0 = attend(r, col, line, h1, [a4], "quarters", 0)
    s1, p2, sa, w0, h1, pa = fence(s1, p2, sa, w0, h1, pa)
    s2, p3, x0 = sides(p2), along_z(pa, 3), across(w0)
    sa, w1 = attend(r, col, line, h1, [p1, *s1], "pieces", 1, sa)
    s2, p3, x0, sa, w1, h1, pc = fence(s2, p3, x0, sa, w1, h1, pc)
    s3, c1, c3 = sides(p3), along_z(pc, 1), along_z(pc, 3)
    sa, w2 = attend(r, col, line, h1, [p2, *s2], "pieces", 2, sa)
    sb, _ = attend(r, col, line, h1, [x0], "packed", 0)
    s3, c1, c3, sa, w1, w2, sb, h1 = fence(s3, c1, c3, sa, w1, w2, sb, h1)
    cs = stack_z(r, [c1, c2, c3])
    cx = [beside(cs, 1), beside(cs, 2)]
    x1, x2 = across(w1), across(w2)
    sb, _ = attend(r, col, line, h1, [x1, x2], "packed", 1, sb)
    sa, w3 = attend(r, col, line, h1, [p3, *s3], "pieces", 3, sa)
    cx, sa, sb, w3, h1, cs = fence(cx, sa, sb, w3, h1, cs)
    cx, x3 = [*cx, beside(cs, 3)], across(w3)
    ws = [w0, w1, w2, w3, x0, x1, x2, x3]
    sb, _ = attend(r, col, line, h1, [x3], "packed", 3, sb)
    res, h2 = join(tokens, sa[1], sb[1], ws, gains, shifts)
    ab, lb = up(place, h2, up_all, sb[3], 1)
    aa, la = up(place, h2, up_all, sa[3], 0)
    cx, aa, ab, la, lb, h2 = fence(cx, aa, ab, la, lb, h2)
    da = stack_units(r, c4, [cs, *cx])
    db = across(da)
    down_b, down_a = outer_all(ab, aa, gf)
    da, db, down_a, down_b = fence(da, db, down_a, down_b)
    down_x = across(down_b)
    ga, gb = slope(gf, la, lb, da, db)
    down_x, ga, gb, h2 = fence(down_x, ga, gb, h2)
    g_down = combine(down_a, down_x)
    fx, gb_x, h2_x = sides3(g_down), across(gb), across(h2)
    gr, branch, go_a, go_b, two = back(place, ga, gb, gf, up_all, ws, res, gains)
    back_b1 = attend_back(col, line, go_b, sb, 2, 2)
    g_up, total = outer(ga, gb_x, h2, h2_x)
    fx, gr, branch, go_a, go_b, back_b1, g_up, total = fence(fx, gr, branch, go_a, go_b, back_b1, g_up, total)
    td = added(g_down[0], *fx).reshape(4, PAIR, d)
    columns = [[2 * i + core for i in range(4)] for core in range(2)]
    f_down = lax.psum_scatter(jnp.stack(by_z(td)), "mp", scatter_dimension=0, tiled=False, axis_index_groups=columns)
    down_sum = lax.all_gather(f_down, "rows")
    fx = sides3(g_up)
    back_a1 = attend_back(col, line, go_a, sa, 2, 2)
    nb1, na1 = outer_attn(back_b1, back_a1, sb[1], sa[1], 2, h1, branch, up_sums(total, 2, 4))
    back_b2 = attend_back(col, line, go_b, sb, 0, 2)
    back_a2 = attend_back(col, line, go_a, sa, 0, 2)
    nb2, na2 = outer_attn(back_b2, back_a2, sb[1], sa[1], 0, h1, branch, up_sums(total, 0, 2))
    fx, back_a1, back_b2, back_a2, nb1, na1, nb2, na2, aa = fence(fx, back_a1, back_b2, back_a2, nb1, na1, nb2, na2, aa)
    tu = added(g_up[0], *fx).reshape(4, PAIR, d)
    n1_x, n2_x = across(nb1), across(nb2)
    zu = [along_z(tu[i], i) for i in (1, 2)]
    mixed, loss = down(aa, ab, da, db, res, gf, shifts)
    n1_x, n2_x, zu, mixed, loss, tu, gr = fence(n1_x, n2_x, zu, mixed, loss, tu, gr)
    n1, n2 = combine(na1, n1_x), combine(na2, n2_x)
    ex, u3 = sides3(n1), along_z(tu[3], 3)
    input_grad, one = finish([(back_a2, 0, 0), (back_a1, 0, 2), (back_b2, 1, 0), (back_b1, 1, 2)], ws, tokens, gr, gains)
    ex, u3, input_grad, one, n2 = fence(ex, u3, input_grad, one, n2)
    t1 = added(n1[0], *ex).reshape(2, ATTN, d)
    ex, y2, y3 = sides3(n2), along_z(t1[0], 2), along_z(t1[1], 3)
    vectors = stacked_vectors(one, two, loss)
    ex, y2, y3, vectors, down_sum = fence(ex, y2, y3, vectors, down_sum)
    t2 = added(n2[0], *ex).reshape(2, ATTN, d)
    y1, vx = along_z(t2[1], 1), sides(vectors)
    vx, y1, vectors, t2 = fence(vx, y1, vectors, t2)
    f = jnp.concatenate([added(t2[0], y1, y2, y3), added(tu[0], *zu, u3)], axis=0)
    d_last = sides(f)
    vectors = (vectors + vx[0]) + (vx[1] + vx[2])
    vectors = vectors + across(vectors)
    vz = [along_z(vectors, i) for i in (1, 2, 3)]
    vectors = (vectors + vz[0]) + (vz[1] + vz[2])
    down_grad = down_sum.reshape(-1, d).astype(F32)
    d_last, down_grad, vectors = fence(d_last, down_grad, vectors)
    qkv_grad, biases, out_grad, up_grad = settle(r, [f, *d_last])
    up_bias_grad = biases[:4, :PAIR].reshape(-1)
    qv_bias_grad = jnp.stack([biases[:4, at : at + PART].reshape(-1) for at in (PAIR, 2 * PAIR)])
    return mixed, input_grad, qkv_grad, qv_bias_grad, out_grad, up_grad, up_bias_grad, down_grad, vectors


def body(tokens, qkv_weight, qv_bias, out_weight, up_weight, up_bias, down_weight, norm_gains, shift_vectors, lengths, cotangent):
    n, d = tokens.shape
    place, row = lax.axis_index("mp"), lax.axis_index("rows")
    endings = jnp.cumsum(lax.dynamic_slice_in_dim(lengths, place, 1, 0)[0])
    position = jnp.arange(SLOTS, dtype=jnp.int32)
    segment = jnp.sum((position[:, None] >= endings[None, :]).astype(jnp.int32), axis=1)
    live = (segment < DOCS).astype(F32)[:, None]
    ident = jnp.where(segment < DOCS, segment, DOCS + position).astype(jnp.int32)
    layer = small_mesh if (lax.axis_size("rows"), lax.axis_size("mp")) == (4, 8) else any_mesh
    mixed, input_grad, qkv_grad, qv_bias_grad, out_grad, up_grad, up_bias_grad, down_grad, vectors = layer(
        tokens, jnp.swapaxes(qkv_weight, 1, 2), qv_bias, out_weight, up_weight.T, up_bias, down_weight,
        norm_gains.astype(F32), shift_vectors.astype(F32), live, ident.reshape(n, 1), ident.reshape(1, n), cotangent,
    )
    share = d // lax.axis_size("mp")
    vector_grad = lax.dynamic_slice_in_dim(vectors[:6], place * share, share, 1)
    block_loss = lax.dynamic_slice_in_dim(vectors[6], row * lax.axis_size("mp"), lax.axis_size("mp"), 0)
    return (
        mixed, block_loss, input_grad, qkv_grad, qv_bias_grad, out_grad,
        up_grad, up_bias_grad, down_grad, vector_grad,
    )


def solution(mesh):
    placed = (
        P(("rows", "mp"), None),
        P(None, None, "mp"),
        P(None, "mp"),
        P("mp", None),
        P(None, "mp"),
        P("mp"),
        P("mp", None),
        P(),
        P(),
        P("rows", None),
        P(("rows", "mp"), None),
    )
    return jax.shard_map(
        body,
        mesh=mesh,
        in_specs=placed,
        out_specs=(
            P(("rows", "mp"), None),
            P("rows"),
            P(("rows", "mp"), None),
            P(None, None, "mp"),
            P(None, "mp"),
            P("mp", None),
            P(None, "mp"),
            P("mp"),
            P("mp", None),
            P(None, "mp"),
        ),
        check_vma=False,
    )
```

```python
import functools
import math

import jax
import jax.numpy as jnp
from jax import lax
from jax.experimental import pallas as pl
from jax.experimental.pallas import tpu as pltpu
from jax.sharding import PartitionSpec as P

HD = 64
PAIR = 128
PART = 32
ATTN = 144
TILE = 256
UNITS = 512
SCALE = 0.4e9
SLOTS = 1024
DOCS = 6
EPSILON = 1e-05
MASKED = -1e30
LOG2E = math.log2(math.e)
F32, BF16 = jnp.float32, jnp.bfloat16
NN = (((1,), (0,)), ((), ()))
NT = (((1,), (1,)), ((), ()))
TN = (((0,), (0,)), ((), ()))


def mm(a, b, dims):
    return lax.dot_general(a, b, dims, preferred_element_type=F32)


def whole(shape):
    return pl.BlockSpec(shape, lambda *_: (0,) * len(shape), pipeline_mode=pl.Buffered(1))


ANYWHERE = pl.BlockSpec(memory_space=pl.ANY)
FAR = pl.BlockSpec(memory_space=pltpu.HBM)
SCALARS = pl.BlockSpec(memory_space=pltpu.SMEM)


def call(kernel, grid, ins, outs, scratch=(), gflop=1.0, name=None, limit=56, aliases=None, far=()):
    nbytes = sum(a.size * a.dtype.itemsize for a, _ in ins)
    nbytes += sum(math.prod(s) * jnp.dtype(d).itemsize for s, d, _ in outs)
    return pl.pallas_call(
        kernel,
        grid=grid,
        in_specs=[s for _, s in ins],
        out_specs=[s for _, _, s in outs],
        out_shape=[pltpu.HBM(s, d) if i in far else jax.ShapeDtypeStruct(s, d) for i, (s, d, _) in enumerate(outs)],
        scratch_shapes=list(scratch),
        input_output_aliases=aliases or {},
        compiler_params=pltpu.CompilerParams(vmem_limit_bytes=limit << 20),
        cost_estimate=pl.CostEstimate(flops=int(gflop * SCALE), bytes_accessed=nbytes, transcendentals=0),
        name=name,
    )(*[a for a, _ in ins])


def normed(v):
    spread = v - jnp.mean(v, axis=1, keepdims=True)
    rstd = lax.rsqrt(jnp.mean(spread * spread, axis=1, keepdims=True) + EPSILON)
    return spread * rstd, rstd


def norm_back(v, gy, gain):
    norm, rstd = normed(v)
    gn = gy * gain
    gv = rstd * (gn - jnp.mean(gn, axis=1, keepdims=True) - norm * jnp.mean(gn * norm, axis=1, keepdims=True))
    return gv, gy * norm


def column_sums(*values):
    d = values[0].shape[1]
    rows = [jnp.sum(v, axis=0, keepdims=True) for v in values]
    return jnp.concatenate(rows + [jnp.zeros((8 - len(rows), d), F32)], axis=0)


def prep_kernel(x_ref, cot_ref, live_ref, gain_ref, shift_ref, h_ref, gf_ref):
    norm, _ = normed(x_ref[...].astype(F32))
    h_ref[...] = (norm * gain_ref[0:1, :] + shift_ref[0:1, :]).astype(BF16)
    gf_ref[...] = (cot_ref[...].astype(F32) * live_ref[...]).astype(BF16)


def prep(x, cot, live, gains, shifts):
    n, d = x.shape
    rows = pl.BlockSpec((TILE, d), lambda i: (i, 0))
    return call(
        prep_kernel, (n // TILE,),
        [(x, rows), (cot, rows), (live, pl.BlockSpec((TILE, 1), lambda i: (i, 0))), (gains, whole(gains.shape)), (shifts, whole(shifts.shape))],
        [((n, d), BF16, rows), ((n, d), BF16, rows)], gflop=1.0, name="prep", limit=20,
    )


def fill_mask(bias_ref, row_ref, transposed):
    n = row_ref.shape[1]
    col = jnp.transpose(jnp.broadcast_to(row_ref[...], (8, n)))[:, :1]
    for i in range(n // TILE):
        part, upto = slice(i * TILE, (i + 1) * TILE), (i + 1) * TILE
        if transposed:
            same = col[:upto, :] == row_ref[:, part]
            key = lax.broadcasted_iota(jnp.int32, (upto, TILE), 0)
            query = lax.broadcasted_iota(jnp.int32, (upto, TILE), 1) + i * TILE
            bias_ref[:upto, part] = jnp.where(same & (key <= query), 0.0, MASKED)
        else:
            same = col[part, :] == row_ref[:, :upto]
            query = lax.broadcasted_iota(jnp.int32, (TILE, upto), 0) + i * TILE
            key = lax.broadcasted_iota(jnp.int32, (TILE, upto), 1)
            bias_ref[part, :upto] = jnp.where(same & (key <= query), 0.0, MASKED)


def pair_bias(pieces, at):
    lane = lax.broadcasted_iota(jnp.int32, (1, PAIR), 1) // PART
    row = jnp.zeros((1, PAIR), F32)
    for j in range(4):
        row = jnp.where(lane == j, pieces[j][4 * PART : ATTN, at : at + PAIR].astype(F32)[0:1, :], row)
    return row


def split_heads(a):
    first = lax.broadcasted_iota(jnp.int32, (1, PAIR), 1) < HD
    zero = jnp.zeros((), a.dtype)
    return jnp.where(first, a, zero), jnp.where(first, zero, a)


def attend_kernel(r_ref, row_ref, h_ref, *refs, mode, stacked, count):
    w_refs, refs = refs[:count], refs[count + (STACKS if stacked else 0) :]
    qkv_ref, o_ref, lse_ref, up_ref = refs[:STACKS]
    bias_ref, held_ref = refs[-2:]
    n = h_ref.shape[0]

    @pl.when(pl.program_id(0) == 0)
    def _():
        fill_mask(bias_ref, row_ref, False)

    if mode == "packed":
        for p in range(count):

            @pl.when(pl.program_id(0) == p)
            def _():
                held_ref[...] = w_refs[p][...]
    else:
        for j in range(4):
            piece = w_refs[0][r_ref[0] ^ j] if mode == "quarters" else w_refs[j][...]
            held_ref[j] = piece
            refs[STACKS][j] = piece
    pieces = [held_ref[j] for j in range(4)]
    up_ref[0] = jnp.concatenate([piece[4 * PART :, :PAIR].astype(F32)[0:1] for piece in pieces], axis=0)
    wall = jnp.concatenate([pieces[j][i * PART : (i + 1) * PART] for i in (1, 2, 3) for j in range(4)], axis=0)
    qkv = mm(h_ref[...], wall, NT)
    qkv_ref[:, :PAIR] = ((qkv[:, :PAIR] + pair_bias(pieces, 128)) * HD**-0.5).astype(BF16)
    qkv_ref[:, PAIR : 2 * PAIR] = qkv[:, PAIR : 2 * PAIR].astype(BF16)
    v = (qkv[:, 2 * PAIR :] + pair_bias(pieces, 256)).astype(BF16)
    qkv_ref[:, 2 * PAIR :] = v
    vx = jnp.concatenate([v, jnp.ones((n, PAIR), BF16)], axis=1)
    first = lax.broadcasted_iota(jnp.int32, (1, PAIR), 1) < HD
    work = [(i, h) for i in range(n // TILE) for h in range(2)]
    outs = {}

    def scores(i, h):
        q = split_heads(qkv_ref[i * TILE : (i + 1) * TILE, :PAIR])[h]
        return mm(q, qkv_ref[: (i + 1) * TILE, PAIR : 2 * PAIR], NT)

    def weigh(i, h, e, top):
        part = slice(i * TILE, (i + 1) * TILE)
        ov = mm(e, vx[: (i + 1) * TILE], NN)
        total = ov[:, PAIR:]
        outs[h] = ov[:, :PAIR] / total
        lse_ref[0, h : h + 1, part] = jnp.transpose(top + jnp.log(total))[0:1, :]
        if h:
            o_ref[part, :] = jnp.where(first, outs[0], outs[1]).astype(BF16)

    s, held = scores(*work[0]), None
    for t, (i, h) in enumerate(work):
        ahead = scores(*work[t + 1]) if t + 1 < len(work) else None
        s = s + bias_ref[i * TILE : (i + 1) * TILE, : (i + 1) * TILE]
        top = jnp.max(s, axis=1, keepdims=True)
        e = jnp.exp2((s - top) * LOG2E).astype(BF16)
        if held is not None:
            weigh(*work[t - 1], *held)
        s, held = ahead, (e, top)
    weigh(*work[-1], *held)


STACKS = 4


def attend(r, row, h, w, mode, z, stacks=None):
    n, d = h.shape
    pairs = len(w) if mode == "packed" else 1
    outs = [
        ((n, 12 * PAIR), BF16, pl.BlockSpec((n, 3 * PAIR), lambda p: (0, z + p))),
        ((n, 4 * PAIR), BF16, pl.BlockSpec((n, PAIR), lambda p: (0, z + p))),
        ((4, 2, n), F32, pl.BlockSpec((1, 2, n), lambda p: (z + p, 0, 0))),
        ((4, 4, PAIR), F32, pl.BlockSpec((1, 4, PAIR), lambda p: (z + p, 0, 0))),
    ]
    if mode != "packed":
        outs.append(((4, ATTN, d), BF16, whole((4, ATTN, d))))
    ins = [(r, SCALARS), (row, whole(row.shape)), (h, whole(h.shape))] + [(a, whole(a.shape)) for a in w]
    aliases = {len(ins) + i: i for i in range(STACKS)} if stacks else None
    ins += [(a, FAR) for a in stacks or ()]
    *stacks, last = *call(
        functools.partial(attend_kernel, mode=mode, stacked=bool(aliases), count=len(w)), (pairs,), ins, outs,
        [pltpu.VMEM((n, n), F32), pltpu.VMEM((4, ATTN, d), BF16)], gflop=5.0 * pairs, name="attend", limit=28, aliases=aliases, far=range(STACKS),
    ), *([None] if mode == "packed" else [])
    return stacks, last


def out_copies(refs, held_ref, sem):
    return [[pltpu.make_async_copy(ref.at[:, pl.ds(0, PART)], held_ref.at[i], sem.at[i]) for i, ref in enumerate(refs)]]


def join_kernel(x_ref, oa_ref, ob_ref, gain_ref, shift_ref, *refs):
    r_ref, h_ref, held_ref, sem = refs[8:]

    @pl.when(pl.program_id(0) == 0)
    def _():
        copies = out_copies(refs[:8], held_ref, sem)
        begin(copies)
        end(copies[0])

    half = lambda a: held_ref[a : a + 4].reshape(4 * PAIR, -1)
    branch = mm(oa_ref[...], half(0), NN) + mm(ob_ref[...], half(4), NN)
    r = x_ref[...].astype(F32) + (branch + shift_ref[1:2, :])
    r_ref[...] = r
    norm, _ = normed(r)
    h_ref[...] = (norm * gain_ref[1:2, :] + shift_ref[2:3, :]).astype(BF16)


def join(x, oa, ob, ws, gains, shifts):
    n, d = x.shape
    rows = pl.BlockSpec((TILE, d), lambda i: (i, 0))
    half = pl.BlockSpec((TILE, 4 * PAIR), lambda i: (i, 0))
    return call(
        join_kernel, (n // TILE,),
        [(x, rows), (oa, half), (ob, half), (gains, whole(gains.shape)), (shifts, whole(shifts.shape))] + [(w, FAR) for w in ws],
        [((n, d), F32, rows), ((n, d), BF16, rows)], [pltpu.VMEM((8, 4, PART, d), BF16), pltpu.SemaphoreType.DMA((8,))],
        gflop=4.0, name="join", limit=56, far=(0,),
    )


def unit_copies(w_ref, held_ref, sem, first):
    spans = [(j * UNITS, first + j * UNITS) for j in range(4)]
    return [[pltpu.make_async_copy(w_ref.at[pl.ds(a, UNITS)], held_ref.at[pl.ds(b, UNITS)], sem.at[b // UNITS])] for a, b in spans]


def gathered_copies(place_ref, w_ref, held_ref, sem, half, first):
    r, at, core = place_ref[0], place_ref[1], place_ref[2]
    copies = []
    for j in range(4):
        lo = first + j * UNITS
        source = lambda z: w_ref.at[((r ^ j) * 4 + (at ^ z)) * 2 + (core ^ half)]
        copies.append([pltpu.make_async_copy(source(z), held_ref.at[pl.ds(lo + z * PAIR, PAIR)], sem.at[lo // PAIR + z]) for z in range(4)])
    return copies


def begin(copies):
    for pair in copies:
        for copy in pair:
            copy.start()


def end(pair):
    for copy in pair:
        copy.wait()


def up_kernel(place_ref, h_ref, gf_ref, bias_ref, w_ref, act_ref, slope_ref, g_ref, held_ref, sem, *, half):
    copies = gathered_copies(place_ref, w_ref, held_ref, sem, half, 0)
    step = pl.program_id(0)

    @pl.when(step == 0)
    def _():
        begin(copies)

    for j in range(4):

        @pl.when(step == j)
        def _():
            end(copies[j])
            bias = jnp.concatenate([bias_ref[z, j : j + 1, :] for z in range(4)], axis=1)
            c0, c1 = math.sqrt(2 / math.pi), math.sqrt(2 / math.pi) * 0.044715
            u = mm(h_ref[...], held_ref[j * UNITS : (j + 1) * UNITS, :], NT) + bias
            square = u * u
            s = 0.5 + 0.5 * jnp.tanh(u * (c0 + c1 * square))
            us = u * s
            act = us.astype(BF16)
            act_ref[...] = act
            slope_ref[...] = (s + (us - us * s) * (2 * c0 + 6 * c1 * square)).astype(BF16)
            g_ref[0] = mm(act, gf_ref[...], TN).astype(BF16)


def up(place, h, gf, w, bias, half):
    n, d = h.shape
    blk = pl.BlockSpec((n, UNITS), lambda i: (0, i))
    shape = (n, 4 * UNITS)
    return call(
        functools.partial(up_kernel, half=half), (4,),
        [(place, SCALARS), (h, whole(h.shape)), (gf, whole(gf.shape)), (bias, whole(bias.shape)), (w, FAR)],
        [(shape, BF16, blk), (shape, BF16, blk), ((4, UNITS, d), BF16, pl.BlockSpec((1, UNITS, d), lambda i: (i, 0, 0)))],
        [pltpu.VMEM((4 * UNITS, d), BF16), pltpu.SemaphoreType.DMA((16,))], gflop=6.0, name="up", limit=48, far=(0, 1, 2),
    )


def down_kernel(aa_ref, ab_ref, res_ref, gf_ref, shift_ref, wa_ref, wb_ref, mixed_ref, loss_ref, held_ref, sem):
    half = 4 * UNITS
    copies = unit_copies(wa_ref, held_ref, sem, 0) + unit_copies(wb_ref, held_ref, sem, half)
    step = pl.program_id(0)

    def rest(feed):
        out = res_ref[...] + (feed + shift_ref[3:4, :])
        mixed_ref[...] = out.astype(BF16)
        loss = jnp.sum(out * gf_ref[...].astype(F32), axis=0, keepdims=True)
        loss = jnp.broadcast_to(jnp.sum(loss, axis=1, keepdims=True), loss_ref.shape)
        loss_ref[...] = jnp.where(step == 0, loss, loss_ref[...] + loss)

    @pl.when(step == 0)
    def _():
        begin(copies)
        feed = None
        for c in range(8):
            end(copies[c])
            a_ref, lo = (aa_ref, c * UNITS) if c < 4 else (ab_ref, (c - 4) * UNITS)
            part = mm(a_ref[:, lo : lo + UNITS], held_ref[c * UNITS : (c + 1) * UNITS, :], NN)
            feed = part if feed is None else feed + part
        rest(feed)

    @pl.when(step > 0)
    def _():
        rest(mm(aa_ref[...], held_ref[:half, :], NN) + mm(ab_ref[...], held_ref[half:, :], NN))


def down(aa, ab, wa, wb, res, gf, shifts):
    n, d = res.shape
    rows = pl.BlockSpec((TILE, d), lambda i: (i, 0))
    units = pl.BlockSpec((TILE, 4 * UNITS), lambda i: (i, 0))
    return call(
        down_kernel, (n // TILE,),
        [(aa, units), (ab, units), (res, rows), (gf, rows), (shifts, whole(shifts.shape)), (wa, ANYWHERE), (wb, ANYWHERE)],
        [((n, d), BF16, rows), ((8, 128), F32, whole((8, 128)))],
        [pltpu.VMEM((8 * UNITS, d), BF16), pltpu.SemaphoreType.DMA((8,))], gflop=9.0, name="down", limit=50,
    )


def slope_kernel(gf_ref, h_ref, sb_ref, sa_ref, wb_ref, wa_ref, gb_ref, ga_ref, nb_ref, na_ref, tb_ref, ta_ref):
    for half, (s_ref, w_ref, g_ref, n_ref, t_ref) in enumerate(((sb_ref, wb_ref, gb_ref, nb_ref, tb_ref), (sa_ref, wa_ref, ga_ref, na_ref, ta_ref))):

        @pl.when((pl.program_id(0) >= 4) == (half == 1))
        def _():
            g = (mm(gf_ref[...], w_ref[...], NT) * s_ref[...].astype(F32)).astype(BF16)
            g_ref[...] = g
            n_ref[0] = mm(g, h_ref[...], TN).astype(BF16)
            t_ref[...] = jnp.sum(g.astype(F32), axis=0, keepdims=True)


def slope(gf, h, sb, sa, wb, wa):
    n, d = gf.shape
    low, high = (lambda t: jnp.minimum(t, 3)), (lambda t: jnp.maximum(t - 4, 0))
    units = lambda at: pl.BlockSpec((n, UNITS), lambda t: (0, at(t)))
    rows = lambda at: pl.BlockSpec((UNITS, d), lambda t: (at(t), 0))
    outs = [(sa.shape, BF16, units(at)) for at in (low, high)]
    outs += [((4, UNITS, d), BF16, pl.BlockSpec((1, UNITS, d), lambda t, at=at: (at(t), 0, 0))) for at in (low, high)]
    outs += [((1, 4 * UNITS), F32, pl.BlockSpec((1, UNITS), lambda t, at=at: (0, at(t)))) for at in (low, high)]
    return call(
        slope_kernel, (8,),
        [(gf, whole(gf.shape)), (h, whole(h.shape)), (sb, units(low)), (sa, units(high)), (wb, rows(low)), (wa, rows(high))], outs,
        gflop=9.0, name="slope", limit=50, far=(0, 1, 2, 3),
    )


def back_kernel(place_ref, ga_ref, gb_ref, gf_ref, res_ref, gain_ref, w_ref, *refs):
    gr_ref, br_ref, oa_ref, ob_ref, vec_ref, held_ref, out_ref, sem, out_sem = refs[8:]
    half = 4 * UNITS
    copies = [c for i in range(2) for c in gathered_copies(place_ref, w_ref, held_ref, sem, i, i * half)]
    outs = out_copies(refs[:8], out_ref, out_sem)
    step = pl.program_id(0)

    def rest(gy, first):
        c = gf_ref[...].astype(F32)
        gv, terms = norm_back(res_ref[...], gy, gain_ref[1:2, :])
        gr = c + gv
        gr_ref[...] = gr
        branch = gr.astype(BF16)
        br_ref[...] = branch
        if first:
            end(outs[0])
        go = mm(branch, out_ref[...].reshape(8 * PAIR, -1), NT).astype(BF16)
        oa_ref[...] = go[:, : 4 * PAIR]
        ob_ref[...] = go[:, 4 * PAIR :]
        sums = column_sums(terms, gy, branch.astype(F32), c)
        vec_ref[...] = sums if first else vec_ref[...] + sums

    @pl.when(step == 0)
    def _():
        begin(copies)
        begin(outs)
        gy = None
        for c in range(8):
            end(copies[c])
            g_ref, lo = (ga_ref, c * UNITS) if c < 4 else (gb_ref, (c - 4) * UNITS)
            part = mm(g_ref[:, lo : lo + UNITS], held_ref[c * UNITS : (c + 1) * UNITS, :], NN)
            gy = part if gy is None else gy + part
        rest(gy, True)

    @pl.when(step > 0)
    def _():
        rest(mm(ga_ref[...], held_ref[:half, :], NN) + mm(gb_ref[...], held_ref[half:, :], NN), False)


def back(place, ga, gb, gf, w, ws, res, gains):
    n, d = res.shape
    rows = pl.BlockSpec((TILE, d), lambda i: (i, 0))
    units = pl.BlockSpec((TILE, 4 * UNITS), lambda i: (i, 0))
    heads = pl.BlockSpec((TILE, 4 * PAIR), lambda i: (i, 0))
    return call(
        back_kernel, (n // TILE,),
        [(place, SCALARS), (ga, units), (gb, units), (gf, rows), (res, rows), (gains, whole(gains.shape)), (w, FAR)] + [(w, FAR) for w in ws],
        [((n, d), F32, rows), ((n, d), BF16, rows), ((n, 4 * PAIR), BF16, heads), ((n, 4 * PAIR), BF16, heads), ((8, d), F32, whole((8, d)))],
        [pltpu.VMEM((8 * UNITS, d), BF16), pltpu.VMEM((8, 4, PART, d), BF16), pltpu.SemaphoreType.DMA((32,)), pltpu.SemaphoreType.DMA((8,))],
        gflop=12.0, name="back", limit=50, far=(0,),
    )


def attend_back_kernel(row_ref, go_ref, qkv_ref, o_ref, lse_ref, g_ref, bias_ref, p_ref, d_ref):
    n = go_ref.shape[0]

    @pl.when(pl.program_id(0) == 0)
    def _():
        fill_mask(bias_ref, row_ref, True)

    q_at, k_at, v_at = slice(0, PAIR), slice(PAIR, 2 * PAIR), slice(2 * PAIR, 3 * PAIR)
    k_turned = jnp.transpose(qkv_ref[:, k_at])
    work = [(i, h) for i in range(n // TILE) for h in range(2)]
    qs, gs, deltas, halves = {}, {}, {}, {}

    def products(i, h):
        part, upto = slice(i * TILE, (i + 1) * TILE), (i + 1) * TILE
        if h == 0:
            go = go_ref[part, :]
            qs[i], gs[i] = split_heads(qkv_ref[part, q_at]), split_heads(go)
            both = jnp.transpose(go.astype(F32) * o_ref[part, :].astype(F32))
            deltas[i] = [jnp.sum(both[k * HD : (k + 1) * HD], axis=0, keepdims=True) for k in range(2)]
        return mm(qkv_ref[:upto, k_at], qs[i][h], NT), mm(qkv_ref[:upto, v_at], gs[i][h], NT)

    def query_grad(i, h, ds):
        part, upto = slice(i * TILE, (i + 1) * TILE), (i + 1) * TILE
        halves[h] = mm(k_turned[h * HD : (h + 1) * HD, :upto], ds, NN)
        if h:
            gq = jnp.transpose(jnp.concatenate([halves[0], halves[1]], axis=0))
            g_ref[part, q_at] = (gq.astype(BF16).astype(F32) * HD**-0.5).astype(BF16)

    now, held = products(*work[0]), None
    for t, (i, h) in enumerate(work):
        part, upto = slice(i * TILE, (i + 1) * TILE), (i + 1) * TILE
        ahead = products(*work[t + 1]) if t + 1 < len(work) else None
        p = jnp.exp2((now[0] + bias_ref[:upto, part] - lse_ref[0, h : h + 1, part]) * LOG2E)
        ds = (p * (now[1] - deltas[i][h])).astype(BF16)
        p_ref[h, :upto, part] = p.astype(BF16)
        d_ref[h, :upto, part] = ds
        if held is not None:
            query_grad(*work[t - 1], held)
        now, held = ahead, ds
    query_grad(*work[-1], held)
    qa, qb = split_heads(qkv_ref[:, q_at])
    ga, gb = split_heads(go_ref[...])
    for i in range(n // TILE):
        part, lo = slice(i * TILE, (i + 1) * TILE), i * TILE
        g_ref[part, k_at] = (mm(d_ref[0, part, lo:], qa[lo:], NN) + mm(d_ref[1, part, lo:], qb[lo:], NN)).astype(BF16)
        g_ref[part, v_at] = (mm(p_ref[0, part, lo:], ga[lo:], NN) + mm(p_ref[1, part, lo:], gb[lo:], NN)).astype(BF16)


def attend_back(row, go, stacks, base, pairs):
    qkv, o, lse = stacks[:3]
    n = go.shape[0]
    pair = pl.BlockSpec((n, PAIR), lambda p: (0, p + base))
    return call(
        attend_back_kernel, (pairs,),
        [(row, whole(row.shape)), (go, pair), (qkv, pl.BlockSpec((n, 3 * PAIR), lambda p: (0, p + base))), (o, pair),
         (lse, pl.BlockSpec((1, 2, n), lambda p: (p + base, 0, 0)))],
        [((n, 3 * PAIR * pairs), BF16, pl.BlockSpec((n, 3 * PAIR), lambda p: (0, p)))],
        [pltpu.VMEM((n, n), F32), pltpu.VMEM((2, n, n), BF16), pltpu.VMEM((2, n, n), BF16)],
        gflop=5.0 * pairs, name="attend_back", limit=32,
    )[0]


def outer_attn_kernel(gb_ref, ga_ref, ob_ref, oa_ref, h_ref, branch_ref, ub_ref, ua_ref, nb_ref, na_ref, *, pairs):
    d = h_ref.shape[1]
    for half, (g_ref, o_ref, up_ref, n_ref) in enumerate(((gb_ref, ob_ref, ub_ref, nb_ref), (ga_ref, oa_ref, ua_ref, na_ref))):

        @pl.when((pl.program_id(0) >= pairs) == (half == 1))
        def _():
            out = mm(o_ref[...], branch_ref[...], TN).astype(BF16)
            qkv = mm(g_ref[...], h_ref[...], TN).astype(BF16)
            sums = jnp.sum(g_ref[...].astype(F32), axis=0, keepdims=True)
            qsum, vsum = sums[:, :PAIR], sums[:, 2 * PAIR :]
            for j in range(4):
                turn = lambda a: jnp.concatenate([a[:, j * PART :], a[:, : j * PART]], axis=1) if j else a
                line = jnp.concatenate([up_ref[j, 0, 0:1, :], turn(qsum), turn(vsum), jnp.zeros((1, d - 3 * PAIR), F32)], axis=1)
                line = jnp.concatenate([line, jnp.zeros((15, d), F32)], axis=0).astype(BF16)
                rows = [out[j * PART : (j + 1) * PART]] + [qkv[i * PAIR + j * PART : i * PAIR + (j + 1) * PART] for i in range(3)]
                n_ref[j] = jnp.concatenate(rows + [line], axis=0)


def outer_attn(gb, ga, ob, oa, base, h, branch, ub, ua):
    n, m = ga.shape
    d = h.shape[1]
    pairs = m // (3 * PAIR)
    low, high = (lambda p: jnp.minimum(p, pairs - 1)), (lambda p: jnp.maximum(p - pairs, 0))
    grad = lambda at: pl.BlockSpec((n, 3 * PAIR), lambda p: (0, at(p)))
    head = lambda at: pl.BlockSpec((n, PAIR), lambda p: (0, at(p) + base))
    out = lambda at: ((4, pairs * ATTN, d), BF16, pl.BlockSpec((4, ATTN, d), lambda p: (0, at(p), 0)))
    return call(
        functools.partial(outer_attn_kernel, pairs=pairs), (2 * pairs,),
        [(gb, grad(low)), (ga, grad(high)), (ob, head(low)), (oa, head(high)), (h, whole(h.shape)), (branch, whole(branch.shape)),
         (ub, pl.BlockSpec((4, 1, 8, PAIR), lambda p: (0, low(p), 0, 0))), (ua, pl.BlockSpec((4, 1, 8, PAIR), lambda p: (0, high(p), 0, 0)))],
        [out(low), out(high)], gflop=2.5 * pairs, name="outer_attn", limit=30, far=(0, 1),
    )


def combine_kernel(a_ref, b_ref, *outs):
    for j in range(4):
        outs[j][...] = (a_ref[j].astype(F32) + b_ref[j].astype(F32)).astype(BF16)


def combine(a, b):
    _, m, d = a.shape
    rows = 128 if m % 128 == 0 else 96
    block = pl.BlockSpec((4, rows, d), lambda i: (0, i, 0))
    return call(combine_kernel, (m // rows,), [(a, block), (b, block)], [((m, d), BF16, pl.BlockSpec((rows, d), lambda i: (i, 0)))] * 4, gflop=0.1, name="combine", limit=56)


def finish_kernel(*refs, plan):
    grads, w_refs = refs[: len(plan)], refs[len(plan) : len(plan) + 8]
    x_ref, gr_ref, gain_ref, out_ref, vec_ref, held_ref, sem = refs[len(plan) + 8 :]
    step = pl.program_id(0)
    copies, spans, lo = [], [], 0
    for half, base, count in plan:
        spans.append(slice(3 * lo, 3 * (lo + count)))
        mine = []
        for z in range(base, base + count):
            for i in range(3):
                at = 3 * lo + i
                mine.append(pltpu.make_async_copy(w_refs[4 * half + z].at[:, pl.ds((1 + i) * PART, PART)], held_ref.at[at], sem.at[at]))
            lo += 1
        copies.append(mine)

    def tile(first):
        gy = None
        for g_ref, span, mine in zip(grads, spans, copies):
            if first:
                end(mine)
            part = mm(g_ref[...], held_ref[span].reshape(g_ref.shape[1], -1), NN)
            gy = part if gy is None else gy + part
        gv, terms = norm_back(x_ref[...].astype(F32), gy, gain_ref[0:1, :])
        out_ref[...] = gr_ref[...] + gv
        sums = column_sums(terms, gy)
        vec_ref[...] = sums if first else vec_ref[...] + sums

    @pl.when(step == 0)
    def _():
        begin(copies)
        tile(True)

    @pl.when(step > 0)
    def _():
        tile(False)


def finish(grads, ws, x, gr, gains):
    n, d = x.shape
    rows = pl.BlockSpec((TILE, d), lambda i: (i, 0))
    plan = tuple((half, base, g.shape[1] // (3 * PAIR)) for g, half, base in grads)
    return call(
        functools.partial(finish_kernel, plan=plan), (n // TILE,),
        [(g, pl.BlockSpec((TILE, g.shape[1]), lambda i: (i, 0))) for g, _, _ in grads]
        + [(w, FAR) for w in ws] + [(x, rows), (gr, rows), (gains, whole(gains.shape))],
        [((n, d), F32, rows), ((8, d), F32, whole((8, d)))],
        [pltpu.VMEM((24, 4, PART, d), BF16), pltpu.SemaphoreType.DMA((24,))], gflop=10.0, name="finish", limit=56,
    )


def pack_kernel(r_ref, *refs, plan, bands):
    srcs, (out_ref, held_ref, in_sem, out_sem) = refs[:-4], refs[-4:]
    copies = []
    for at, (src, quarter, count, dst) in enumerate(plan):
        source = srcs[src] if quarter is None else srcs[src].at[r_ref[0] ^ quarter]
        copies.append(pltpu.make_async_copy(source, held_ref.at[pl.ds(dst, count)], in_sem.at[at]))
    begin((copies,))
    band = held_ref.shape[0] // bands
    outs = []
    for b in range(bands):
        end([copy for copy, (_, _, _, dst) in zip(copies, plan) if dst // band == b])
        outs.append(pltpu.make_async_copy(held_ref.at[pl.ds(b * band, band)], out_ref.at[pl.ds(b * band, band)], out_sem.at[b]))
        begin((outs[-1:],))
    end(outs)


def pack(r, arrays, plan, bands):
    rows = sum(count for _, _, count, _ in plan)
    d = arrays[0].shape[-1]
    return call(
        functools.partial(pack_kernel, plan=plan, bands=bands), (), [(r, SCALARS)] + [(a, ANYWHERE) for a in arrays], [((rows, d), BF16, ANYWHERE)],
        [pltpu.VMEM((rows, d), BF16), pltpu.SemaphoreType.DMA((len(plan),)), pltpu.SemaphoreType.DMA((bands,))], gflop=0.0, name="pack", limit=14,
    )[0]


def stack_z(r, parts):
    n = parts[0].shape[0]
    return pack(r, parts, [(i, None, n, i * n) for i in range(3)], 3)


def stack_units(r, quarters, sides):
    n = quarters.shape[1]
    plan = [(0, j, n, 4 * n * j) for j in range(4)] + [(1 + j, None, 3 * n, 4 * n * j + n) for j in range(4)]
    return pack(r, [quarters, *sides], plan, 4)


def settle_kernel(r_ref, *refs):
    qkv_ref, bias_ref, out_ref, held_ref = refs[4:]
    for j in range(4):
        held_ref[j] = refs[j][...]
    quarters = [held_ref[r_ref[0] ^ q].astype(F32) for q in range(4)]
    for i in range(3):
        qkv_ref[i] = jnp.transpose(jnp.concatenate([a[(1 + i) * PART : (2 + i) * PART] for a in quarters], axis=0))
    bias_ref[...] = jnp.concatenate([a[4 * PART : 4 * PART + 1, : 3 * PAIR] for a in quarters] + [jnp.zeros((4, 3 * PAIR), F32)], axis=0)
    out_ref[...] = jnp.concatenate([a[:PART] for a in quarters], axis=0)


def settle(r, pieces):
    d = pieces[0].shape[1]
    shapes = [(3, d, PAIR), (8, 3 * PAIR), (PAIR, d)]
    return call(
        settle_kernel, (), [(r, SCALARS)] + [(a, whole(a.shape)) for a in pieces], [(shape, F32, whole(shape)) for shape in shapes],
        [pltpu.VMEM((4, ATTN, d), BF16)], gflop=0.1, name="settle", limit=24,
    )


def settle_units_kernel(g_ref, down_ref, up_ref):
    down_ref[...] = g_ref[0, 0].astype(F32)
    up_ref[...] = jnp.transpose(g_ref[0, 1].astype(F32))


def settle_units(g):
    d = g.shape[-1]
    return call(
        settle_units_kernel, (4,), [(g, pl.BlockSpec((1, 2, PAIR, d), lambda q: (q, 0, 0, 0)))],
        [((4 * PAIR, d), F32, pl.BlockSpec((PAIR, d), lambda q: (q, 0))), ((d, 4 * PAIR), F32, pl.BlockSpec((d, PAIR), lambda q: (0, q)))],
        gflop=0.1, name="settle_units", limit=24,
    )


def moved(array, axis, mask):
    size = lax.axis_size(axis)
    return lax.ppermute(array, axis, [(i, i ^ mask) for i in range(size)])


def across(array):
    return moved(array, "mp", 1)


def beside(array, j):
    return moved(array, "rows", j)


def along_z(array, z):
    return moved(array, "mp", 2 * z)


def fence(*trees):
    return lax.optimization_barrier(trees)


def by_z(a):
    z = lax.axis_index("mp") // 2
    low = [jnp.where(z & 1, a[i ^ 1], a[i]) for i in range(4)]
    return [jnp.where(z & 2, low[i ^ 2], low[i]) for i in range(4)]


def added(*terms):
    total = terms[0].astype(F32)
    for term in terms[1:]:
        total = total + term.astype(F32)
    return total.astype(BF16)


def any_spread(parts):
    core = lax.axis_index("mp") % 2
    return [lax.dynamic_index_in_dim(parts, c, 0, False) for c in (core, 1 - core)]


def any_reduced(full, axis):
    return lax.psum(lax.psum_scatter(full, "mp", scatter_dimension=axis, tiled=True), "rows")


def up_sums(total, first, last):
    return jnp.pad(total.reshape(4, 4, 1, PAIR)[:, first:last], ((0, 0), (0, 0), (0, 7), (0, 0)))


def stacked_vectors(one, two, loss):
    d = one.shape[1]
    at = lax.axis_index("rows") * lax.axis_size("mp") + lax.axis_index("mp")
    losses = jnp.where(jnp.arange(d, dtype=jnp.int32) == at, loss[0, 0] / math.sqrt(SLOTS * d), 0.0)
    return jnp.stack([one[0], two[0], one[1], two[2], two[1], two[3], losses, jnp.zeros_like(losses)])


def any_mesh(tokens, qkv_rows, qv_bias, out_weight, up_rows, up_bias, down_weight, gains, shifts, live, line, cotangent):
    d = tokens.shape[1]
    r = jnp.zeros((1,), jnp.int32)
    every = lambda a, axis=0: lax.all_gather(a, "mp", axis=axis, tiled=True)
    heads = lambda a: a.reshape(2, 4, 4, PART, d)
    qkv_all, qvb_all = every(qkv_rows, 1), every(qv_bias, 1)
    small = lambda a: jnp.tile(a.reshape(2, 4, 4, PART), (1, 1, 1, 4))
    ups = every(up_bias).reshape(2, 4, 4, PAIR).swapaxes(1, 2)
    bias = jnp.concatenate([ups, small(qvb_all[0]), small(qvb_all[1])], axis=3)
    bias = jnp.pad(bias[:, :, :, None, :], ((0, 0), (0, 0), (0, 0), (0, 15), (0, d - 3 * PAIR)))
    wa, wb = any_spread(jnp.concatenate([heads(every(out_weight)), heads(qkv_all[0]), heads(qkv_all[1]), heads(qkv_all[2]), bias], axis=3))

    place = jnp.zeros((3,), jnp.int32)
    da, db = any_spread(every(down_weight).reshape(2, 16 * PAIR, d))
    by_half = jnp.stack(any_spread(every(up_rows).reshape(2, 4, 4, PAIR, d)))
    up_all = jnp.moveaxis(by_half, 0, 2).reshape(32, PAIR, d)
    h1, gf = prep(tokens, cotangent, live, gains, shifts)
    stacks, ws = [], [w[z] for w in (wa, wb) for z in range(4)]
    for w in (wa, wb):
        stacks.append(attend(r, line, h1, [w[0], w[1], w[2], w[3]], "packed", 0)[0])
    stack_a, stack_b = stacks
    res, h2 = join(tokens, stack_a[1], stack_b[1], ws, gains, shifts)
    aa, sa, down_a = up(place, h2, gf, up_all, stack_a[3], 0)
    ab, sb, down_b = up(place, h2, gf, up_all, stack_b[3], 1)
    g_down = added(down_a, across(down_b))
    mixed, loss = down(aa, ab, da, db, res, gf, shifts)
    gb, ga, up_b, up_a, total_b, total_a = slope(gf, h2, sb, sa, db, da)
    g_up = added(up_a, across(up_b))
    gr, branch, go_a, go_b, two = back(place, ga, gb, gf, up_all, ws, res, gains)
    back_b = attend_back(line, go_b, stack_b, 0, 4)
    back_a = attend_back(line, go_a, stack_a, 0, 4)
    nb, na = outer_attn(back_b, back_a, stack_b[1], stack_a[1], 0, h1, branch, up_sums(total_b, 0, 4), up_sums(total_a, 0, 4))
    g_attn = added(na, across(nb)).reshape(4, 4, ATTN, d)
    input_grad, one = finish([(back_a, 0, 0), (back_b, 1, 0)], ws, tokens, gr, gains)
    vectors = lax.psum(stacked_vectors(one, two, loss), ("rows", "mp"))
    core = lax.axis_index("mp") % 2
    full = lambda g: lax.dynamic_update_index_in_dim(jnp.zeros((2,) + g.shape, F32), g.astype(F32), core, 0)
    ordered = lambda g: full(g).swapaxes(1, 2).reshape(-1, g.shape[-1])
    down_grad, up_grad = [any_reduced(full(g).reshape(-1, d), 0) for g in (g_down, g_up)]
    out_grad = any_reduced(ordered(g_attn[:, :, :PART]), 0)
    qkv_grad = any_reduced(jnp.stack([ordered(g_attn[:, :, i * PART : (i + 1) * PART]) for i in (1, 2, 3)]), 1)
    lines = g_attn[:, :, 4 * PART]
    up_bias_grad = any_reduced(full(lines[:, :, :PAIR]).reshape(-1), 0)
    ordered = lambda g: full(g).swapaxes(1, 2).reshape(-1)
    qv_bias_grad = any_reduced(jnp.stack([ordered(lines[:, :, at : at + PART]) for at in (PAIR, 2 * PAIR)]), 1)
    qkv_grad, up_grad = jnp.swapaxes(qkv_grad, 1, 2), up_grad.T
    return mixed, input_grad, qkv_grad, qv_bias_grad, out_grad, up_grad, up_bias_grad, down_grad, vectors


def small_mesh(tokens, qkv_rows, qv_bias, out_weight, up_rows, up_bias, down_weight, gains, shifts, live, line, cotangent):
    d = tokens.shape[1]
    row = lax.axis_index("rows")
    r = row.reshape(1).astype(jnp.int32)
    mine = lambda a: lax.dynamic_index_in_dim(a, row, 0, False)
    sides = lambda a: [beside(a, j) for j in (1, 2, 3)]
    sides3 = lambda g: [beside(g[j], j) for j in (1, 2, 3)]

    bias = jnp.concatenate(
        [up_bias.reshape(4, PAIR), jnp.tile(qv_bias[0].reshape(4, PART), (1, 4)), jnp.tile(qv_bias[1].reshape(4, PART), (1, 4))], axis=1
    )
    bias = jnp.pad(bias[:, None, :], ((0, 0), (0, 15), (0, d - 3 * PAIR)))
    qkv4 = qkv_rows.reshape(3, 4, PART, d).swapaxes(0, 1).reshape(4, 3 * PART, d)
    a4 = jnp.concatenate([out_weight.reshape(4, PART, d), qkv4, bias], axis=1)
    pa = mine(a4)
    c4 = down_weight.reshape(4, PAIR, d)
    pc = mine(c4)
    index = lax.axis_index("mp").astype(jnp.int32)
    place = jnp.stack([row.astype(jnp.int32), index // 2, index % 2])
    up_all = lax.all_gather(mine(up_rows.reshape(4, PAIR, d)), ("rows", "mp"))
    p1, c2 = along_z(pa, 1), along_z(pc, 2)
    h1, gf = prep(tokens, cotangent, live, gains, shifts)
    p1, c2, h1, gf, pa, pc = fence(p1, c2, h1, gf, pa, pc)
    s1, p2 = sides(p1), along_z(pa, 2)
    sa, w0 = attend(r, line, h1, [a4], "quarters", 0)
    s1, p2, sa, w0, h1, pa = fence(s1, p2, sa, w0, h1, pa)
    s2, p3, x0 = sides(p2), along_z(pa, 3), across(w0)
    sa, w1 = attend(r, line, h1, [p1, *s1], "pieces", 1, sa)
    s2, p3, x0, sa, w1, h1, pc = fence(s2, p3, x0, sa, w1, h1, pc)
    s3, c1 = sides(p3), along_z(pc, 1)
    sa, w2 = attend(r, line, h1, [p2, *s2], "pieces", 2, sa)
    sb, _ = attend(r, line, h1, [x0], "packed", 0)
    s3, c1, sa, w1, w2, sb, h1, pc = fence(s3, c1, sa, w1, w2, sb, h1, pc)
    c3, x1, x2 = along_z(pc, 3), across(w1), across(w2)
    sb, _ = attend(r, line, h1, [x1, x2], "packed", 1, sb)
    sa, w3 = attend(r, line, h1, [p3, *s3], "pieces", 3, sa)
    c3, sa, sb, w3, h1 = fence(c3, sa, sb, w3, h1)
    cs = stack_z(r, [c1, c2, c3])
    cx, x3 = sides(cs), across(w3)
    ws = [w0, w1, w2, w3, x0, x1, x2, x3]
    sb, _ = attend(r, line, h1, [x3], "packed", 3, sb)
    res, h2 = join(tokens, sa[1], sb[1], ws, gains, shifts)
    ab, lb, down_b = up(place, h2, gf, up_all, sb[3], 1)
    cx, ab, lb, down_b, h2 = fence(cx, ab, lb, down_b, h2)
    da = stack_units(r, c4, [cs, *cx])
    db, down_x = across(da), across(down_b)
    aa, la, down_a = up(place, h2, gf, up_all, sa[3], 0)
    da, db, down_x, aa, la, down_a, h2 = fence(da, db, down_x, aa, la, down_a, h2)
    g_down = combine(down_a, down_x)
    fx = [beside(g_down[j], j) for j in (1, 2)]
    gb, ga, up_b, up_a, total_b, total_a = slope(gf, h2, lb, la, db, da)
    fx, gb, ga, up_b, up_a, g3 = fence(fx, gb, ga, up_b, up_a, g_down[3])
    fx, up_x = [*fx, beside(g3, 3)], across(up_b)
    gr, branch, go_a, go_b, two = back(place, ga, gb, gf, up_all, ws, res, gains)
    back_b1 = attend_back(line, go_b, sb, 2, 2)
    fx, up_x, gr, branch, go_a, go_b, back_b1 = fence(fx, up_x, gr, branch, go_a, go_b, back_b1)
    td = added(g_down[0], *fx).reshape(4, PAIR, d)
    td, up_a, up_x = fence(jnp.stack(by_z(td)), up_a, up_x)
    columns = [[2 * i + core for i in range(4)] for core in range(2)]
    reduce_z = lambda t: lax.psum_scatter(t, "mp", scatter_dimension=0, tiled=False, axis_index_groups=columns)
    f_down = reduce_z(td)
    g_up = combine(up_a, up_x)
    fx = [beside(g_up[j], j) for j in (1, 2)]
    back_a1 = attend_back(line, go_a, sa, 2, 2)
    nb1, na1 = outer_attn(back_b1, back_a1, sb[1], sa[1], 2, h1, branch, up_sums(total_b, 2, 4), up_sums(total_a, 2, 4))
    back_b2 = attend_back(line, go_b, sb, 0, 2)
    fx, back_a1, back_b2, nb1, na1, go_a, g3, f_down = fence(fx, back_a1, back_b2, nb1, na1, go_a, g_up[3], f_down)
    fx, n1_x = [*fx, beside(g3, 3)], across(nb1)
    back_a2 = attend_back(line, go_a, sa, 0, 2)
    nb2, na2 = outer_attn(back_b2, back_a2, sb[1], sa[1], 0, h1, branch, up_sums(total_b, 0, 2), up_sums(total_a, 0, 2))
    fx, n1_x, back_a2, nb2, na2, gr = fence(fx, n1_x, back_a2, nb2, na2, gr)
    f_up = reduce_z(jnp.stack(by_z(added(g_up[0], *fx).reshape(4, PAIR, d))))
    n1 = combine(na1, n1_x)
    ex, n2_x = sides3(n1), across(nb2)
    input_grad, one = finish([(back_a2, 0, 0), (back_a1, 0, 2), (back_b2, 1, 0), (back_b1, 1, 2)], ws, tokens, gr, gains)
    ex, n2_x, input_grad, one, na2, aa, f_up = fence(ex, n2_x, input_grad, one, na2, aa, f_up)
    units = lax.all_gather(jnp.stack([f_down, f_up]), "rows")
    n2 = combine(na2, n2_x)
    t1 = added(n1[0], *ex).reshape(2, ATTN, d)
    ex, y2, y3 = sides3(n2), along_z(t1[0], 2), along_z(t1[1], 3)
    mixed, loss = down(aa, ab, da, db, res, gf, shifts)
    vectors = stacked_vectors(one, two, loss)
    ex, y2, y3, mixed, vectors = fence(ex, y2, y3, mixed, vectors)
    t2 = added(n2[0], *ex).reshape(2, ATTN, d)
    y1, vx = along_z(t2[1], 1), sides(vectors)
    vx, y1, vectors, t2 = fence(vx, y1, vectors, t2)
    f = added(t2[0], y1, y2, y3)
    d_last = sides(f)
    vectors = (vectors + vx[0]) + (vx[1] + vx[2])
    vectors = vectors + across(vectors)
    vz = [along_z(vectors, i) for i in (1, 2, 3)]
    vectors = (vectors + vz[0]) + (vz[1] + vz[2])
    down_grad, up_grad = settle_units(units)
    d_last, down_grad, up_grad, vectors = fence(d_last, down_grad, up_grad, vectors)
    qkv_grad, biases, out_grad = settle(r, [f, *d_last])
    up_bias_grad = biases[:4, :PAIR].reshape(-1)
    qv_bias_grad = jnp.stack([biases[:4, at : at + PART].reshape(-1) for at in (PAIR, 2 * PAIR)])
    return mixed, input_grad, qkv_grad, qv_bias_grad, out_grad, up_grad, up_bias_grad, down_grad, vectors


def body(tokens, qkv_weight, qv_bias, out_weight, up_weight, up_bias, down_weight, norm_gains, shift_vectors, lengths, cotangent):
    n, d = tokens.shape
    place, row = lax.axis_index("mp"), lax.axis_index("rows")
    endings = jnp.cumsum(lax.dynamic_slice_in_dim(lengths, place, 1, 0)[0])
    position = jnp.arange(SLOTS, dtype=jnp.int32)
    segment = jnp.sum((position[:, None] >= endings[None, :]).astype(jnp.int32), axis=1)
    live = (segment < DOCS).astype(F32)[:, None]
    ident = jnp.where(segment < DOCS, segment, DOCS + position).astype(jnp.int32)
    layer = small_mesh if (lax.axis_size("rows"), lax.axis_size("mp")) == (4, 8) else any_mesh
    mixed, input_grad, qkv_grad, qv_bias_grad, out_grad, up_grad, up_bias_grad, down_grad, vectors = layer(
        tokens, jnp.swapaxes(qkv_weight, 1, 2), qv_bias, out_weight, up_weight.T, up_bias, down_weight,
        norm_gains.astype(F32), shift_vectors.astype(F32), live, ident.reshape(1, n), cotangent,
    )
    share = d // lax.axis_size("mp")
    vector_grad = lax.dynamic_slice_in_dim(vectors[:6], place * share, share, 1)
    block_loss = lax.dynamic_slice_in_dim(vectors[6], row * lax.axis_size("mp"), lax.axis_size("mp"), 0)
    return (
        mixed, block_loss, input_grad, qkv_grad, qv_bias_grad, out_grad,
        up_grad, up_bias_grad, down_grad, vector_grad,
    )


def solution(mesh):
    placed = (
        P(("rows", "mp"), None),
        P(None, None, "mp"),
        P(None, "mp"),
        P("mp", None),
        P(None, "mp"),
        P("mp"),
        P("mp", None),
        P(),
        P(),
        P("rows", None),
        P(("rows", "mp"), None),
    )
    return jax.shard_map(
        body,
        mesh=mesh,
        in_specs=placed,
        out_specs=(
            P(("rows", "mp"), None),
            P("rows"),
            P(("rows", "mp"), None),
            P(None, None, "mp"),
            P(None, "mp"),
            P("mp", None),
            P(None, "mp"),
            P("mp"),
            P("mp", None),
            P(None, "mp"),
        ),
        check_vma=False,
    )
```

```python
import functools
import math

import jax
import jax.numpy as jnp
from jax import lax
from jax.experimental import pallas as pl
from jax.experimental.pallas import tpu as pltpu
from jax.sharding import PartitionSpec as P

HD = 64
PAIR = 128
PART = 32
ATTN = 144
TILE = 256
UNITS = 512
SCALE = 0.4e9
SLOTS = 1024
DOCS = 6
EPSILON = 1e-05
MASKED = -1e30
LOG2E = math.log2(math.e)
F32, BF16 = jnp.float32, jnp.bfloat16
NN = (((1,), (0,)), ((), ()))
NT = (((1,), (1,)), ((), ()))
TN = (((0,), (0,)), ((), ()))


def mm(a, b, dims):
    return lax.dot_general(a, b, dims, preferred_element_type=F32)


def whole(shape):
    return pl.BlockSpec(shape, lambda *_: (0,) * len(shape), pipeline_mode=pl.Buffered(1))


ANYWHERE = pl.BlockSpec(memory_space=pl.ANY)
FAR = pl.BlockSpec(memory_space=pltpu.HBM)
SCALARS = pl.BlockSpec(memory_space=pltpu.SMEM)


def call(kernel, grid, ins, outs, scratch=(), gflop=1.0, name=None, limit=56, aliases=None, far=()):
    nbytes = sum(a.size * a.dtype.itemsize for a, _ in ins)
    nbytes += sum(math.prod(s) * jnp.dtype(d).itemsize for s, d, _ in outs)
    return pl.pallas_call(
        kernel,
        grid=grid,
        in_specs=[s for _, s in ins],
        out_specs=[s for _, _, s in outs],
        out_shape=[pltpu.HBM(s, d) if i in far else jax.ShapeDtypeStruct(s, d) for i, (s, d, _) in enumerate(outs)],
        scratch_shapes=list(scratch),
        input_output_aliases=aliases or {},
        compiler_params=pltpu.CompilerParams(vmem_limit_bytes=limit << 20),
        cost_estimate=pl.CostEstimate(flops=int(gflop * SCALE), bytes_accessed=nbytes, transcendentals=0),
        name=name,
    )(*[a for a, _ in ins])


def normed(v):
    spread = v - jnp.mean(v, axis=1, keepdims=True)
    rstd = lax.rsqrt(jnp.mean(spread * spread, axis=1, keepdims=True) + EPSILON)
    return spread * rstd, rstd


def norm_back(v, gy, gain):
    norm, rstd = normed(v)
    gn = gy * gain
    gv = rstd * (gn - jnp.mean(gn, axis=1, keepdims=True) - norm * jnp.mean(gn * norm, axis=1, keepdims=True))
    return gv, gy * norm


def column_sums(*values):
    d = values[0].shape[1]
    rows = [jnp.sum(v, axis=0, keepdims=True) for v in values]
    return jnp.concatenate(rows + [jnp.zeros((8 - len(rows), d), F32)], axis=0)


def prep_kernel(x_ref, cot_ref, live_ref, gain_ref, shift_ref, h_ref, gf_ref):
    norm, _ = normed(x_ref[...].astype(F32))
    h_ref[...] = (norm * gain_ref[0:1, :] + shift_ref[0:1, :]).astype(BF16)
    gf_ref[...] = (cot_ref[...].astype(F32) * live_ref[...]).astype(BF16)


def prep(x, cot, live, gains, shifts):
    n, d = x.shape
    rows = pl.BlockSpec((TILE, d), lambda i: (i, 0))
    return call(
        prep_kernel, (n // TILE,),
        [(x, rows), (cot, rows), (live, pl.BlockSpec((TILE, 1), lambda i: (i, 0))), (gains, whole(gains.shape)), (shifts, whole(shifts.shape))],
        [((n, d), BF16, rows), ((n, d), BF16, rows)], gflop=1.0, name="prep", limit=20,
    )


def fill_mask(bias_ref, row_ref, transposed):
    n = row_ref.shape[1]
    col = jnp.transpose(jnp.broadcast_to(row_ref[...], (8, n)))[:, :1]
    for i in range(n // TILE):
        part, upto = slice(i * TILE, (i + 1) * TILE), (i + 1) * TILE
        if transposed:
            same = col[:upto, :] == row_ref[:, part]
            key = lax.broadcasted_iota(jnp.int32, (upto, TILE), 0)
            query = lax.broadcasted_iota(jnp.int32, (upto, TILE), 1) + i * TILE
            bias_ref[:upto, part] = jnp.where(same & (key <= query), 0.0, MASKED)
        else:
            same = col[part, :] == row_ref[:, :upto]
            query = lax.broadcasted_iota(jnp.int32, (TILE, upto), 0) + i * TILE
            key = lax.broadcasted_iota(jnp.int32, (TILE, upto), 1)
            bias_ref[part, :upto] = jnp.where(same & (key <= query), 0.0, MASKED)


def pair_bias(pieces, at):
    lane = lax.broadcasted_iota(jnp.int32, (1, PAIR), 1) // PART
    row = jnp.zeros((1, PAIR), F32)
    for j in range(4):
        row = jnp.where(lane == j, pieces[j][4 * PART : ATTN, at : at + PAIR].astype(F32)[0:1, :], row)
    return row


def split_heads(a):
    first = lax.broadcasted_iota(jnp.int32, (1, PAIR), 1) < HD
    zero = jnp.zeros((), a.dtype)
    return jnp.where(first, a, zero), jnp.where(first, zero, a)


def attend_kernel(r_ref, row_ref, h_ref, *refs, mode, stacked, count):
    w_refs, refs = refs[:count], refs[count + (STACKS if stacked else 0) :]
    qkv_ref, o_ref, lse_ref, up_ref = refs[:STACKS]
    bias_ref, held_ref = refs[-2:]
    n = h_ref.shape[0]

    @pl.when(pl.program_id(0) == 0)
    def _():
        fill_mask(bias_ref, row_ref, False)

    if mode == "packed":
        for p in range(count):

            @pl.when(pl.program_id(0) == p)
            def _():
                held_ref[...] = w_refs[p][...]
    else:
        for j in range(4):
            piece = w_refs[0][r_ref[0] ^ j] if mode == "quarters" else w_refs[j][...]
            held_ref[j] = piece
            refs[STACKS][j] = piece
    pieces = [held_ref[j] for j in range(4)]
    up_ref[0] = jnp.concatenate([piece[4 * PART :, :PAIR].astype(F32)[0:1] for piece in pieces], axis=0)
    wall = jnp.concatenate([pieces[j][i * PART : (i + 1) * PART] for i in (1, 2, 3) for j in range(4)], axis=0)
    qkv = mm(h_ref[...], wall, NT)
    qkv_ref[:, :PAIR] = ((qkv[:, :PAIR] + pair_bias(pieces, 128)) * HD**-0.5).astype(BF16)
    qkv_ref[:, PAIR : 2 * PAIR] = qkv[:, PAIR : 2 * PAIR].astype(BF16)
    v = (qkv[:, 2 * PAIR :] + pair_bias(pieces, 256)).astype(BF16)
    qkv_ref[:, 2 * PAIR :] = v
    vx = jnp.concatenate([v, jnp.ones((n, PAIR), BF16)], axis=1)
    first = lax.broadcasted_iota(jnp.int32, (1, PAIR), 1) < HD
    work = [(i, h) for i in range(n // TILE) for h in range(2)]
    outs = {}

    def scores(i, h):
        q = split_heads(qkv_ref[i * TILE : (i + 1) * TILE, :PAIR])[h]
        return mm(q, qkv_ref[: (i + 1) * TILE, PAIR : 2 * PAIR], NT)

    def weigh(i, h, e, top):
        part = slice(i * TILE, (i + 1) * TILE)
        ov = mm(e, vx[: (i + 1) * TILE], NN)
        total = ov[:, PAIR:]
        outs[h] = ov[:, :PAIR] / total
        lse_ref[0, h : h + 1, part] = jnp.transpose(top + jnp.log(total))[0:1, :]
        if h:
            o_ref[part, :] = jnp.where(first, outs[0], outs[1]).astype(BF16)

    s, held = scores(*work[0]), None
    for t, (i, h) in enumerate(work):
        ahead = scores(*work[t + 1]) if t + 1 < len(work) else None
        s = s + bias_ref[i * TILE : (i + 1) * TILE, : (i + 1) * TILE]
        top = jnp.max(s, axis=1, keepdims=True)
        e = jnp.exp2((s - top) * LOG2E).astype(BF16)
        if held is not None:
            weigh(*work[t - 1], *held)
        s, held = ahead, (e, top)
    weigh(*work[-1], *held)


STACKS = 4


def attend(r, row, h, w, mode, z, stacks=None):
    n, d = h.shape
    pairs = len(w) if mode == "packed" else 1
    outs = [
        ((n, 12 * PAIR), BF16, pl.BlockSpec((n, 3 * PAIR), lambda p: (0, z + p))),
        ((n, 4 * PAIR), BF16, pl.BlockSpec((n, PAIR), lambda p: (0, z + p))),
        ((4, 2, n), F32, pl.BlockSpec((1, 2, n), lambda p: (z + p, 0, 0))),
        ((4, 4, PAIR), F32, pl.BlockSpec((1, 4, PAIR), lambda p: (z + p, 0, 0))),
    ]
    if mode != "packed":
        outs.append(((4, ATTN, d), BF16, whole((4, ATTN, d))))
    ins = [(r, SCALARS), (row, whole(row.shape)), (h, whole(h.shape))] + [(a, whole(a.shape)) for a in w]
    aliases = {len(ins) + i: i for i in range(STACKS)} if stacks else None
    ins += [(a, FAR) for a in stacks or ()]
    *stacks, last = *call(
        functools.partial(attend_kernel, mode=mode, stacked=bool(aliases), count=len(w)), (pairs,), ins, outs,
        [pltpu.VMEM((n, n), F32), pltpu.VMEM((4, ATTN, d), BF16)], gflop=5.0 * pairs, name="attend", limit=28, aliases=aliases, far=range(STACKS),
    ), *([None] if mode == "packed" else [])
    return stacks, last


def out_copies(refs, held_ref, sem):
    return [[pltpu.make_async_copy(ref.at[:, pl.ds(0, PART)], held_ref.at[i], sem.at[i]) for i, ref in enumerate(refs)]]


def join_kernel(x_ref, oa_ref, ob_ref, gain_ref, shift_ref, *refs):
    r_ref, h_ref, held_ref, sem = refs[8:]

    @pl.when(pl.program_id(0) == 0)
    def _():
        copies = out_copies(refs[:8], held_ref, sem)
        begin(copies)
        end(copies[0])

    half = lambda a: held_ref[a : a + 4].reshape(4 * PAIR, -1)
    branch = mm(oa_ref[...], half(0), NN) + mm(ob_ref[...], half(4), NN)
    r = x_ref[...].astype(F32) + (branch + shift_ref[1:2, :])
    r_ref[...] = r
    norm, _ = normed(r)
    h_ref[...] = (norm * gain_ref[1:2, :] + shift_ref[2:3, :]).astype(BF16)


def join(x, oa, ob, ws, gains, shifts):
    n, d = x.shape
    rows = pl.BlockSpec((TILE, d), lambda i: (i, 0))
    half = pl.BlockSpec((TILE, 4 * PAIR), lambda i: (i, 0))
    return call(
        join_kernel, (n // TILE,),
        [(x, rows), (oa, half), (ob, half), (gains, whole(gains.shape)), (shifts, whole(shifts.shape))] + [(w, FAR) for w in ws],
        [((n, d), F32, rows), ((n, d), BF16, rows)], [pltpu.VMEM((8, 4, PART, d), BF16), pltpu.SemaphoreType.DMA((8,))],
        gflop=4.0, name="join", limit=56, far=(0,),
    )


def unit_copies(w_ref, held_ref, sem, first):
    spans = [(j * UNITS, first + j * UNITS) for j in range(4)]
    return [[pltpu.make_async_copy(w_ref.at[pl.ds(a, UNITS)], held_ref.at[pl.ds(b, UNITS)], sem.at[b // UNITS])] for a, b in spans]


def gathered_copies(place_ref, w_ref, held_ref, sem, half, first):
    r, at, core = place_ref[0], place_ref[1], place_ref[2]
    copies = []
    for j in range(4):
        lo = first + j * UNITS
        source = lambda z: w_ref.at[((r ^ j) * 4 + (at ^ z)) * 2 + (core ^ half)]
        copies.append([pltpu.make_async_copy(source(z), held_ref.at[pl.ds(lo + z * PAIR, PAIR)], sem.at[lo // PAIR + z]) for z in range(4)])
    return copies


def begin(copies):
    for pair in copies:
        for copy in pair:
            copy.start()


def end(pair):
    for copy in pair:
        copy.wait()


def up_kernel(place_ref, h_ref, gf_ref, bias_ref, w_ref, act_ref, slope_ref, g_ref, held_ref, sem, *, half):
    copies = gathered_copies(place_ref, w_ref, held_ref, sem, half, 0)
    step = pl.program_id(0)

    @pl.when(step == 0)
    def _():
        begin(copies)

    for j in range(4):

        @pl.when(step == j)
        def _():
            end(copies[j])
            bias = jnp.concatenate([bias_ref[z, j : j + 1, :] for z in range(4)], axis=1)
            c0, c1 = math.sqrt(2 / math.pi), math.sqrt(2 / math.pi) * 0.044715
            u = mm(h_ref[...], held_ref[j * UNITS : (j + 1) * UNITS, :], NT) + bias
            square = u * u
            s = 0.5 + 0.5 * jnp.tanh(u * (c0 + c1 * square))
            us = u * s
            act = us.astype(BF16)
            act_ref[...] = act
            slope_ref[...] = (s + (us - us * s) * (2 * c0 + 6 * c1 * square)).astype(BF16)
            g_ref[0] = mm(act, gf_ref[...], TN).astype(BF16)


def up(place, h, gf, w, bias, half):
    n, d = h.shape
    blk = pl.BlockSpec((n, UNITS), lambda i: (0, i))
    shape = (n, 4 * UNITS)
    return call(
        functools.partial(up_kernel, half=half), (4,),
        [(place, SCALARS), (h, whole(h.shape)), (gf, whole(gf.shape)), (bias, whole(bias.shape)), (w, FAR)],
        [(shape, BF16, blk), (shape, BF16, blk), ((4, UNITS, d), BF16, pl.BlockSpec((1, UNITS, d), lambda i: (i, 0, 0)))],
        [pltpu.VMEM((4 * UNITS, d), BF16), pltpu.SemaphoreType.DMA((16,))], gflop=6.0, name="up", limit=48, far=(0, 1),
    )


def down_kernel(aa_ref, ab_ref, res_ref, gf_ref, shift_ref, wa_ref, wb_ref, mixed_ref, loss_ref, held_ref, sem):
    half = 4 * UNITS
    copies = unit_copies(wa_ref, held_ref, sem, 0) + unit_copies(wb_ref, held_ref, sem, half)
    step = pl.program_id(0)

    def rest(feed):
        out = res_ref[...] + (feed + shift_ref[3:4, :])
        mixed_ref[...] = out.astype(BF16)
        loss = jnp.sum(out * gf_ref[...].astype(F32), axis=0, keepdims=True)
        loss = jnp.broadcast_to(jnp.sum(loss, axis=1, keepdims=True), loss_ref.shape)
        loss_ref[...] = jnp.where(step == 0, loss, loss_ref[...] + loss)

    @pl.when(step == 0)
    def _():
        begin(copies)
        feed = None
        for c in range(8):
            end(copies[c])
            a_ref, lo = (aa_ref, c * UNITS) if c < 4 else (ab_ref, (c - 4) * UNITS)
            part = mm(a_ref[:, lo : lo + UNITS], held_ref[c * UNITS : (c + 1) * UNITS, :], NN)
            feed = part if feed is None else feed + part
        rest(feed)

    @pl.when(step > 0)
    def _():
        rest(mm(aa_ref[...], held_ref[:half, :], NN) + mm(ab_ref[...], held_ref[half:, :], NN))


def down(aa, ab, wa, wb, res, gf, shifts):
    n, d = res.shape
    rows = pl.BlockSpec((TILE, d), lambda i: (i, 0))
    units = pl.BlockSpec((TILE, 4 * UNITS), lambda i: (i, 0))
    return call(
        down_kernel, (n // TILE,),
        [(aa, units), (ab, units), (res, rows), (gf, rows), (shifts, whole(shifts.shape)), (wa, ANYWHERE), (wb, ANYWHERE)],
        [((n, d), BF16, rows), ((8, 128), F32, whole((8, 128)))],
        [pltpu.VMEM((8 * UNITS, d), BF16), pltpu.SemaphoreType.DMA((8,))], gflop=9.0, name="down", limit=50,
    )


def slope_kernel(gf_ref, h_ref, sb_ref, sa_ref, wb_ref, wa_ref, gb_ref, ga_ref, nb_ref, na_ref, tb_ref, ta_ref):
    for half, (s_ref, w_ref, g_ref, n_ref, t_ref) in enumerate(((sb_ref, wb_ref, gb_ref, nb_ref, tb_ref), (sa_ref, wa_ref, ga_ref, na_ref, ta_ref))):

        @pl.when((pl.program_id(0) >= 4) == (half == 1))
        def _():
            g = (mm(gf_ref[...], w_ref[...], NT) * s_ref[...].astype(F32)).astype(BF16)
            g_ref[...] = g
            n_ref[0] = mm(g, h_ref[...], TN).astype(BF16)
            t_ref[...] = jnp.sum(g.astype(F32), axis=0, keepdims=True)


def slope(gf, h, sb, sa, wb, wa):
    n, d = gf.shape
    low, high = (lambda t: jnp.minimum(t, 3)), (lambda t: jnp.maximum(t - 4, 0))
    units = lambda at: pl.BlockSpec((n, UNITS), lambda t: (0, at(t)))
    rows = lambda at: pl.BlockSpec((UNITS, d), lambda t: (at(t), 0))
    outs = [(sa.shape, BF16, units(at)) for at in (low, high)]
    outs += [((4, UNITS, d), BF16, pl.BlockSpec((1, UNITS, d), lambda t, at=at: (at(t), 0, 0))) for at in (low, high)]
    outs += [((1, 4 * UNITS), F32, pl.BlockSpec((1, UNITS), lambda t, at=at: (0, at(t)))) for at in (low, high)]
    return call(
        slope_kernel, (8,),
        [(gf, whole(gf.shape)), (h, whole(h.shape)), (sb, units(low)), (sa, units(high)), (wb, rows(low)), (wa, rows(high))], outs,
        gflop=9.0, name="slope", limit=50, far=(0, 1),
    )


def back_kernel(place_ref, ga_ref, gb_ref, gf_ref, res_ref, gain_ref, w_ref, *refs):
    gr_ref, br_ref, oa_ref, ob_ref, vec_ref, held_ref, out_ref, sem, out_sem = refs[8:]
    half = 4 * UNITS
    copies = [c for i in range(2) for c in gathered_copies(place_ref, w_ref, held_ref, sem, i, i * half)]
    outs = out_copies(refs[:8], out_ref, out_sem)
    step = pl.program_id(0)

    def rest(gy, first):
        c = gf_ref[...].astype(F32)
        gv, terms = norm_back(res_ref[...], gy, gain_ref[1:2, :])
        gr = c + gv
        gr_ref[...] = gr
        branch = gr.astype(BF16)
        br_ref[...] = branch
        if first:
            end(outs[0])
        go = mm(branch, out_ref[...].reshape(8 * PAIR, -1), NT).astype(BF16)
        oa_ref[...] = go[:, : 4 * PAIR]
        ob_ref[...] = go[:, 4 * PAIR :]
        sums = column_sums(terms, gy, branch.astype(F32), c)
        vec_ref[...] = sums if first else vec_ref[...] + sums

    @pl.when(step == 0)
    def _():
        begin(copies)
        begin(outs)
        gy = None
        for c in range(8):
            end(copies[c])
            g_ref, lo = (ga_ref, c * UNITS) if c < 4 else (gb_ref, (c - 4) * UNITS)
            part = mm(g_ref[:, lo : lo + UNITS], held_ref[c * UNITS : (c + 1) * UNITS, :], NN)
            gy = part if gy is None else gy + part
        rest(gy, True)

    @pl.when(step > 0)
    def _():
        rest(mm(ga_ref[...], held_ref[:half, :], NN) + mm(gb_ref[...], held_ref[half:, :], NN), False)


def back(place, ga, gb, gf, w, ws, res, gains):
    n, d = res.shape
    rows = pl.BlockSpec((TILE, d), lambda i: (i, 0))
    units = pl.BlockSpec((TILE, 4 * UNITS), lambda i: (i, 0))
    heads = pl.BlockSpec((TILE, 4 * PAIR), lambda i: (i, 0))
    return call(
        back_kernel, (n // TILE,),
        [(place, SCALARS), (ga, units), (gb, units), (gf, rows), (res, rows), (gains, whole(gains.shape)), (w, FAR)] + [(w, FAR) for w in ws],
        [((n, d), F32, rows), ((n, d), BF16, rows), ((n, 4 * PAIR), BF16, heads), ((n, 4 * PAIR), BF16, heads), ((8, d), F32, whole((8, d)))],
        [pltpu.VMEM((8 * UNITS, d), BF16), pltpu.VMEM((8, 4, PART, d), BF16), pltpu.SemaphoreType.DMA((32,)), pltpu.SemaphoreType.DMA((8,))],
        gflop=12.0, name="back", limit=50, far=(0,),
    )


def attend_back_kernel(row_ref, go_ref, qkv_ref, o_ref, lse_ref, g_ref, bias_ref, p_ref, d_ref):
    n = go_ref.shape[0]

    @pl.when(pl.program_id(0) == 0)
    def _():
        fill_mask(bias_ref, row_ref, True)

    q_at, k_at, v_at = slice(0, PAIR), slice(PAIR, 2 * PAIR), slice(2 * PAIR, 3 * PAIR)
    k_turned = jnp.transpose(qkv_ref[:, k_at])
    work = [(i, h) for i in range(n // TILE) for h in range(2)]
    qs, gs, deltas, halves = {}, {}, {}, {}

    def products(i, h):
        part, upto = slice(i * TILE, (i + 1) * TILE), (i + 1) * TILE
        if h == 0:
            go = go_ref[part, :]
            qs[i], gs[i] = split_heads(qkv_ref[part, q_at]), split_heads(go)
            both = jnp.transpose(go.astype(F32) * o_ref[part, :].astype(F32))
            deltas[i] = [jnp.sum(both[k * HD : (k + 1) * HD], axis=0, keepdims=True) for k in range(2)]
        return mm(qkv_ref[:upto, k_at], qs[i][h], NT), mm(qkv_ref[:upto, v_at], gs[i][h], NT)

    def query_grad(i, h, ds):
        part, upto = slice(i * TILE, (i + 1) * TILE), (i + 1) * TILE
        halves[h] = mm(k_turned[h * HD : (h + 1) * HD, :upto], ds, NN)
        if h:
            gq = jnp.transpose(jnp.concatenate([halves[0], halves[1]], axis=0))
            g_ref[part, q_at] = (gq.astype(BF16).astype(F32) * HD**-0.5).astype(BF16)

    now, held = products(*work[0]), None
    for t, (i, h) in enumerate(work):
        part, upto = slice(i * TILE, (i + 1) * TILE), (i + 1) * TILE
        ahead = products(*work[t + 1]) if t + 1 < len(work) else None
        p = jnp.exp2((now[0] + bias_ref[:upto, part] - lse_ref[0, h : h + 1, part]) * LOG2E)
        ds = (p * (now[1] - deltas[i][h])).astype(BF16)
        p_ref[h, :upto, part] = p.astype(BF16)
        d_ref[h, :upto, part] = ds
        if held is not None:
            query_grad(*work[t - 1], held)
        now, held = ahead, ds
    query_grad(*work[-1], held)
    qa, qb = split_heads(qkv_ref[:, q_at])
    ga, gb = split_heads(go_ref[...])
    for i in range(n // TILE):
        part, lo = slice(i * TILE, (i + 1) * TILE), i * TILE
        g_ref[part, k_at] = (mm(d_ref[0, part, lo:], qa[lo:], NN) + mm(d_ref[1, part, lo:], qb[lo:], NN)).astype(BF16)
        g_ref[part, v_at] = (mm(p_ref[0, part, lo:], ga[lo:], NN) + mm(p_ref[1, part, lo:], gb[lo:], NN)).astype(BF16)


def attend_back(row, go, stacks, base, pairs):
    qkv, o, lse = stacks[:3]
    n = go.shape[0]
    pair = pl.BlockSpec((n, PAIR), lambda p: (0, p + base))
    return call(
        attend_back_kernel, (pairs,),
        [(row, whole(row.shape)), (go, pair), (qkv, pl.BlockSpec((n, 3 * PAIR), lambda p: (0, p + base))), (o, pair),
         (lse, pl.BlockSpec((1, 2, n), lambda p: (p + base, 0, 0)))],
        [((n, 3 * PAIR * pairs), BF16, pl.BlockSpec((n, 3 * PAIR), lambda p: (0, p)))],
        [pltpu.VMEM((n, n), F32), pltpu.VMEM((2, n, n), BF16), pltpu.VMEM((2, n, n), BF16)],
        gflop=5.0 * pairs, name="attend_back", limit=32,
    )[0]


def outer_attn_kernel(gb_ref, ga_ref, ob_ref, oa_ref, h_ref, branch_ref, ub_ref, ua_ref, nb_ref, na_ref, *, pairs):
    d = h_ref.shape[1]
    for half, (g_ref, o_ref, up_ref, n_ref) in enumerate(((gb_ref, ob_ref, ub_ref, nb_ref), (ga_ref, oa_ref, ua_ref, na_ref))):

        @pl.when((pl.program_id(0) >= pairs) == (half == 1))
        def _():
            out = mm(o_ref[...], branch_ref[...], TN).astype(BF16)
            qkv = mm(g_ref[...], h_ref[...], TN).astype(BF16)
            sums = jnp.sum(g_ref[...].astype(F32), axis=0, keepdims=True)
            qsum, vsum = sums[:, :PAIR], sums[:, 2 * PAIR :]
            for j in range(4):
                turn = lambda a: jnp.concatenate([a[:, j * PART :], a[:, : j * PART]], axis=1) if j else a
                line = jnp.concatenate([up_ref[j, 0, 0:1, :], turn(qsum), turn(vsum), jnp.zeros((1, d - 3 * PAIR), F32)], axis=1)
                line = jnp.concatenate([line, jnp.zeros((15, d), F32)], axis=0).astype(BF16)
                rows = [out[j * PART : (j + 1) * PART]] + [qkv[i * PAIR + j * PART : i * PAIR + (j + 1) * PART] for i in range(3)]
                n_ref[j] = jnp.concatenate(rows + [line], axis=0)


def outer_attn(gb, ga, ob, oa, base, h, branch, ub, ua):
    n, m = ga.shape
    d = h.shape[1]
    pairs = m // (3 * PAIR)
    low, high = (lambda p: jnp.minimum(p, pairs - 1)), (lambda p: jnp.maximum(p - pairs, 0))
    grad = lambda at: pl.BlockSpec((n, 3 * PAIR), lambda p: (0, at(p)))
    head = lambda at: pl.BlockSpec((n, PAIR), lambda p: (0, at(p) + base))
    out = lambda at: ((4, pairs * ATTN, d), BF16, pl.BlockSpec((4, ATTN, d), lambda p: (0, at(p), 0)))
    return call(
        functools.partial(outer_attn_kernel, pairs=pairs), (2 * pairs,),
        [(gb, grad(low)), (ga, grad(high)), (ob, head(low)), (oa, head(high)), (h, whole(h.shape)), (branch, whole(branch.shape)),
         (ub, pl.BlockSpec((4, 1, 8, PAIR), lambda p: (0, low(p), 0, 0))), (ua, pl.BlockSpec((4, 1, 8, PAIR), lambda p: (0, high(p), 0, 0)))],
        [out(low), out(high)], gflop=2.5 * pairs, name="outer_attn", limit=30,
    )


def combine_kernel(a_ref, b_ref, *outs):
    for j in range(4):
        outs[j][...] = (a_ref[j].astype(F32) + b_ref[j].astype(F32)).astype(BF16)


def combine(a, b):
    _, m, d = a.shape
    rows = 128 if m % 128 == 0 else 96
    block = pl.BlockSpec((4, rows, d), lambda i: (0, i, 0))
    return call(combine_kernel, (m // rows,), [(a, block), (b, block)], [((m, d), BF16, pl.BlockSpec((rows, d), lambda i: (i, 0)))] * 4, gflop=0.1, name="combine", limit=16)


def finish_kernel(*refs, plan):
    grads, w_refs = refs[: len(plan)], refs[len(plan) : len(plan) + 8]
    x_ref, gr_ref, gain_ref, out_ref, vec_ref, held_ref, sem = refs[len(plan) + 8 :]
    step = pl.program_id(0)
    copies, spans, lo = [], [], 0
    for half, base, count in plan:
        spans.append(slice(3 * lo, 3 * (lo + count)))
        mine = []
        for z in range(base, base + count):
            for i in range(3):
                at = 3 * lo + i
                mine.append(pltpu.make_async_copy(w_refs[4 * half + z].at[:, pl.ds((1 + i) * PART, PART)], held_ref.at[at], sem.at[at]))
            lo += 1
        copies.append(mine)

    def tile(first):
        gy = None
        for g_ref, span, mine in zip(grads, spans, copies):
            if first:
                end(mine)
            part = mm(g_ref[...], held_ref[span].reshape(g_ref.shape[1], -1), NN)
            gy = part if gy is None else gy + part
        gv, terms = norm_back(x_ref[...].astype(F32), gy, gain_ref[0:1, :])
        out_ref[...] = gr_ref[...] + gv
        sums = column_sums(terms, gy)
        vec_ref[...] = sums if first else vec_ref[...] + sums

    @pl.when(step == 0)
    def _():
        begin(copies)
        tile(True)

    @pl.when(step > 0)
    def _():
        tile(False)


def finish(grads, ws, x, gr, gains):
    n, d = x.shape
    rows = pl.BlockSpec((TILE, d), lambda i: (i, 0))
    plan = tuple((half, base, g.shape[1] // (3 * PAIR)) for g, half, base in grads)
    return call(
        functools.partial(finish_kernel, plan=plan), (n // TILE,),
        [(g, pl.BlockSpec((TILE, g.shape[1]), lambda i: (i, 0))) for g, _, _ in grads]
        + [(w, FAR) for w in ws] + [(x, rows), (gr, rows), (gains, whole(gains.shape))],
        [((n, d), F32, rows), ((8, d), F32, whole((8, d)))],
        [pltpu.VMEM((24, 4, PART, d), BF16), pltpu.SemaphoreType.DMA((24,))], gflop=10.0, name="finish", limit=56,
    )


def pack_kernel(r_ref, *refs, plan, bands):
    srcs, (out_ref, held_ref, in_sem, out_sem) = refs[:-4], refs[-4:]
    copies = []
    for at, (src, quarter, count, dst) in enumerate(plan):
        source = srcs[src] if quarter is None else srcs[src].at[r_ref[0] ^ quarter]
        copies.append(pltpu.make_async_copy(source, held_ref.at[pl.ds(dst, count)], in_sem.at[at]))
    begin((copies,))
    band = held_ref.shape[0] // bands
    outs = []
    for b in range(bands):
        end([copy for copy, (_, _, _, dst) in zip(copies, plan) if dst // band == b])
        outs.append(pltpu.make_async_copy(held_ref.at[pl.ds(b * band, band)], out_ref.at[pl.ds(b * band, band)], out_sem.at[b]))
        begin((outs[-1:],))
    end(outs)


def pack(r, arrays, plan, bands):
    rows = sum(count for _, _, count, _ in plan)
    d = arrays[0].shape[-1]
    return call(
        functools.partial(pack_kernel, plan=plan, bands=bands), (), [(r, SCALARS)] + [(a, ANYWHERE) for a in arrays], [((rows, d), BF16, ANYWHERE)],
        [pltpu.VMEM((rows, d), BF16), pltpu.SemaphoreType.DMA((len(plan),)), pltpu.SemaphoreType.DMA((bands,))], gflop=0.0, name="pack", limit=14,
    )[0]


def stack_z(r, parts):
    n = parts[0].shape[0]
    return pack(r, parts, [(i, None, n, i * n) for i in range(3)], 3)


def stack_units(r, quarters, sides):
    n = quarters.shape[1]
    plan = [(0, j, n, 4 * n * j) for j in range(4)] + [(1 + j, None, 3 * n, 4 * n * j + n) for j in range(4)]
    return pack(r, [quarters, *sides], plan, 4)


def settle_kernel(r_ref, *refs):
    qkv_ref, bias_ref, out_ref, held_ref = refs[4:]
    for j in range(4):
        held_ref[j] = refs[j][...]
    quarters = [held_ref[r_ref[0] ^ q].astype(F32) for q in range(4)]
    for i in range(3):
        qkv_ref[i] = jnp.transpose(jnp.concatenate([a[(1 + i) * PART : (2 + i) * PART] for a in quarters], axis=0))
    bias_ref[...] = jnp.concatenate([a[4 * PART : 4 * PART + 1, : 3 * PAIR] for a in quarters] + [jnp.zeros((4, 3 * PAIR), F32)], axis=0)
    out_ref[...] = jnp.concatenate([a[:PART] for a in quarters], axis=0)


def settle(r, pieces):
    d = pieces[0].shape[1]
    shapes = [(3, d, PAIR), (8, 3 * PAIR), (PAIR, d)]
    return call(
        settle_kernel, (), [(r, SCALARS)] + [(a, whole(a.shape)) for a in pieces], [(shape, F32, whole(shape)) for shape in shapes],
        [pltpu.VMEM((4, ATTN, d), BF16)], gflop=0.1, name="settle", limit=24,
    )


def settle_units_kernel(g_ref, down_ref, up_ref):
    down_ref[...] = g_ref[0, 0].astype(F32)
    up_ref[...] = jnp.transpose(g_ref[0, 1].astype(F32))


def settle_units(g):
    d = g.shape[-1]
    return call(
        settle_units_kernel, (4,), [(g, pl.BlockSpec((1, 2, PAIR, d), lambda q: (q, 0, 0, 0)))],
        [((4 * PAIR, d), F32, pl.BlockSpec((PAIR, d), lambda q: (q, 0))), ((d, 4 * PAIR), F32, pl.BlockSpec((d, PAIR), lambda q: (0, q)))],
        gflop=0.1, name="settle_units", limit=24,
    )


def moved(array, axis, mask):
    size = lax.axis_size(axis)
    return lax.ppermute(array, axis, [(i, i ^ mask) for i in range(size)])


def across(array):
    return moved(array, "mp", 1)


def beside(array, j):
    return moved(array, "rows", j)


def along_z(array, z):
    return moved(array, "mp", 2 * z)


def fence(*trees):
    return lax.optimization_barrier(trees)


def by_z(a):
    z = lax.axis_index("mp") // 2
    low = [jnp.where(z & 1, a[i ^ 1], a[i]) for i in range(4)]
    return [jnp.where(z & 2, low[i ^ 2], low[i]) for i in range(4)]


def added(*terms):
    total = terms[0].astype(F32)
    for term in terms[1:]:
        total = total + term.astype(F32)
    return total.astype(BF16)


def any_spread(parts):
    core = lax.axis_index("mp") % 2
    return [lax.dynamic_index_in_dim(parts, c, 0, False) for c in (core, 1 - core)]


def any_reduced(full, axis):
    return lax.psum(lax.psum_scatter(full, "mp", scatter_dimension=axis, tiled=True), "rows")


def up_sums(total, first, last):
    return jnp.pad(total.reshape(4, 4, 1, PAIR)[:, first:last], ((0, 0), (0, 0), (0, 7), (0, 0)))


def stacked_vectors(one, two, loss):
    d = one.shape[1]
    at = lax.axis_index("rows") * lax.axis_size("mp") + lax.axis_index("mp")
    losses = jnp.where(jnp.arange(d, dtype=jnp.int32) == at, loss[0, 0] / math.sqrt(SLOTS * d), 0.0)
    return jnp.stack([one[0], two[0], one[1], two[2], two[1], two[3], losses, jnp.zeros_like(losses)])


def any_mesh(tokens, qkv_rows, qv_bias, out_weight, up_rows, up_bias, down_weight, gains, shifts, live, line, cotangent):
    d = tokens.shape[1]
    r = jnp.zeros((1,), jnp.int32)
    every = lambda a, axis=0: lax.all_gather(a, "mp", axis=axis, tiled=True)
    heads = lambda a: a.reshape(2, 4, 4, PART, d)
    qkv_all, qvb_all = every(qkv_rows, 1), every(qv_bias, 1)
    small = lambda a: jnp.tile(a.reshape(2, 4, 4, PART), (1, 1, 1, 4))
    ups = every(up_bias).reshape(2, 4, 4, PAIR).swapaxes(1, 2)
    bias = jnp.concatenate([ups, small(qvb_all[0]), small(qvb_all[1])], axis=3)
    bias = jnp.pad(bias[:, :, :, None, :], ((0, 0), (0, 0), (0, 0), (0, 15), (0, d - 3 * PAIR)))
    wa, wb = any_spread(jnp.concatenate([heads(every(out_weight)), heads(qkv_all[0]), heads(qkv_all[1]), heads(qkv_all[2]), bias], axis=3))

    place = jnp.zeros((3,), jnp.int32)
    da, db = any_spread(every(down_weight).reshape(2, 16 * PAIR, d))
    by_half = jnp.stack(any_spread(every(up_rows).reshape(2, 4, 4, PAIR, d)))
    up_all = jnp.moveaxis(by_half, 0, 2).reshape(32, PAIR, d)
    h1, gf = prep(tokens, cotangent, live, gains, shifts)
    stacks, ws = [], [w[z] for w in (wa, wb) for z in range(4)]
    for w in (wa, wb):
        stacks.append(attend(r, line, h1, [w[0], w[1], w[2], w[3]], "packed", 0)[0])
    stack_a, stack_b = stacks
    res, h2 = join(tokens, stack_a[1], stack_b[1], ws, gains, shifts)
    aa, sa, down_a = up(place, h2, gf, up_all, stack_a[3], 0)
    ab, sb, down_b = up(place, h2, gf, up_all, stack_b[3], 1)
    g_down = added(down_a, across(down_b))
    mixed, loss = down(aa, ab, da, db, res, gf, shifts)
    gb, ga, up_b, up_a, total_b, total_a = slope(gf, h2, sb, sa, db, da)
    g_up = added(up_a, across(up_b))
    gr, branch, go_a, go_b, two = back(place, ga, gb, gf, up_all, ws, res, gains)
    back_b = attend_back(line, go_b, stack_b, 0, 4)
    back_a = attend_back(line, go_a, stack_a, 0, 4)
    nb, na = outer_attn(back_b, back_a, stack_b[1], stack_a[1], 0, h1, branch, up_sums(total_b, 0, 4), up_sums(total_a, 0, 4))
    g_attn = added(na, across(nb)).reshape(4, 4, ATTN, d)
    input_grad, one = finish([(back_a, 0, 0), (back_b, 1, 0)], ws, tokens, gr, gains)
    vectors = lax.psum(stacked_vectors(one, two, loss), ("rows", "mp"))
    core = lax.axis_index("mp") % 2
    full = lambda g: lax.dynamic_update_index_in_dim(jnp.zeros((2,) + g.shape, F32), g.astype(F32), core, 0)
    ordered = lambda g: full(g).swapaxes(1, 2).reshape(-1, g.shape[-1])
    down_grad, up_grad = [any_reduced(full(g).reshape(-1, d), 0) for g in (g_down, g_up)]
    out_grad = any_reduced(ordered(g_attn[:, :, :PART]), 0)
    qkv_grad = any_reduced(jnp.stack([ordered(g_attn[:, :, i * PART : (i + 1) * PART]) for i in (1, 2, 3)]), 1)
    lines = g_attn[:, :, 4 * PART]
    up_bias_grad = any_reduced(full(lines[:, :, :PAIR]).reshape(-1), 0)
    ordered = lambda g: full(g).swapaxes(1, 2).reshape(-1)
    qv_bias_grad = any_reduced(jnp.stack([ordered(lines[:, :, at : at + PART]) for at in (PAIR, 2 * PAIR)]), 1)
    qkv_grad, up_grad = jnp.swapaxes(qkv_grad, 1, 2), up_grad.T
    return mixed, input_grad, qkv_grad, qv_bias_grad, out_grad, up_grad, up_bias_grad, down_grad, vectors


def small_mesh(tokens, qkv_rows, qv_bias, out_weight, up_rows, up_bias, down_weight, gains, shifts, live, line, cotangent):
    d = tokens.shape[1]
    row = lax.axis_index("rows")
    r = row.reshape(1).astype(jnp.int32)
    mine = lambda a: lax.dynamic_index_in_dim(a, row, 0, False)
    sides = lambda a: [beside(a, j) for j in (1, 2, 3)]
    sides3 = lambda g: [beside(g[j], j) for j in (1, 2, 3)]

    bias = jnp.concatenate(
        [up_bias.reshape(4, PAIR), jnp.tile(qv_bias[0].reshape(4, PART), (1, 4)), jnp.tile(qv_bias[1].reshape(4, PART), (1, 4))], axis=1
    )
    bias = jnp.pad(bias[:, None, :], ((0, 0), (0, 15), (0, d - 3 * PAIR)))
    qkv4 = qkv_rows.reshape(3, 4, PART, d).swapaxes(0, 1).reshape(4, 3 * PART, d)
    a4 = jnp.concatenate([out_weight.reshape(4, PART, d), qkv4, bias], axis=1)
    pa = mine(a4)
    c4 = down_weight.reshape(4, PAIR, d)
    pc = mine(c4)
    index = lax.axis_index("mp").astype(jnp.int32)
    place = jnp.stack([row.astype(jnp.int32), index // 2, index % 2])
    up_all = lax.all_gather(mine(up_rows.reshape(4, PAIR, d)), ("rows", "mp"))
    p1, c2 = along_z(pa, 1), along_z(pc, 2)
    h1, gf = prep(tokens, cotangent, live, gains, shifts)
    p1, c2, h1, gf, pa, pc = fence(p1, c2, h1, gf, pa, pc)
    s1, p2 = sides(p1), along_z(pa, 2)
    sa, w0 = attend(r, line, h1, [a4], "quarters", 0)
    s1, p2, sa, w0, h1, pa = fence(s1, p2, sa, w0, h1, pa)
    s2, p3, x0 = sides(p2), along_z(pa, 3), across(w0)
    sa, w1 = attend(r, line, h1, [p1, *s1], "pieces", 1, sa)
    s2, p3, x0, sa, w1, h1, pc = fence(s2, p3, x0, sa, w1, h1, pc)
    s3, c1 = sides(p3), along_z(pc, 1)
    sa, w2 = attend(r, line, h1, [p2, *s2], "pieces", 2, sa)
    sb, _ = attend(r, line, h1, [x0], "packed", 0)
    s3, c1, sa, w1, w2, sb, h1, pc = fence(s3, c1, sa, w1, w2, sb, h1, pc)
    c3, x1, x2 = along_z(pc, 3), across(w1), across(w2)
    sb, _ = attend(r, line, h1, [x1, x2], "packed", 1, sb)
    sa, w3 = attend(r, line, h1, [p3, *s3], "pieces", 3, sa)
    c3, sa, sb, w3, h1 = fence(c3, sa, sb, w3, h1)
    cs = stack_z(r, [c1, c2, c3])
    cx, x3 = sides(cs), across(w3)
    ws = [w0, w1, w2, w3, x0, x1, x2, x3]
    sb, _ = attend(r, line, h1, [x3], "packed", 3, sb)
    res, h2 = join(tokens, sa[1], sb[1], ws, gains, shifts)
    ab, lb, down_b = up(place, h2, gf, up_all, sb[3], 1)
    cx, ab, lb, down_b, h2 = fence(cx, ab, lb, down_b, h2)
    da = stack_units(r, c4, [cs, *cx])
    db, down_x = across(da), across(down_b)
    aa, la, down_a = up(place, h2, gf, up_all, sa[3], 0)
    da, db, down_x, aa, la, down_a, h2 = fence(da, db, down_x, aa, la, down_a, h2)
    g_down = combine(down_a, down_x)
    fx = [beside(g_down[j], j) for j in (1, 2)]
    gb, ga, up_b, up_a, total_b, total_a = slope(gf, h2, lb, la, db, da)
    fx, gb, ga, up_b, up_a, g3 = fence(fx, gb, ga, up_b, up_a, g_down[3])
    fx, up_x = [*fx, beside(g3, 3)], across(up_b)
    gr, branch, go_a, go_b, two = back(place, ga, gb, gf, up_all, ws, res, gains)
    g_up = combine(up_a, up_x)
    fx, gr, branch, go_a, go_b, g_up = fence(fx, gr, branch, go_a, go_b, g_up)
    columns = [[2 * i + core for i in range(4)] for core in range(2)]
    reduce_z = lambda t: lax.psum_scatter(jnp.stack(by_z(t)), "mp", scatter_dimension=0, tiled=False, axis_index_groups=columns)
    f_down = reduce_z(added(g_down[0], *fx).reshape(4, PAIR, d))
    fx = [beside(g_up[j], j) for j in (1, 2)]
    back_b1 = attend_back(line, go_b, sb, 2, 2)
    back_a1 = attend_back(line, go_a, sa, 2, 2)
    nb1, na1 = outer_attn(back_b1, back_a1, sb[1], sa[1], 2, h1, branch, up_sums(total_b, 2, 4), up_sums(total_a, 2, 4))
    fx, back_a1, back_b1, nb1, na1, go_a, go_b, g3 = fence(fx, back_a1, back_b1, nb1, na1, go_a, go_b, g_up[3])
    fx, n1_x = [*fx, beside(g3, 3)], across(nb1)
    back_b2 = attend_back(line, go_b, sb, 0, 2)
    back_a2 = attend_back(line, go_a, sa, 0, 2)
    nb2, na2 = outer_attn(back_b2, back_a2, sb[1], sa[1], 0, h1, branch, up_sums(total_b, 0, 2), up_sums(total_a, 0, 2))
    n1 = combine(na1, n1_x)
    fx, n1, back_b2, back_a2, nb2, na2, gr, f_down = fence(fx, n1, back_b2, back_a2, nb2, na2, gr, f_down)
    f_up = reduce_z(added(g_up[0], *fx).reshape(4, PAIR, d))
    ex, n2_x = sides3(n1), across(nb2)
    input_grad, one = finish([(back_a2, 0, 0), (back_a1, 0, 2), (back_b2, 1, 0), (back_b1, 1, 2)], ws, tokens, gr, gains)
    n2 = combine(na2, n2_x)
    ex, input_grad, one, n2, aa, f_up = fence(ex, input_grad, one, n2, aa, f_up)
    units = lax.all_gather(jnp.stack([f_down, f_up]), "rows")
    t1 = added(n1[0], *ex).reshape(2, ATTN, d)
    ex, y2, y3 = sides3(n2), along_z(t1[0], 2), along_z(t1[1], 3)
    mixed, loss = down(aa, ab, da, db, res, gf, shifts)
    vectors = stacked_vectors(one, two, loss)
    ex, y2, y3, mixed, vectors = fence(ex, y2, y3, mixed, vectors)
    t2 = added(n2[0], *ex).reshape(2, ATTN, d)
    y1, vx = along_z(t2[1], 1), sides(vectors)
    vx, y1, vectors, t2 = fence(vx, y1, vectors, t2)
    f = added(t2[0], y1, y2, y3)
    d_last = sides(f)
    vectors = (vectors + vx[0]) + (vx[1] + vx[2])
    vectors = vectors + across(vectors)
    vz = [along_z(vectors, i) for i in (1, 2, 3)]
    vectors = (vectors + vz[0]) + (vz[1] + vz[2])
    down_grad, up_grad = settle_units(units)
    d_last, down_grad, up_grad, vectors = fence(d_last, down_grad, up_grad, vectors)
    qkv_grad, biases, out_grad = settle(r, [f, *d_last])
    up_bias_grad = biases[:4, :PAIR].reshape(-1)
    qv_bias_grad = jnp.stack([biases[:4, at : at + PART].reshape(-1) for at in (PAIR, 2 * PAIR)])
    return mixed, input_grad, qkv_grad, qv_bias_grad, out_grad, up_grad, up_bias_grad, down_grad, vectors


def body(tokens, qkv_weight, qv_bias, out_weight, up_weight, up_bias, down_weight, norm_gains, shift_vectors, lengths, cotangent):
    n, d = tokens.shape
    place, row = lax.axis_index("mp"), lax.axis_index("rows")
    endings = jnp.cumsum(lax.dynamic_slice_in_dim(lengths, place, 1, 0)[0])
    position = jnp.arange(SLOTS, dtype=jnp.int32)
    segment = jnp.sum((position[:, None] >= endings[None, :]).astype(jnp.int32), axis=1)
    live = (segment < DOCS).astype(F32)[:, None]
    ident = jnp.where(segment < DOCS, segment, DOCS + position).astype(jnp.int32)
    layer = small_mesh if (lax.axis_size("rows"), lax.axis_size("mp")) == (4, 8) else any_mesh
    mixed, input_grad, qkv_grad, qv_bias_grad, out_grad, up_grad, up_bias_grad, down_grad, vectors = layer(
        tokens, jnp.swapaxes(qkv_weight, 1, 2), qv_bias, out_weight, up_weight.T, up_bias, down_weight,
        norm_gains.astype(F32), shift_vectors.astype(F32), live, ident.reshape(1, n), cotangent,
    )
    share = d // lax.axis_size("mp")
    vector_grad = lax.dynamic_slice_in_dim(vectors[:6], place * share, share, 1)
    block_loss = lax.dynamic_slice_in_dim(vectors[6], row * lax.axis_size("mp"), lax.axis_size("mp"), 0)
    return (
        mixed, block_loss, input_grad, qkv_grad, qv_bias_grad, out_grad,
        up_grad, up_bias_grad, down_grad, vector_grad,
    )


def solution(mesh):
    placed = (
        P(("rows", "mp"), None),
        P(None, None, "mp"),
        P(None, "mp"),
        P("mp", None),
        P(None, "mp"),
        P("mp"),
        P("mp", None),
        P(),
        P(),
        P("rows", None),
        P(("rows", "mp"), None),
    )
    return jax.shard_map(
        body,
        mesh=mesh,
        in_specs=placed,
        out_specs=(
            P(("rows", "mp"), None),
            P("rows"),
            P(("rows", "mp"), None),
            P(None, None, "mp"),
            P(None, "mp"),
            P("mp", None),
            P(None, "mp"),
            P("mp"),
            P("mp", None),
            P(None, "mp"),
        ),
        check_vma=False,
    )
```

```python
import functools
import math

import jax
import jax.numpy as jnp
from jax import lax
from jax.experimental import pallas as pl
from jax.experimental.pallas import tpu as pltpu
from jax.sharding import PartitionSpec as P

HD = 64
PAIR = 128
PART = 32
ATTN = 144
TILE = 256
UNITS = 512
SCALE = 0.4e9
SLOTS = 1024
DOCS = 6
EPSILON = 1e-05
MASKED = -1e30
LOG2E = math.log2(math.e)
F32, BF16 = jnp.float32, jnp.bfloat16
NN = (((1,), (0,)), ((), ()))
NT = (((1,), (1,)), ((), ()))
TN = (((0,), (0,)), ((), ()))


def mm(a, b, dims):
    return lax.dot_general(a, b, dims, preferred_element_type=F32)


def whole(shape):
    return pl.BlockSpec(shape, lambda *_: (0,) * len(shape), pipeline_mode=pl.Buffered(1))


ANYWHERE = pl.BlockSpec(memory_space=pl.ANY)
FAR = pl.BlockSpec(memory_space=pltpu.HBM)
SCALARS = pl.BlockSpec(memory_space=pltpu.SMEM)


def call(kernel, grid, ins, outs, scratch=(), gflop=1.0, name=None, limit=56, aliases=None, far=()):
    nbytes = sum(a.size * a.dtype.itemsize for a, _ in ins)
    nbytes += sum(math.prod(s) * jnp.dtype(d).itemsize for s, d, _ in outs)
    return pl.pallas_call(
        kernel,
        grid=grid,
        in_specs=[s for _, s in ins],
        out_specs=[s for _, _, s in outs],
        out_shape=[pltpu.HBM(s, d) if i in far else jax.ShapeDtypeStruct(s, d) for i, (s, d, _) in enumerate(outs)],
        scratch_shapes=list(scratch),
        input_output_aliases=aliases or {},
        compiler_params=pltpu.CompilerParams(vmem_limit_bytes=limit << 20),
        cost_estimate=pl.CostEstimate(flops=int(gflop * SCALE), bytes_accessed=nbytes, transcendentals=0),
        name=name,
    )(*[a for a, _ in ins])


def normed(v):
    spread = v - jnp.mean(v, axis=1, keepdims=True)
    rstd = lax.rsqrt(jnp.mean(spread * spread, axis=1, keepdims=True) + EPSILON)
    return spread * rstd, rstd


def norm_back(v, gy, gain):
    norm, rstd = normed(v)
    gn = gy * gain
    gv = rstd * (gn - jnp.mean(gn, axis=1, keepdims=True) - norm * jnp.mean(gn * norm, axis=1, keepdims=True))
    return gv, gy * norm


def column_sums(*values):
    d = values[0].shape[1]
    rows = [jnp.sum(v, axis=0, keepdims=True) for v in values]
    return jnp.concatenate(rows + [jnp.zeros((8 - len(rows), d), F32)], axis=0)


def prep_kernel(x_ref, cot_ref, live_ref, gain_ref, shift_ref, h_ref, gf_ref):
    norm, _ = normed(x_ref[...].astype(F32))
    h_ref[...] = (norm * gain_ref[0:1, :] + shift_ref[0:1, :]).astype(BF16)
    gf_ref[...] = (cot_ref[...].astype(F32) * live_ref[...]).astype(BF16)


def prep(x, cot, live, gains, shifts):
    n, d = x.shape
    rows = pl.BlockSpec((TILE, d), lambda i: (i, 0))
    return call(
        prep_kernel, (n // TILE,),
        [(x, rows), (cot, rows), (live, pl.BlockSpec((TILE, 1), lambda i: (i, 0))), (gains, whole(gains.shape)), (shifts, whole(shifts.shape))],
        [((n, d), BF16, rows), ((n, d), BF16, rows)], gflop=1.0, name="prep", limit=20,
    )


def fill_mask(bias_ref, row_ref, transposed):
    n = row_ref.shape[1]
    col = jnp.transpose(jnp.broadcast_to(row_ref[...], (8, n)))[:, :1]
    for i in range(n // TILE):
        part, upto = slice(i * TILE, (i + 1) * TILE), (i + 1) * TILE
        if transposed:
            same = col[:upto, :] == row_ref[:, part]
            key = lax.broadcasted_iota(jnp.int32, (upto, TILE), 0)
            query = lax.broadcasted_iota(jnp.int32, (upto, TILE), 1) + i * TILE
            bias_ref[:upto, part] = jnp.where(same & (key <= query), 0.0, MASKED)
        else:
            same = col[part, :] == row_ref[:, :upto]
            query = lax.broadcasted_iota(jnp.int32, (TILE, upto), 0) + i * TILE
            key = lax.broadcasted_iota(jnp.int32, (TILE, upto), 1)
            bias_ref[part, :upto] = jnp.where(same & (key <= query), 0.0, MASKED)


def pair_bias(pieces, at):
    lane = lax.broadcasted_iota(jnp.int32, (1, PAIR), 1) // PART
    row = jnp.zeros((1, PAIR), F32)
    for j in range(4):
        row = jnp.where(lane == j, pieces[j][4 * PART : ATTN, at : at + PAIR].astype(F32)[0:1, :], row)
    return row


def split_heads(a):
    first = lax.broadcasted_iota(jnp.int32, (1, PAIR), 1) < HD
    zero = jnp.zeros((), a.dtype)
    return jnp.where(first, a, zero), jnp.where(first, zero, a)


def attend_kernel(r_ref, row_ref, h_ref, *refs, mode, stacked, count):
    w_refs, refs = refs[:count], refs[count + (STACKS if stacked else 0) :]
    qkv_ref, o_ref, lse_ref, up_ref = refs[:STACKS]
    bias_ref, held_ref = refs[-2:]
    n = h_ref.shape[0]

    @pl.when(pl.program_id(0) == 0)
    def _():
        fill_mask(bias_ref, row_ref, False)

    if mode == "packed":
        for p in range(count):

            @pl.when(pl.program_id(0) == p)
            def _():
                held_ref[...] = w_refs[p][...]
    else:
        for j in range(4):
            piece = w_refs[0][r_ref[0] ^ j] if mode == "quarters" else w_refs[j][...]
            held_ref[j] = piece
            refs[STACKS][j] = piece
    pieces = [held_ref[j] for j in range(4)]
    up_ref[0] = jnp.concatenate([piece[4 * PART :, :PAIR].astype(F32)[0:1] for piece in pieces], axis=0)
    wall = jnp.concatenate([pieces[j][i * PART : (i + 1) * PART] for i in (1, 2, 3) for j in range(4)], axis=0)
    qkv = mm(h_ref[...], wall, NT)
    qkv_ref[:, :PAIR] = ((qkv[:, :PAIR] + pair_bias(pieces, 128)) * HD**-0.5).astype(BF16)
    qkv_ref[:, PAIR : 2 * PAIR] = qkv[:, PAIR : 2 * PAIR].astype(BF16)
    v = (qkv[:, 2 * PAIR :] + pair_bias(pieces, 256)).astype(BF16)
    qkv_ref[:, 2 * PAIR :] = v
    vx = jnp.concatenate([v, jnp.ones((n, PAIR), BF16)], axis=1)
    first = lax.broadcasted_iota(jnp.int32, (1, PAIR), 1) < HD
    work = [(i, h) for i in range(n // TILE) for h in range(2)]
    outs = {}

    def scores(i, h):
        q = split_heads(qkv_ref[i * TILE : (i + 1) * TILE, :PAIR])[h]
        return mm(q, qkv_ref[: (i + 1) * TILE, PAIR : 2 * PAIR], NT)

    def weigh(i, h, e, top):
        part = slice(i * TILE, (i + 1) * TILE)
        ov = mm(e, vx[: (i + 1) * TILE], NN)
        total = ov[:, PAIR:]
        outs[h] = ov[:, :PAIR] / total
        lse_ref[0, h : h + 1, part] = jnp.transpose(top + jnp.log(total))[0:1, :]
        if h:
            o_ref[part, :] = jnp.where(first, outs[0], outs[1]).astype(BF16)

    s, held = scores(*work[0]), None
    for t, (i, h) in enumerate(work):
        ahead = scores(*work[t + 1]) if t + 1 < len(work) else None
        s = s + bias_ref[i * TILE : (i + 1) * TILE, : (i + 1) * TILE]
        top = jnp.max(s, axis=1, keepdims=True)
        e = jnp.exp2((s - top) * LOG2E).astype(BF16)
        if held is not None:
            weigh(*work[t - 1], *held)
        s, held = ahead, (e, top)
    weigh(*work[-1], *held)


STACKS = 4


def attend(r, row, h, w, mode, z, stacks=None):
    n, d = h.shape
    pairs = len(w) if mode == "packed" else 1
    outs = [
        ((n, 12 * PAIR), BF16, pl.BlockSpec((n, 3 * PAIR), lambda p: (0, z + p))),
        ((n, 4 * PAIR), BF16, pl.BlockSpec((n, PAIR), lambda p: (0, z + p))),
        ((4, 2, n), F32, pl.BlockSpec((1, 2, n), lambda p: (z + p, 0, 0))),
        ((4, 4, PAIR), F32, pl.BlockSpec((1, 4, PAIR), lambda p: (z + p, 0, 0))),
    ]
    if mode != "packed":
        outs.append(((4, ATTN, d), BF16, whole((4, ATTN, d))))
    ins = [(r, SCALARS), (row, whole(row.shape)), (h, whole(h.shape))] + [(a, whole(a.shape)) for a in w]
    aliases = {len(ins) + i: i for i in range(STACKS)} if stacks else None
    ins += [(a, FAR) for a in stacks or ()]
    *stacks, last = *call(
        functools.partial(attend_kernel, mode=mode, stacked=bool(aliases), count=len(w)), (pairs,), ins, outs,
        [pltpu.VMEM((n, n), F32), pltpu.VMEM((4, ATTN, d), BF16)], gflop=5.0 * pairs, name="attend", limit=28, aliases=aliases, far=range(STACKS),
    ), *([None] if mode == "packed" else [])
    return stacks, last


def out_copies(refs, held_ref, sem):
    return [[pltpu.make_async_copy(ref.at[:, pl.ds(0, PART)], held_ref.at[i], sem.at[i]) for i, ref in enumerate(refs)]]


def join_kernel(x_ref, oa_ref, ob_ref, gain_ref, shift_ref, *refs):
    r_ref, h_ref, held_ref, sem = refs[8:]

    @pl.when(pl.program_id(0) == 0)
    def _():
        copies = out_copies(refs[:8], held_ref, sem)
        begin(copies)
        end(copies[0])

    half = lambda a: held_ref[a : a + 4].reshape(4 * PAIR, -1)
    branch = mm(oa_ref[...], half(0), NN) + mm(ob_ref[...], half(4), NN)
    r = x_ref[...].astype(F32) + (branch + shift_ref[1:2, :])
    r_ref[...] = r
    norm, _ = normed(r)
    h_ref[...] = (norm * gain_ref[1:2, :] + shift_ref[2:3, :]).astype(BF16)


def join(x, oa, ob, ws, gains, shifts):
    n, d = x.shape
    rows = pl.BlockSpec((TILE, d), lambda i: (i, 0))
    half = pl.BlockSpec((TILE, 4 * PAIR), lambda i: (i, 0))
    return call(
        join_kernel, (n // TILE,),
        [(x, rows), (oa, half), (ob, half), (gains, whole(gains.shape)), (shifts, whole(shifts.shape))] + [(w, FAR) for w in ws],
        [((n, d), F32, rows), ((n, d), BF16, rows)], [pltpu.VMEM((8, 4, PART, d), BF16), pltpu.SemaphoreType.DMA((8,))],
        gflop=4.0, name="join", limit=56, far=(0,),
    )


def unit_copies(w_ref, held_ref, sem, first):
    spans = [(j * UNITS, first + j * UNITS) for j in range(4)]
    return [[pltpu.make_async_copy(w_ref.at[pl.ds(a, UNITS)], held_ref.at[pl.ds(b, UNITS)], sem.at[b // UNITS])] for a, b in spans]


def gathered_copies(place_ref, w_ref, held_ref, sem, half, first):
    r, at, core = place_ref[0], place_ref[1], place_ref[2]
    copies = []
    for j in range(4):
        lo = first + j * UNITS
        source = lambda z: w_ref.at[((r ^ j) * 4 + (at ^ z)) * 2 + (core ^ half)]
        copies.append([pltpu.make_async_copy(source(z), held_ref.at[pl.ds(lo + z * PAIR, PAIR)], sem.at[lo // PAIR + z]) for z in range(4)])
    return copies


def begin(copies):
    for pair in copies:
        for copy in pair:
            copy.start()


def end(pair):
    for copy in pair:
        copy.wait()


def up_kernel(place_ref, h_ref, gf_ref, bias_ref, w_ref, act_ref, slope_ref, g_ref, held_ref, sem, *, half):
    copies = gathered_copies(place_ref, w_ref, held_ref, sem, half, 0)
    step = pl.program_id(0)

    @pl.when(step == 0)
    def _():
        begin(copies)

    for j in range(4):

        @pl.when(step == j)
        def _():
            end(copies[j])
            bias = jnp.concatenate([bias_ref[z, j : j + 1, :] for z in range(4)], axis=1)
            c0, c1 = math.sqrt(2 / math.pi), math.sqrt(2 / math.pi) * 0.044715
            u = mm(h_ref[...], held_ref[j * UNITS : (j + 1) * UNITS, :], NT) + bias
            square = u * u
            s = 0.5 + 0.5 * jnp.tanh(u * (c0 + c1 * square))
            us = u * s
            act = us.astype(BF16)
            act_ref[...] = act
            slope_ref[...] = (s + (us - us * s) * (2 * c0 + 6 * c1 * square)).astype(BF16)
            g_ref[0] = mm(act, gf_ref[...], TN).astype(BF16)


def up(place, h, gf, w, bias, half):
    n, d = h.shape
    blk = pl.BlockSpec((n, UNITS), lambda i: (0, i))
    shape = (n, 4 * UNITS)
    return call(
        functools.partial(up_kernel, half=half), (4,),
        [(place, SCALARS), (h, whole(h.shape)), (gf, whole(gf.shape)), (bias, whole(bias.shape)), (w, FAR)],
        [(shape, BF16, blk), (shape, BF16, blk), ((4, UNITS, d), BF16, pl.BlockSpec((1, UNITS, d), lambda i: (i, 0, 0)))],
        [pltpu.VMEM((4 * UNITS, d), BF16), pltpu.SemaphoreType.DMA((16,))], gflop=6.0, name="up", limit=48, far=(0, 1),
    )


def down_kernel(aa_ref, ab_ref, res_ref, gf_ref, shift_ref, wa_ref, wb_ref, mixed_ref, loss_ref, held_ref, sem):
    half = 4 * UNITS
    copies = unit_copies(wa_ref, held_ref, sem, 0) + unit_copies(wb_ref, held_ref, sem, half)
    step = pl.program_id(0)

    def rest(feed):
        out = res_ref[...] + (feed + shift_ref[3:4, :])
        mixed_ref[...] = out.astype(BF16)
        loss = jnp.sum(out * gf_ref[...].astype(F32), axis=0, keepdims=True)
        loss = jnp.broadcast_to(jnp.sum(loss, axis=1, keepdims=True), loss_ref.shape)
        loss_ref[...] = jnp.where(step == 0, loss, loss_ref[...] + loss)

    @pl.when(step == 0)
    def _():
        begin(copies)
        feed = None
        for c in range(8):
            end(copies[c])
            a_ref, lo = (aa_ref, c * UNITS) if c < 4 else (ab_ref, (c - 4) * UNITS)
            part = mm(a_ref[:, lo : lo + UNITS], held_ref[c * UNITS : (c + 1) * UNITS, :], NN)
            feed = part if feed is None else feed + part
        rest(feed)

    @pl.when(step > 0)
    def _():
        rest(mm(aa_ref[...], held_ref[:half, :], NN) + mm(ab_ref[...], held_ref[half:, :], NN))


def down(aa, ab, wa, wb, res, gf, shifts):
    n, d = res.shape
    rows = pl.BlockSpec((TILE, d), lambda i: (i, 0))
    units = pl.BlockSpec((TILE, 4 * UNITS), lambda i: (i, 0))
    return call(
        down_kernel, (n // TILE,),
        [(aa, units), (ab, units), (res, rows), (gf, rows), (shifts, whole(shifts.shape)), (wa, ANYWHERE), (wb, ANYWHERE)],
        [((n, d), BF16, rows), ((8, 128), F32, whole((8, 128)))],
        [pltpu.VMEM((8 * UNITS, d), BF16), pltpu.SemaphoreType.DMA((8,))], gflop=9.0, name="down", limit=50,
    )


def slope_kernel(gf_ref, h_ref, sb_ref, sa_ref, wb_ref, wa_ref, gb_ref, ga_ref, nb_ref, na_ref, tb_ref, ta_ref):
    for half, (s_ref, w_ref, g_ref, n_ref, t_ref) in enumerate(((sb_ref, wb_ref, gb_ref, nb_ref, tb_ref), (sa_ref, wa_ref, ga_ref, na_ref, ta_ref))):

        @pl.when((pl.program_id(0) >= 4) == (half == 1))
        def _():
            g = (mm(gf_ref[...], w_ref[...], NT) * s_ref[...].astype(F32)).astype(BF16)
            g_ref[...] = g
            n_ref[0] = mm(g, h_ref[...], TN).astype(BF16)
            t_ref[...] = jnp.sum(g.astype(F32), axis=0, keepdims=True)


def slope(gf, h, sb, sa, wb, wa):
    n, d = gf.shape
    low, high = (lambda t: jnp.minimum(t, 3)), (lambda t: jnp.maximum(t - 4, 0))
    units = lambda at: pl.BlockSpec((n, UNITS), lambda t: (0, at(t)))
    rows = lambda at: pl.BlockSpec((UNITS, d), lambda t: (at(t), 0))
    outs = [(sa.shape, BF16, units(at)) for at in (low, high)]
    outs += [((4, UNITS, d), BF16, pl.BlockSpec((1, UNITS, d), lambda t, at=at: (at(t), 0, 0))) for at in (low, high)]
    outs += [((1, 4 * UNITS), F32, pl.BlockSpec((1, UNITS), lambda t, at=at: (0, at(t)))) for at in (low, high)]
    return call(
        slope_kernel, (8,),
        [(gf, whole(gf.shape)), (h, whole(h.shape)), (sb, units(low)), (sa, units(high)), (wb, rows(low)), (wa, rows(high))], outs,
        gflop=9.0, name="slope", limit=50, far=(0, 1),
    )


def back_kernel(place_ref, ga_ref, gb_ref, gf_ref, res_ref, gain_ref, w_ref, *refs):
    gr_ref, br_ref, oa_ref, ob_ref, vec_ref, held_ref, out_ref, sem, out_sem = refs[8:]
    half = 4 * UNITS
    copies = [c for i in range(2) for c in gathered_copies(place_ref, w_ref, held_ref, sem, i, i * half)]
    outs = out_copies(refs[:8], out_ref, out_sem)
    step = pl.program_id(0)

    def rest(gy, first):
        c = gf_ref[...].astype(F32)
        gv, terms = norm_back(res_ref[...], gy, gain_ref[1:2, :])
        gr = c + gv
        gr_ref[...] = gr
        branch = gr.astype(BF16)
        br_ref[...] = branch
        if first:
            end(outs[0])
        go = mm(branch, out_ref[...].reshape(8 * PAIR, -1), NT).astype(BF16)
        oa_ref[...] = go[:, : 4 * PAIR]
        ob_ref[...] = go[:, 4 * PAIR :]
        sums = column_sums(terms, gy, branch.astype(F32), c)
        vec_ref[...] = sums if first else vec_ref[...] + sums

    @pl.when(step == 0)
    def _():
        begin(copies)
        begin(outs)
        gy = None
        for c in range(8):
            end(copies[c])
            g_ref, lo = (ga_ref, c * UNITS) if c < 4 else (gb_ref, (c - 4) * UNITS)
            part = mm(g_ref[:, lo : lo + UNITS], held_ref[c * UNITS : (c + 1) * UNITS, :], NN)
            gy = part if gy is None else gy + part
        rest(gy, True)

    @pl.when(step > 0)
    def _():
        rest(mm(ga_ref[...], held_ref[:half, :], NN) + mm(gb_ref[...], held_ref[half:, :], NN), False)


def back(place, ga, gb, gf, w, ws, res, gains):
    n, d = res.shape
    rows = pl.BlockSpec((TILE, d), lambda i: (i, 0))
    units = pl.BlockSpec((TILE, 4 * UNITS), lambda i: (i, 0))
    heads = pl.BlockSpec((TILE, 4 * PAIR), lambda i: (i, 0))
    return call(
        back_kernel, (n // TILE,),
        [(place, SCALARS), (ga, units), (gb, units), (gf, rows), (res, rows), (gains, whole(gains.shape)), (w, FAR)] + [(w, FAR) for w in ws],
        [((n, d), F32, rows), ((n, d), BF16, rows), ((n, 4 * PAIR), BF16, heads), ((n, 4 * PAIR), BF16, heads), ((8, d), F32, whole((8, d)))],
        [pltpu.VMEM((8 * UNITS, d), BF16), pltpu.VMEM((8, 4, PART, d), BF16), pltpu.SemaphoreType.DMA((32,)), pltpu.SemaphoreType.DMA((8,))],
        gflop=12.0, name="back", limit=50, far=(0,),
    )


def attend_back_kernel(row_ref, go_ref, qkv_ref, o_ref, lse_ref, g_ref, bias_ref, p_ref, d_ref):
    n = go_ref.shape[0]

    @pl.when(pl.program_id(0) == 0)
    def _():
        fill_mask(bias_ref, row_ref, True)

    q_at, k_at, v_at = slice(0, PAIR), slice(PAIR, 2 * PAIR), slice(2 * PAIR, 3 * PAIR)
    k_turned = jnp.transpose(qkv_ref[:, k_at])
    work = [(i, h) for i in range(n // TILE) for h in range(2)]
    qs, gs, deltas, halves = {}, {}, {}, {}

    def products(i, h):
        part, upto = slice(i * TILE, (i + 1) * TILE), (i + 1) * TILE
        if h == 0:
            go = go_ref[part, :]
            qs[i], gs[i] = split_heads(qkv_ref[part, q_at]), split_heads(go)
            both = jnp.transpose(go.astype(F32) * o_ref[part, :].astype(F32))
            deltas[i] = [jnp.sum(both[k * HD : (k + 1) * HD], axis=0, keepdims=True) for k in range(2)]
        return mm(qkv_ref[:upto, k_at], qs[i][h], NT), mm(qkv_ref[:upto, v_at], gs[i][h], NT)

    def query_grad(i, h, ds):
        part, upto = slice(i * TILE, (i + 1) * TILE), (i + 1) * TILE
        halves[h] = mm(k_turned[h * HD : (h + 1) * HD, :upto], ds, NN)
        if h:
            gq = jnp.transpose(jnp.concatenate([halves[0], halves[1]], axis=0))
            g_ref[part, q_at] = (gq.astype(BF16).astype(F32) * HD**-0.5).astype(BF16)

    now, held = products(*work[0]), None
    for t, (i, h) in enumerate(work):
        part, upto = slice(i * TILE, (i + 1) * TILE), (i + 1) * TILE
        ahead = products(*work[t + 1]) if t + 1 < len(work) else None
        p = jnp.exp2((now[0] + bias_ref[:upto, part] - lse_ref[0, h : h + 1, part]) * LOG2E)
        ds = (p * (now[1] - deltas[i][h])).astype(BF16)
        p_ref[h, :upto, part] = p.astype(BF16)
        d_ref[h, :upto, part] = ds
        if held is not None:
            query_grad(*work[t - 1], held)
        now, held = ahead, ds
    query_grad(*work[-1], held)
    qa, qb = split_heads(qkv_ref[:, q_at])
    ga, gb = split_heads(go_ref[...])
    for i in range(n // TILE):
        part, lo = slice(i * TILE, (i + 1) * TILE), i * TILE
        g_ref[part, k_at] = (mm(d_ref[0, part, lo:], qa[lo:], NN) + mm(d_ref[1, part, lo:], qb[lo:], NN)).astype(BF16)
        g_ref[part, v_at] = (mm(p_ref[0, part, lo:], ga[lo:], NN) + mm(p_ref[1, part, lo:], gb[lo:], NN)).astype(BF16)


def attend_back(row, go, stacks, base, pairs):
    qkv, o, lse = stacks[:3]
    n = go.shape[0]
    pair = pl.BlockSpec((n, PAIR), lambda p: (0, p + base))
    return call(
        attend_back_kernel, (pairs,),
        [(row, whole(row.shape)), (go, pair), (qkv, pl.BlockSpec((n, 3 * PAIR), lambda p: (0, p + base))), (o, pair),
         (lse, pl.BlockSpec((1, 2, n), lambda p: (p + base, 0, 0)))],
        [((n, 3 * PAIR * pairs), BF16, pl.BlockSpec((n, 3 * PAIR), lambda p: (0, p)))],
        [pltpu.VMEM((n, n), F32), pltpu.VMEM((2, n, n), BF16), pltpu.VMEM((2, n, n), BF16)],
        gflop=5.0 * pairs, name="attend_back", limit=32,
    )[0]


def outer_attn_kernel(gb_ref, ga_ref, ob_ref, oa_ref, h_ref, branch_ref, ub_ref, ua_ref, nb_ref, na_ref, *, pairs):
    d = h_ref.shape[1]
    for half, (g_ref, o_ref, up_ref, n_ref) in enumerate(((gb_ref, ob_ref, ub_ref, nb_ref), (ga_ref, oa_ref, ua_ref, na_ref))):

        @pl.when((pl.program_id(0) >= pairs) == (half == 1))
        def _():
            out = mm(o_ref[...], branch_ref[...], TN).astype(BF16)
            qkv = mm(g_ref[...], h_ref[...], TN).astype(BF16)
            sums = jnp.sum(g_ref[...].astype(F32), axis=0, keepdims=True)
            qsum, vsum = sums[:, :PAIR], sums[:, 2 * PAIR :]
            for j in range(4):
                turn = lambda a: jnp.concatenate([a[:, j * PART :], a[:, : j * PART]], axis=1) if j else a
                line = jnp.concatenate([up_ref[j, 0, 0:1, :], turn(qsum), turn(vsum), jnp.zeros((1, d - 3 * PAIR), F32)], axis=1)
                line = jnp.concatenate([line, jnp.zeros((15, d), F32)], axis=0).astype(BF16)
                rows = [out[j * PART : (j + 1) * PART]] + [qkv[i * PAIR + j * PART : i * PAIR + (j + 1) * PART] for i in range(3)]
                n_ref[j] = jnp.concatenate(rows + [line], axis=0)


def outer_attn(gb, ga, ob, oa, base, h, branch, ub, ua):
    n, m = ga.shape
    d = h.shape[1]
    pairs = m // (3 * PAIR)
    low, high = (lambda p: jnp.minimum(p, pairs - 1)), (lambda p: jnp.maximum(p - pairs, 0))
    grad = lambda at: pl.BlockSpec((n, 3 * PAIR), lambda p: (0, at(p)))
    head = lambda at: pl.BlockSpec((n, PAIR), lambda p: (0, at(p) + base))
    out = lambda at: ((4, pairs * ATTN, d), BF16, pl.BlockSpec((4, ATTN, d), lambda p: (0, at(p), 0)))
    return call(
        functools.partial(outer_attn_kernel, pairs=pairs), (2 * pairs,),
        [(gb, grad(low)), (ga, grad(high)), (ob, head(low)), (oa, head(high)), (h, whole(h.shape)), (branch, whole(branch.shape)),
         (ub, pl.BlockSpec((4, 1, 8, PAIR), lambda p: (0, low(p), 0, 0))), (ua, pl.BlockSpec((4, 1, 8, PAIR), lambda p: (0, high(p), 0, 0)))],
        [out(low), out(high)], gflop=2.5 * pairs, name="outer_attn", limit=30,
    )


def combine_kernel(a_ref, b_ref, *outs):
    for j in range(4):
        outs[j][...] = (a_ref[j].astype(F32) + b_ref[j].astype(F32)).astype(BF16)


def combine(a, b):
    _, m, d = a.shape
    rows = 128 if m % 128 == 0 else 96
    block = pl.BlockSpec((4, rows, d), lambda i: (0, i, 0))
    return call(combine_kernel, (m // rows,), [(a, block), (b, block)], [((m, d), BF16, pl.BlockSpec((rows, d), lambda i: (i, 0)))] * 4, gflop=0.1, name="combine", limit=16)


def finish_kernel(*refs, plan):
    grads, w_refs = refs[: len(plan)], refs[len(plan) : len(plan) + 8]
    x_ref, gr_ref, gain_ref, out_ref, vec_ref, held_ref, sem = refs[len(plan) + 8 :]
    step = pl.program_id(0)
    copies, spans, lo = [], [], 0
    for half, base, count in plan:
        spans.append(slice(3 * lo, 3 * (lo + count)))
        mine = []
        for z in range(base, base + count):
            for i in range(3):
                at = 3 * lo + i
                mine.append(pltpu.make_async_copy(w_refs[4 * half + z].at[:, pl.ds((1 + i) * PART, PART)], held_ref.at[at], sem.at[at]))
            lo += 1
        copies.append(mine)

    def tile(first):
        gy = None
        for g_ref, span, mine in zip(grads, spans, copies):
            if first:
                end(mine)
            part = mm(g_ref[...], held_ref[span].reshape(g_ref.shape[1], -1), NN)
            gy = part if gy is None else gy + part
        gv, terms = norm_back(x_ref[...].astype(F32), gy, gain_ref[0:1, :])
        out_ref[...] = gr_ref[...] + gv
        sums = column_sums(terms, gy)
        vec_ref[...] = sums if first else vec_ref[...] + sums

    @pl.when(step == 0)
    def _():
        begin(copies)
        tile(True)

    @pl.when(step > 0)
    def _():
        tile(False)


def finish(grads, ws, x, gr, gains):
    n, d = x.shape
    rows = pl.BlockSpec((TILE, d), lambda i: (i, 0))
    plan = tuple((half, base, g.shape[1] // (3 * PAIR)) for g, half, base in grads)
    return call(
        functools.partial(finish_kernel, plan=plan), (n // TILE,),
        [(g, pl.BlockSpec((TILE, g.shape[1]), lambda i: (i, 0))) for g, _, _ in grads]
        + [(w, FAR) for w in ws] + [(x, rows), (gr, rows), (gains, whole(gains.shape))],
        [((n, d), F32, rows), ((8, d), F32, whole((8, d)))],
        [pltpu.VMEM((24, 4, PART, d), BF16), pltpu.SemaphoreType.DMA((24,))], gflop=10.0, name="finish", limit=56,
    )


def pack_kernel(r_ref, *refs, plan, bands):
    srcs, (out_ref, held_ref, in_sem, out_sem) = refs[:-4], refs[-4:]
    copies = []
    for at, (src, quarter, count, dst) in enumerate(plan):
        source = srcs[src] if quarter is None else srcs[src].at[r_ref[0] ^ quarter]
        copies.append(pltpu.make_async_copy(source, held_ref.at[pl.ds(dst, count)], in_sem.at[at]))
    begin((copies,))
    band = held_ref.shape[0] // bands
    outs = []
    for b in range(bands):
        end([copy for copy, (_, _, _, dst) in zip(copies, plan) if dst // band == b])
        outs.append(pltpu.make_async_copy(held_ref.at[pl.ds(b * band, band)], out_ref.at[pl.ds(b * band, band)], out_sem.at[b]))
        begin((outs[-1:],))
    end(outs)


def pack(r, arrays, plan, bands):
    rows = sum(count for _, _, count, _ in plan)
    d = arrays[0].shape[-1]
    return call(
        functools.partial(pack_kernel, plan=plan, bands=bands), (), [(r, SCALARS)] + [(a, ANYWHERE) for a in arrays], [((rows, d), BF16, ANYWHERE)],
        [pltpu.VMEM((rows, d), BF16), pltpu.SemaphoreType.DMA((len(plan),)), pltpu.SemaphoreType.DMA((bands,))], gflop=0.0, name="pack", limit=14,
    )[0]


def stack_z(r, parts):
    n = parts[0].shape[0]
    return pack(r, parts, [(i, None, n, i * n) for i in range(3)], 3)


def stack_units(r, quarters, sides):
    n = quarters.shape[1]
    plan = [(0, j, n, 4 * n * j) for j in range(4)] + [(1 + j, None, 3 * n, 4 * n * j + n) for j in range(4)]
    return pack(r, [quarters, *sides], plan, 4)


def settle_kernel(r_ref, *refs):
    qkv_ref, bias_ref, out_ref, held_ref = refs[4:]
    for j in range(4):
        held_ref[j] = refs[j][...]
    quarters = [held_ref[r_ref[0] ^ q].astype(F32) for q in range(4)]
    for i in range(3):
        qkv_ref[i] = jnp.transpose(jnp.concatenate([a[(1 + i) * PART : (2 + i) * PART] for a in quarters], axis=0))
    bias_ref[...] = jnp.concatenate([a[4 * PART : 4 * PART + 1, : 3 * PAIR] for a in quarters] + [jnp.zeros((4, 3 * PAIR), F32)], axis=0)
    out_ref[...] = jnp.concatenate([a[:PART] for a in quarters], axis=0)


def settle(r, pieces):
    d = pieces[0].shape[1]
    shapes = [(3, d, PAIR), (8, 3 * PAIR), (PAIR, d)]
    return call(
        settle_kernel, (), [(r, SCALARS)] + [(a, whole(a.shape)) for a in pieces], [(shape, F32, whole(shape)) for shape in shapes],
        [pltpu.VMEM((4, ATTN, d), BF16)], gflop=0.1, name="settle", limit=24,
    )


def settle_units_kernel(g_ref, down_ref, up_ref):
    down_ref[...] = g_ref[0, 0].astype(F32)
    up_ref[...] = jnp.transpose(g_ref[0, 1].astype(F32))


def settle_units(g):
    d = g.shape[-1]
    return call(
        settle_units_kernel, (4,), [(g, pl.BlockSpec((1, 2, PAIR, d), lambda q: (q, 0, 0, 0)))],
        [((4 * PAIR, d), F32, pl.BlockSpec((PAIR, d), lambda q: (q, 0))), ((d, 4 * PAIR), F32, pl.BlockSpec((d, PAIR), lambda q: (0, q)))],
        gflop=0.1, name="settle_units", limit=24,
    )


def moved(array, axis, mask):
    size = lax.axis_size(axis)
    return lax.ppermute(array, axis, [(i, i ^ mask) for i in range(size)])


def across(array):
    return moved(array, "mp", 1)


def beside(array, j):
    return moved(array, "rows", j)


def along_z(array, z):
    return moved(array, "mp", 2 * z)


def fence(*trees):
    return lax.optimization_barrier(trees)


def by_z(a):
    z = lax.axis_index("mp") // 2
    low = [jnp.where(z & 1, a[i ^ 1], a[i]) for i in range(4)]
    return [jnp.where(z & 2, low[i ^ 2], low[i]) for i in range(4)]


def added(*terms):
    total = terms[0].astype(F32)
    for term in terms[1:]:
        total = total + term.astype(F32)
    return total.astype(BF16)


def any_spread(parts):
    core = lax.axis_index("mp") % 2
    return [lax.dynamic_index_in_dim(parts, c, 0, False) for c in (core, 1 - core)]


def any_reduced(full, axis):
    return lax.psum(lax.psum_scatter(full, "mp", scatter_dimension=axis, tiled=True), "rows")


def up_sums(total, first, last):
    return jnp.pad(total.reshape(4, 4, 1, PAIR)[:, first:last], ((0, 0), (0, 0), (0, 7), (0, 0)))


def stacked_vectors(one, two, loss):
    d = one.shape[1]
    at = lax.axis_index("rows") * lax.axis_size("mp") + lax.axis_index("mp")
    losses = jnp.where(jnp.arange(d, dtype=jnp.int32) == at, loss[0, 0] / math.sqrt(SLOTS * d), 0.0)
    return jnp.stack([one[0], two[0], one[1], two[2], two[1], two[3], losses, jnp.zeros_like(losses)])


def own_vectors(vectors):
    place, row, size = lax.axis_index("mp"), lax.axis_index("rows"), lax.axis_size("mp")
    share = vectors.shape[1] // size
    return lax.dynamic_slice_in_dim(vectors[:6], place * share, share, 1), lax.dynamic_slice_in_dim(vectors[6], row * size, size, 0)


def any_mesh(tokens, qkv_rows, qv_bias, out_weight, up_rows, up_bias, down_weight, gains, shifts, live, line, cotangent):
    d = tokens.shape[1]
    r = jnp.zeros((1,), jnp.int32)
    every = lambda a, axis=0: lax.all_gather(a, "mp", axis=axis, tiled=True)
    heads = lambda a: a.reshape(2, 4, 4, PART, d)
    qkv_all, qvb_all = every(qkv_rows, 1), every(qv_bias, 1)
    small = lambda a: jnp.tile(a.reshape(2, 4, 4, PART), (1, 1, 1, 4))
    ups = every(up_bias).reshape(2, 4, 4, PAIR).swapaxes(1, 2)
    bias = jnp.concatenate([ups, small(qvb_all[0]), small(qvb_all[1])], axis=3)
    bias = jnp.pad(bias[:, :, :, None, :], ((0, 0), (0, 0), (0, 0), (0, 15), (0, d - 3 * PAIR)))
    wa, wb = any_spread(jnp.concatenate([heads(every(out_weight)), heads(qkv_all[0]), heads(qkv_all[1]), heads(qkv_all[2]), bias], axis=3))

    place = jnp.zeros((3,), jnp.int32)
    da, db = any_spread(every(down_weight).reshape(2, 16 * PAIR, d))
    by_half = jnp.stack(any_spread(every(up_rows).reshape(2, 4, 4, PAIR, d)))
    up_all = jnp.moveaxis(by_half, 0, 2).reshape(32, PAIR, d)
    h1, gf = prep(tokens, cotangent, live, gains, shifts)
    stacks, ws = [], [w[z] for w in (wa, wb) for z in range(4)]
    for w in (wa, wb):
        stacks.append(attend(r, line, h1, [w[0], w[1], w[2], w[3]], "packed", 0)[0])
    stack_a, stack_b = stacks
    res, h2 = join(tokens, stack_a[1], stack_b[1], ws, gains, shifts)
    aa, sa, down_a = up(place, h2, gf, up_all, stack_a[3], 0)
    ab, sb, down_b = up(place, h2, gf, up_all, stack_b[3], 1)
    g_down = added(down_a, across(down_b))
    mixed, loss = down(aa, ab, da, db, res, gf, shifts)
    gb, ga, up_b, up_a, total_b, total_a = slope(gf, h2, sb, sa, db, da)
    g_up = added(up_a, across(up_b))
    gr, branch, go_a, go_b, two = back(place, ga, gb, gf, up_all, ws, res, gains)
    back_b = attend_back(line, go_b, stack_b, 0, 4)
    back_a = attend_back(line, go_a, stack_a, 0, 4)
    nb, na = outer_attn(back_b, back_a, stack_b[1], stack_a[1], 0, h1, branch, up_sums(total_b, 0, 4), up_sums(total_a, 0, 4))
    g_attn = added(na, across(nb)).reshape(4, 4, ATTN, d)
    input_grad, one = finish([(back_a, 0, 0), (back_b, 1, 0)], ws, tokens, gr, gains)
    vectors = own_vectors(lax.psum(stacked_vectors(one, two, loss), ("rows", "mp")))
    core = lax.axis_index("mp") % 2
    full = lambda g: lax.dynamic_update_index_in_dim(jnp.zeros((2,) + g.shape, F32), g.astype(F32), core, 0)
    ordered = lambda g: full(g).swapaxes(1, 2).reshape(-1, g.shape[-1])
    down_grad, up_grad = [any_reduced(full(g).reshape(-1, d), 0) for g in (g_down, g_up)]
    out_grad = any_reduced(ordered(g_attn[:, :, :PART]), 0)
    qkv_grad = any_reduced(jnp.stack([ordered(g_attn[:, :, i * PART : (i + 1) * PART]) for i in (1, 2, 3)]), 1)
    lines = g_attn[:, :, 4 * PART]
    up_bias_grad = any_reduced(full(lines[:, :, :PAIR]).reshape(-1), 0)
    ordered = lambda g: full(g).swapaxes(1, 2).reshape(-1)
    qv_bias_grad = any_reduced(jnp.stack([ordered(lines[:, :, at : at + PART]) for at in (PAIR, 2 * PAIR)]), 1)
    qkv_grad, up_grad = jnp.swapaxes(qkv_grad, 1, 2), up_grad.T
    return mixed, input_grad, qkv_grad, qv_bias_grad, out_grad, up_grad, up_bias_grad, down_grad, vectors


def small_mesh(tokens, qkv_rows, qv_bias, out_weight, up_rows, up_bias, down_weight, gains, shifts, live, line, cotangent):
    d = tokens.shape[1]
    row = lax.axis_index("rows")
    r = row.reshape(1).astype(jnp.int32)
    mine = lambda a: lax.dynamic_index_in_dim(a, row, 0, False)
    sides = lambda a: [beside(a, j) for j in (1, 2, 3)]
    sides3 = lambda g: [beside(g[j], j) for j in (1, 2, 3)]

    bias = jnp.concatenate(
        [up_bias.reshape(4, PAIR), jnp.tile(qv_bias[0].reshape(4, PART), (1, 4)), jnp.tile(qv_bias[1].reshape(4, PART), (1, 4))], axis=1
    )
    bias = jnp.pad(bias[:, None, :], ((0, 0), (0, 15), (0, d - 3 * PAIR)))
    qkv4 = qkv_rows.reshape(3, 4, PART, d).swapaxes(0, 1).reshape(4, 3 * PART, d)
    a4 = jnp.concatenate([out_weight.reshape(4, PART, d), qkv4, bias], axis=1)
    pa = mine(a4)
    c4 = down_weight.reshape(4, PAIR, d)
    pc = mine(c4)
    index = lax.axis_index("mp").astype(jnp.int32)
    place = jnp.stack([row.astype(jnp.int32), index // 2, index % 2])
    up_all = lax.all_gather(mine(up_rows.reshape(4, PAIR, d)), ("rows", "mp"))
    p1, c2 = along_z(pa, 1), along_z(pc, 2)
    h1, gf = prep(tokens, cotangent, live, gains, shifts)
    p1, c2, h1, gf, pa, pc = fence(p1, c2, h1, gf, pa, pc)
    s1, p2 = sides(p1), along_z(pa, 2)
    sa, w0 = attend(r, line, h1, [a4], "quarters", 0)
    s1, p2, sa, w0, h1, pa = fence(s1, p2, sa, w0, h1, pa)
    s2, p3, x0 = sides(p2), along_z(pa, 3), across(w0)
    sa, w1 = attend(r, line, h1, [p1, *s1], "pieces", 1, sa)
    s2, p3, x0, sa, w1, h1, pc = fence(s2, p3, x0, sa, w1, h1, pc)
    s3, c1 = sides(p3), along_z(pc, 1)
    sa, w2 = attend(r, line, h1, [p2, *s2], "pieces", 2, sa)
    sb, _ = attend(r, line, h1, [x0], "packed", 0)
    s3, c1, sa, w1, w2, sb, h1, pc = fence(s3, c1, sa, w1, w2, sb, h1, pc)
    c3, x1, x2 = along_z(pc, 3), across(w1), across(w2)
    sb, _ = attend(r, line, h1, [x1, x2], "packed", 1, sb)
    sa, w3 = attend(r, line, h1, [p3, *s3], "pieces", 3, sa)
    c3, sa, sb, w3, h1 = fence(c3, sa, sb, w3, h1)
    cs = stack_z(r, [c1, c2, c3])
    cx, x3 = sides(cs), across(w3)
    ws = [w0, w1, w2, w3, x0, x1, x2, x3]
    sb, _ = attend(r, line, h1, [x3], "packed", 3, sb)
    res, h2 = join(tokens, sa[1], sb[1], ws, gains, shifts)
    ab, lb, down_b = up(place, h2, gf, up_all, sb[3], 1)
    cx, ab, lb, down_b, h2 = fence(cx, ab, lb, down_b, h2)
    da = stack_units(r, c4, [cs, *cx])
    db, down_x = across(da), across(down_b)
    aa, la, down_a = up(place, h2, gf, up_all, sa[3], 0)
    da, db, down_x, aa, la, down_a, h2 = fence(da, db, down_x, aa, la, down_a, h2)
    g_down = combine(down_a, down_x)
    fx = [beside(g_down[j], j) for j in (1, 2)]
    gb, ga, up_b, up_a, total_b, total_a = slope(gf, h2, lb, la, db, da)
    fx, gb, ga, up_b, up_a, g3 = fence(fx, gb, ga, up_b, up_a, g_down[3])
    fx, up_x = [*fx, beside(g3, 3)], across(up_b)
    gr, branch, go_a, go_b, two = back(place, ga, gb, gf, up_all, ws, res, gains)
    g_up = combine(up_a, up_x)
    fx, gr, branch, go_a, go_b, g_up = fence(fx, gr, branch, go_a, go_b, g_up)
    columns = [[2 * i + core for i in range(4)] for core in range(2)]
    reduce_z = lambda t: lax.psum_scatter(t, "mp", scatter_dimension=0, tiled=False, axis_index_groups=columns)
    f_down = reduce_z(jnp.stack(by_z(added(g_down[0], *fx).reshape(4, PAIR, d))))
    fx = [beside(g_up[j], j) for j in (1, 2)]
    back_b1 = attend_back(line, go_b, sb, 2, 2)
    back_a1 = attend_back(line, go_a, sa, 2, 2)
    nb1, na1 = outer_attn(back_b1, back_a1, sb[1], sa[1], 2, h1, branch, up_sums(total_b, 2, 4), up_sums(total_a, 2, 4))
    fx, back_a1, back_b1, nb1, na1, go_a, go_b, g3 = fence(fx, back_a1, back_b1, nb1, na1, go_a, go_b, g_up[3])
    fx, n1_x = [*fx, beside(g3, 3)], across(nb1)
    back_b2 = attend_back(line, go_b, sb, 0, 2)
    back_a2 = attend_back(line, go_a, sa, 0, 2)
    nb2, na2 = outer_attn(back_b2, back_a2, sb[1], sa[1], 0, h1, branch, up_sums(total_b, 0, 2), up_sums(total_a, 0, 2))
    tu = jnp.stack(by_z(added(g_up[0], *fx).reshape(4, PAIR, d)))
    n1 = combine(na1, n1_x)
    tu, n1, back_b2, back_a2, nb2, na2, gr, f_down = fence(tu, n1, back_b2, back_a2, nb2, na2, gr, f_down)
    f_up = reduce_z(tu)
    ex, n2_x = sides3(n1), across(nb2)
    input_grad, one = finish([(back_a2, 0, 0), (back_a1, 0, 2), (back_b2, 1, 0), (back_b1, 1, 2)], ws, tokens, gr, gains)
    n2 = combine(na2, n2_x)
    ex, input_grad, one, n2, aa = fence(ex, input_grad, one, n2, aa)
    t1 = added(n1[0], *ex).reshape(2, ATTN, d)
    t1, f_up = fence(t1, f_up)
    units = lax.all_gather(jnp.stack([f_down, f_up]), "rows")
    ex, y2, y3 = sides3(n2), along_z(t1[0], 2), along_z(t1[1], 3)
    mixed, loss = down(aa, ab, da, db, res, gf, shifts)
    vectors = stacked_vectors(one, two, loss)
    ex, y2, y3, mixed, vectors = fence(ex, y2, y3, mixed, vectors)
    t2 = added(n2[0], *ex).reshape(2, ATTN, d)
    y1, vx = along_z(t2[1], 1), sides(vectors)
    vx, y1, vectors, t2 = fence(vx, y1, vectors, t2)
    f = added(t2[0], y1, y2, y3)
    d_last = sides(f)
    vectors = (vectors + vx[0]) + (vx[1] + vx[2])
    vectors = vectors + across(vectors)
    vz = [along_z(vectors, i) for i in (1, 2, 3)]
    vectors = (vectors + vz[0]) + (vz[1] + vz[2])
    down_grad, up_grad = settle_units(units)
    vectors = own_vectors(vectors)
    d_last, down_grad, up_grad, vectors = fence(d_last, down_grad, up_grad, vectors)
    qkv_grad, biases, out_grad = settle(r, [f, *d_last])
    up_bias_grad = biases[:4, :PAIR].reshape(-1)
    qv_bias_grad = jnp.stack([biases[:4, at : at + PART].reshape(-1) for at in (PAIR, 2 * PAIR)])
    return mixed, input_grad, qkv_grad, qv_bias_grad, out_grad, up_grad, up_bias_grad, down_grad, vectors


def body(tokens, qkv_weight, qv_bias, out_weight, up_weight, up_bias, down_weight, norm_gains, shift_vectors, lengths, cotangent):
    n, d = tokens.shape
    place = lax.axis_index("mp")
    endings = jnp.cumsum(lax.dynamic_slice_in_dim(lengths, place, 1, 0)[0])
    position = jnp.arange(SLOTS, dtype=jnp.int32)
    segment = jnp.sum((position[:, None] >= endings[None, :]).astype(jnp.int32), axis=1)
    live = (segment < DOCS).astype(F32)[:, None]
    ident = jnp.where(segment < DOCS, segment, DOCS + position).astype(jnp.int32)
    layer = small_mesh if (lax.axis_size("rows"), lax.axis_size("mp")) == (4, 8) else any_mesh
    mixed, input_grad, qkv_grad, qv_bias_grad, out_grad, up_grad, up_bias_grad, down_grad, vectors = layer(
        tokens, jnp.swapaxes(qkv_weight, 1, 2), qv_bias, out_weight, up_weight.T, up_bias, down_weight,
        norm_gains.astype(F32), shift_vectors.astype(F32), live, ident.reshape(1, n), cotangent,
    )
    vector_grad, block_loss = vectors
    return (
        mixed, block_loss, input_grad, qkv_grad, qv_bias_grad, out_grad,
        up_grad, up_bias_grad, down_grad, vector_grad,
    )


def solution(mesh):
    placed = (
        P(("rows", "mp"), None),
        P(None, None, "mp"),
        P(None, "mp"),
        P("mp", None),
        P(None, "mp"),
        P("mp"),
        P("mp", None),
        P(),
        P(),
        P("rows", None),
        P(("rows", "mp"), None),
    )
    return jax.shard_map(
        body,
        mesh=mesh,
        in_specs=placed,
        out_specs=(
            P(("rows", "mp"), None),
            P("rows"),
            P(("rows", "mp"), None),
            P(None, None, "mp"),
            P(None, "mp"),
            P("mp", None),
            P(None, "mp"),
            P("mp"),
            P("mp", None),
            P(None, "mp"),
        ),
        check_vma=False,
    )
```
